128 devices in a mesh: seq: 32 (over x, z, y_hi), head: 4 (over y_lo, core).
Axes of the slice: x: 4, y: 4 (y_hi: 2, y_lo: 2; y = y_hi * 2 + y_lo), z: 4, core: 2. Of those that a mesh axis runs over, the one named last changes fastest.
Arguments:
- inputs: bfloat16 [2, 4096, 2048], P(None, 'seq'), may hold values from -6 to 6
- doc_lengths: int32 [2, 8], replicated, may hold values from 1 to 4089, as said below
- norm_in: bfloat16 [2048], P('seq'), may hold values from 0.5 to 1.5
- query_weight: bfloat16 [2048, 2048], P('seq', 'head'), may hold values from -0.125 to 0.125
- key_weight: bfloat16 [2048, 2048], P('seq', 'head'), may hold values from -0.125 to 0.125
- value_weight: bfloat16 [2048, 2048], P('seq', 'head'), may hold values from -0.125 to 0.125
- outgate_weight: bfloat16 [2048, 2048], P('seq', 'head'), may hold values from -0.125 to 0.125
- scalar_weight: bfloat16 [2048, 2, 16], P('seq', None, 'head'), may hold values from -0.125 to 0.125
- conv_kernel: bfloat16 [3, 4, 2048], P(None, None, 'head'), may hold values from -3 to 3
- decay_rate: bfloat16 [16], P('head'), may hold values from 0.00029945374 to 0.049804688
- head_norm: bfloat16 [128], replicated, may hold values from 0.5 to 1.5
- output_weight: bfloat16 [2048, 2048], P('head', 'seq'), may hold values from -0.25 to 0.25
- norm_ffn: bfloat16 [2048], P('seq'), may hold values from 0.5 to 1.5
- gate_weight: bfloat16 [2048, 5632], P('seq', 'head'), may hold values from -0.125 to 0.125
- up_weight: bfloat16 [2048, 5632], P('seq', 'head'), may hold values from -0.125 to 0.125
- down_weight: bfloat16 [5632, 2048], P('head', 'seq'), may hold values from -0.15625 to 0.15625
- grad_out: bfloat16 [2, 4096, 2048], P(None, 'seq'), may hold values from -6 to 6
Outputs:
- outputs: bfloat16 [2, 4096, 2048], P(None, 'seq')
- grad_in: float32 [2, 4096, 2048], P(None, 'seq')
- grad_norm_in: float32 [2048], P('seq')
- grad_query: float32 [2048, 2048], P('seq', 'head')
- grad_key: float32 [2048, 2048], P('seq', 'head')
- grad_value: float32 [2048, 2048], P('seq', 'head')
- grad_outgate: float32 [2048, 2048], P('seq', 'head')
- grad_scalars: float32 [2048, 2, 16], P('seq', None, 'head')
- grad_conv: float32 [3, 4, 2048], P(None, None, 'head')
- grad_decay: float32 [16], P('head')
- grad_head_norm: float32 [128], replicated
- grad_output: float32 [2048, 2048], P('head', 'seq')
- grad_norm_ffn: float32 [2048], P('seq')
- grad_gate: float32 [2048, 5632], P('seq', 'head')
- grad_up: float32 [2048, 5632], P('seq', 'head')
- grad_down: float32 [5632, 2048], P('head', 'seq')
The draws below stay inside these ranges and needn't reach their ends.
Inputs may be any that keep to these rules, and one draw needn't show every extreme that they name: `doc_lengths`: each row holds the lengths of 8 packed documents and sums to 4096; in every row the second document starts within the first 128 positions and ends within the last 128.
All inputs are finite; a program needn't handle non-finite values.
Results may differ from the reference program's by a relative error of at most 0.03145.
Values may be sent and summed in bfloat16 or wider, within the bound.
No kernel may reach another device: no remote copies, remote signals or barrier semaphores. Data moves between devices by JAX's collectives and lax.ppermute only.
A program may use at most 192 MiB of HBM per device.

```python
import math
from functools import partial
import jax
import jax.numpy as jnp
from jax import lax

D = 2048
H = 16
DK = 128
FF = 5632
CONV = 4
GROUP = 64
TOK_SEQ = 128
DOCS = 8
SEQS = 2
LEN = 4096


def draw_doc_lengths(key, part):
    key = jax.random.fold_in(key, 11)
    first_key, tail_key = jax.random.split(key)
    lead_length = jax.random.randint(first_key, (SEQS, 1), 1, TOK_SEQ, dtype=jnp.int32)
    tail_lengths = jax.random.randint(tail_key, (SEQS, DOCS - 2), 1, TOK_SEQ // DOCS + 1, dtype=jnp.int32)
    middle_length = LEN - lead_length - jnp.sum(tail_lengths, axis=1, keepdims=True)
    return jnp.concatenate([lead_length, middle_length, tail_lengths], axis=1).astype(jnp.int32)


def level_of(rng, shape, shards, smallest, largest):
    level = 1.0
    for position, blocks in shards:
        draws = jax.random.uniform(jax.random.fold_in(jax.random.fold_in(rng, 6), position), (blocks,), jnp.float32, smallest / len(shards), largest / len(shards))
        level = level * jnp.repeat(jnp.exp(draws), shape[position] // blocks).reshape((-1,) + (1,) * (len(shape) - 1 - position))
    return level


def normal_values(rng, dims, width, bound, cuts=(), kind=jnp.bfloat16):
    drawn = width * jax.random.normal(rng, dims, jnp.float32)
    if cuts:
        drawn = drawn * level_of(rng, dims, cuts, -0.22, 0.18)
    return jnp.clip(drawn, -bound, bound).astype(kind)


def setup_inputs(seed: int = 0) -> dict:
    key_list = jax.random.split(jax.random.key(seed), 18)
    return {
        "inputs": normal_values(key_list[0], (SEQS, LEN, D), 1.0, 6.0, ((1, 32),)),
        "doc_lengths": draw_doc_lengths(jax.random.fold_in(key_list[17], 71), 0),
        "norm_in": jnp.clip(1.0 + 0.1 * jax.random.normal(key_list[2], (D,), jnp.float32), 0.5, 1.5).astype(jnp.bfloat16),
        "query_weight": normal_values(key_list[3], (D, H * DK), D ** -0.5, 0.125, ((0, 32), (1, 4))),
        "key_weight": normal_values(key_list[4], (D, H * DK), D ** -0.5, 0.125, ((0, 32), (1, 4))),
        "value_weight": normal_values(key_list[5], (D, H * DK), D ** -0.5, 0.125, ((0, 32), (1, 4))),
        "outgate_weight": normal_values(key_list[6], (D, H * DK), D ** -0.5, 0.125, ((0, 32), (1, 4))),
        "scalar_weight": normal_values(key_list[7], (D, 2, H), D ** -0.5, 0.125, ((0, 32), (2, 4))),
        "conv_kernel": normal_values(key_list[8], (3, CONV, H * DK), CONV ** -0.5, 3.0, ((2, 4),)),
        "decay_rate": jnp.clip(jnp.exp(math.log(0.049804688) - 5.1139045 * jax.random.uniform(key_list[9], (H,), jnp.float32) ** level_of(key_list[9], (H,), ((0, 4),), -0.2, 0.2)), 0.00029945374, 0.049804688).astype(jnp.bfloat16),
        "head_norm": jnp.clip(1.0 + 0.1 * jax.random.normal(key_list[10], (DK,), jnp.float32), 0.5, 1.5).astype(jnp.bfloat16),
        "output_weight": normal_values(key_list[11], (H * DK, D), (H * DK // 4) ** -0.5, 0.25, ((0, 4), (1, 32))),
        "norm_ffn": jnp.clip(1.0 + 0.1 * jax.random.normal(key_list[12], (D,), jnp.float32), 0.5, 1.5).astype(jnp.bfloat16),
        "gate_weight": normal_values(key_list[13], (D, FF), D ** -0.5, 0.125, ((0, 32), (1, 4))),
        "up_weight": normal_values(key_list[14], (D, FF), D ** -0.5, 0.125, ((0, 32), (1, 4))),
        "down_weight": normal_values(key_list[15], (FF, D), (FF // 4) ** -0.5, 0.15625, ((0, 4), (1, 32))),
        "grad_out": normal_values(key_list[16], (SEQS, LEN, D), 1.0, 6.0, ((1, 32),)),
    }


highest = lax.Precision.HIGHEST
norm_eps = 1e-06
head_eps = 1e-05

@jax.custom_vjp
def low(v):
    return lax.optimization_barrier(v.astype(jnp.bfloat16)).astype(jnp.float32)

@jax.custom_vjp
def low_back(v):
    return v

def low_keep(v):
    return (low(v), None)

def low_pass(kept, grad):
    return (grad,)

def back_keep(v):
    return (v, None)

def back_low(kept, grad):
    return (low(grad),)
low.defvjp(low_keep, low_pass)
low_back.defvjp(back_keep, back_low)

def doc_numbers(doc_lengths):
    doc_ends = jnp.cumsum(doc_lengths, axis=1)
    places = jnp.arange(LEN, dtype=jnp.int32)
    return lax.optimization_barrier(jnp.sum((places[None, :, None] >= doc_ends[:, None, :]).astype(jnp.int32), axis=2))

def short_conv(pre_values, kernel, docs):
    padded = jnp.pad(pre_values, ((0, 0), (CONV - 1, 0), (0, 0)))
    padded_docs = jnp.pad(docs, ((0, 0), (CONV - 1, 0)), constant_values=-1)
    convolved = jnp.zeros_like(pre_values)
    for offset in range(CONV):
        keep_mask = (padded_docs[:, offset:offset + LEN] == docs).astype(jnp.float32)
        convolved = convolved + padded[:, offset:offset + LEN] * keep_mask[:, :, None] * kernel[offset]
    return jax.nn.silu(convolved)

def unit_rows(vectors):
    return vectors * lax.rsqrt(lax.optimization_barrier(jnp.sum(vectors * vectors, axis=-1, keepdims=True)) + norm_eps)

def token_step(memory, columns):
    queries, key_rows, values, strength, decay_step = columns
    recalled = jnp.einsum('shk,shkv->shv', key_rows, memory, precision=highest)
    fresh_values = values - decay_step[..., None] * recalled
    memory = decay_step[..., None, None] * memory + (strength[..., None] * key_rows)[..., :, None] * fresh_values[..., None, :]
    return (memory, jnp.einsum('shk,shkv->shv', queries, memory, precision=highest))

def group_step(memory, columns):
    return lax.scan(token_step, memory, columns)

def to_blocks(source_array):
    moved_axes = jnp.moveaxis(source_array, 1, 0)
    return moved_axes.reshape((LEN // GROUP, GROUP) + moved_axes.shape[1:])

def delta_rule(queries, key_rows, values, strength, decay_step):
    memory = jnp.zeros((SEQS, H, DK, DK), jnp.float32)
    columns = (to_blocks(queries), to_blocks(key_rows), to_blocks(values), to_blocks(strength), to_blocks(decay_step))
    final_state, produced = lax.scan(jax.checkpoint(group_step), memory, columns)
    produced = produced.reshape((LEN,) + produced.shape[2:])
    return jnp.moveaxis(produced, 0, 1)

def forward(params, docs):
    hidden_in, norm_in, query_weight, key_weight, value_weight, outgate_weight, scalar_weight, conv_kernel, decay_rate, head_norm, output_weight, norm_ffn, gate_weight, up_weight, down_weight = params
    scale_in = lax.rsqrt(lax.optimization_barrier(jnp.mean(hidden_in * hidden_in, axis=-1, keepdims=True)) + norm_eps)
    normed_in = low(hidden_in * scale_in * norm_in)
    pre_query = low_back(low(jnp.dot(normed_in, query_weight, precision=highest)))
    pre_key = low_back(low(jnp.dot(normed_in, key_weight, precision=highest)))
    pre_value = low_back(low(jnp.dot(normed_in, value_weight, precision=highest)))
    out_gate = low_back(jnp.dot(normed_in, outgate_weight, precision=highest))
    scalars = low_back(jnp.einsum('std,dkh->stkh', normed_in, scalar_weight, precision=highest))
    head_shape = (SEQS, LEN, H, DK)
    queries = low(unit_rows(short_conv(pre_query, conv_kernel[0], docs).reshape(head_shape)))
    key_rows = low(unit_rows(short_conv(pre_key, conv_kernel[1], docs).reshape(head_shape)))
    values = low(short_conv(pre_value, conv_kernel[2], docs).reshape(head_shape))
    strength = jax.nn.sigmoid(scalars[:, :, 0])
    continues = jnp.concatenate([jnp.zeros((SEQS, 1), jnp.float32), (docs[:, 1:] == docs[:, :-1]).astype(jnp.float32)], axis=1)
    decay_step = jnp.exp(-decay_rate * jax.nn.softplus(scalars[:, :, 1])) * continues[:, :, None]
    heads_out = delta_rule(queries, key_rows, values, strength, decay_step)
    normed_heads = heads_out * lax.rsqrt(lax.optimization_barrier(jnp.mean(heads_out * heads_out, axis=-1, keepdims=True)) + head_eps) * head_norm
    gated_rows = low(normed_heads.reshape(SEQS, LEN, H * DK) * jax.nn.silu(out_gate))
    residual = hidden_in + low_back(jnp.dot(gated_rows, output_weight, precision=highest))
    scale_ffn = lax.rsqrt(lax.optimization_barrier(jnp.mean(residual * residual, axis=-1, keepdims=True)) + norm_eps)
    normed_ffn = low(residual * scale_ffn * norm_ffn)
    gate_proj = low_back(jnp.dot(normed_ffn, gate_weight, precision=highest))
    up_proj = low_back(jnp.dot(normed_ffn, up_weight, precision=highest))
    product = low(jax.nn.silu(gate_proj) * up_proj)
    return residual + low_back(jnp.dot(product, down_weight, precision=highest))

def reference(inputs, doc_lengths, norm_in, query_weight, key_weight, value_weight, outgate_weight, scalar_weight, conv_kernel, decay_rate, head_norm, output_weight, norm_ffn, gate_weight, up_weight, down_weight, grad_out):
    docs = doc_numbers(doc_lengths)
    params = tuple((member.astype(jnp.float32) for member in (inputs, norm_in, query_weight, key_weight, value_weight, outgate_weight, scalar_weight, conv_kernel, decay_rate, head_norm, output_weight, norm_ffn, gate_weight, up_weight, down_weight)))
    final, pull = jax.vjp(partial(forward, docs=docs), params)
    grads = pull(grad_out.astype(jnp.float32))[0]
    return (final.astype(jnp.bfloat16), grads[0], grads[1], grads[2], grads[3], grads[4], grads[5], grads[6], grads[7], grads[8], grads[9], grads[10], grads[11], grads[12], grads[13], grads[14])
```

```python
from functools import partial

import jax
import jax.numpy as jnp
from jax import lax
from jax.experimental import pallas as pl
from jax.experimental.pallas import tpu as pltpu
from jax.sharding import PartitionSpec as P

f32 = jnp.float32
bf16 = jnp.bfloat16
norm_eps = 1e-06
head_eps = 1e-05
SEQ = 32
HEADS = 4
DK = 128
TOK = 128
TAPS = 4
HALO = 16
VMEM = 56 * 1024 * 1024

NN = (((1,), (0,)), ((), ()))
NT = (((1,), (1,)), ((), ()))
TN = (((0,), (0,)), ((), ()))


def dot1(a, b, dims=NN):
    return lax.dot_general(a.astype(bf16), b.astype(bf16), dims, preferred_element_type=f32)


def split(a):
    high = a.astype(bf16)
    return high, (a - high.astype(f32)).astype(bf16)


def dot3(a, b, dims=NN):
    ah, al = split(a)
    bh, bl = split(b)
    return dot1(ah, bh, dims) + (dot1(ah, bl, dims) + dot1(al, bh, dims))


def dot2(exact, b, dims=NN):
    high = b.astype(bf16)
    rest = b - high.astype(f32)
    mid = rest.astype(bf16)
    low = (rest - mid.astype(f32)).astype(bf16)
    return dot1(exact, high, dims) + (dot1(exact, mid, dims) + dot1(exact, low, dims))


def sigmoid(x):
    return 1.0 / (1.0 + jnp.exp(-x))


def softplus(x):
    return jnp.maximum(x, 0.0) + jnp.log1p(jnp.exp(-jnp.abs(x)))


def iotas():
    rows = lax.broadcasted_iota(jnp.int32, (TOK, TOK), 0)
    cols = lax.broadcasted_iota(jnp.int32, (TOK, TOK), 1)
    return rows, cols


def unit_inverses(stricts):
    rows, cols = iotas()
    eye = (rows == cols).astype(f32)
    apart = jnp.bitwise_xor(rows, cols)
    results = []
    first = (apart == 1) & (rows > cols)
    results = [eye - jnp.where(first, a, 0.0) for a in stricts]
    size = 2
    while size < TOK:
        corner = (apart >= size) & (apart < 2 * size) & (rows > cols)
        parts = [dot3(jnp.where(corner, a, 0.0), x) for a, x in zip(stricts, results)]
        results = [x - dot3(x, c) for x, c in zip(results, parts)]
        size *= 2
    return results


def decays(scal, rates, marks, docs_row):
    rows, cols = iotas()
    strength = sigmoid(scal)
    log_decay = -rates * softplus(scal)
    lower = (rows >= cols).astype(bf16)
    total = dot2(lower, log_decay)
    total_t = jnp.transpose(total)
    same = marks[:, 5:6] == docs_row
    causal = same & (rows >= cols)
    return strength, total, total_t, causal, rows > cols


def conv_parts(ext_ref, weights, marks, lane):
    out = None
    for tap in range(TAPS):
        piece = ext_ref[pl.ds(HALO - TAPS + 1 + tap, TOK), pl.ds(lane, DK)]
        if tap < TAPS - 1:
            piece = piece * marks[:, tap : tap + 1]
        piece = piece * weights[tap : tap + 1, lane : lane + DK]
        out = piece if out is None else out + piece
    return out


def unit_scale(x):
    return lax.rsqrt(jnp.sum(x * x, axis=-1, keepdims=True) + norm_eps)


def chunk_forward(
    pre_ref, rim_ref, scal_ref, rate_ref, taps_ref, marks_ref, docs_ref,
    send_ref, p_ref, z_ref, x_ref, uw_ref, ext_ref,
):
    inner = HEADS * DK
    ext_ref[0:HALO, :] = rim_ref[...].astype(f32)
    ext_ref[HALO:, :] = pre_ref[...].astype(f32)
    marks = marks_ref[0]
    weights = taps_ref[...]
    strength, total, total_t, causal, below = decays(
        scal_ref[...], rate_ref[...], marks, docs_ref[0]
    )
    rows, cols = iotas()
    reached, tail = marks[:, 3:4], marks[:, 4:5]
    heads = []
    for h in range(HEADS):
        acts = []
        for c in range(3):
            conv = conv_parts(ext_ref, weights, marks, c * inner + h * DK)
            acts.append(conv * sigmoid(conv))
        q = (acts[0] * unit_scale(acts[0])).astype(bf16)
        k = (acts[1] * unit_scale(acts[1])).astype(bf16)
        v = acts[2].astype(bf16)
        c_col = total[:, HEADS + h : HEADS + h + 1]
        c_row = total_t[HEADS + h : HEADS + h + 1, :]
        decay = jnp.where(causal, jnp.exp(jnp.where(causal, c_col - c_row, 0.0)), 0.0)
        b = strength[:, h : h + 1]
        gram = dot1(k, k, NT)
        strict = jnp.where(below, b * gram * decay, 0.0)
        heads.append((q, k, v, c_col, decay, b, strict))
    inverses = unit_inverses([head[6] for head in heads])
    for h in range(HEADS):
        q, k, v, c_col, decay, b, strict = heads[h]
        x = inverses[h]
        start = jnp.exp(c_col) * reached
        kf = k.astype(f32)
        uw = dot3(x, jnp.concatenate([b * v.astype(f32), (b * start) * kf], axis=1))
        scores = dot1(q, k, NT) * decay
        suw = dot3(scores, uw)
        last = c_col[TOK - 1 : TOK, :]
        tail_k = kf * (jnp.exp(last - c_col) * tail)
        carry = jnp.exp(last) * reached[TOK - 1 : TOK, :]
        u, w = uw[:, :DK], uw[:, DK:]
        move = jnp.where(rows == cols, carry, 0.0) - dot3(tail_k, w, TN)
        offset_t = dot3(u, tail_k, TN)
        p_ref[h] = (q.astype(f32) * start - suw[:, DK:]).astype(bf16)
        z_ref[h] = suw[:, :DK]
        x_ref[h] = x.astype(bf16)
        uw_ref[h] = uw
        quarter = DK // HEADS
        for j in range(HEADS):
            send_ref[HEADS * h + j, 0:DK, :] = move.astype(bf16)
            send_ref[HEADS * h + j, DK : DK + quarter, :] = offset_t[
                j * quarter : (j + 1) * quarter
            ].astype(bf16)


def scan_forward(got_ref, out_ref):
    state = jnp.zeros((DK // HEADS, DK), f32)
    for i in range(SEQ):
        out_ref[i] = state.astype(bf16)
        if i + 1 < SEQ:
            high, low = split(state)
            both = dot1(jnp.concatenate([high, low], axis=0), got_ref[i, 0:DK, :], NT)
            half = DK // HEADS
            state = both[:half] + both[half:] + got_ref[i, DK : DK + half, :].astype(f32)


def scan_backward(got_ref, local_ref, out_ref):
    state = jnp.zeros((DK // HEADS, DK), f32)
    for i in range(SEQ - 1, -1, -1):
        out_ref[i] = state.astype(bf16)
        if i > 0:
            high, low = split(state)
            both = dot1(jnp.concatenate([high, low], axis=0), got_ref[i, 0:DK, :])
            half = DK // HEADS
            state = both[:half] + both[half:] + local_ref[i].astype(f32)


def gate_forward(p_ref, z_ref, s_ref, og_ref, gain_ref, heads_ref, gated_ref):
    gain = gain_ref[...]
    for h in range(HEADS):
        lanes = slice(h * DK, (h + 1) * DK)
        out = dot1(p_ref[h], s_ref[h], NT) + z_ref[h]
        heads_ref[:, lanes] = out
        r = lax.rsqrt(jnp.mean(out * out, axis=-1, keepdims=True) + head_eps)
        og = og_ref[:, lanes]
        gated_ref[:, lanes] = (out * r * gain * (og * sigmoid(og))).astype(bf16)


def gate_backward(
    gg_ref, heads_ref, og_ref, gain_ref, p_ref, do_ref, mix_ref, local_ref, gain_out_ref
):
    gain = gain_ref[...]
    total = jnp.zeros((1, DK), f32)
    quarter = DK // HEADS
    for h in range(HEADS):
        lanes = slice(h * DK, (h + 1) * DK)
        out = heads_ref[:, lanes]
        og = og_ref[:, lanes]
        gg = gg_ref[:, lanes]
        r = lax.rsqrt(jnp.mean(out * out, axis=-1, keepdims=True) + head_eps)
        u = out * r
        sig = sigmoid(og)
        w = og * sig
        ggw = gg * w
        g = ggw * gain
        total = total + jnp.sum(ggw * u, axis=0, keepdims=True)
        grad = r * (g - u * jnp.mean(g * u, axis=-1, keepdims=True))
        do_ref[:, lanes] = grad
        mix_ref[:, lanes] = (gg * gain * u * sig * (1.0 + og * (1.0 - sig))).astype(bf16)
        local = dot1(grad, p_ref[h], TN).astype(bf16)
        for j in range(HEADS):
            local_ref[HEADS * h + j] = local[j * quarter : (j + 1) * quarter]

    @pl.when(pl.program_id(0) == 0)
    def _():
        gain_out_ref[...] = jnp.zeros_like(gain_out_ref)

    gain_out_ref[0:1, :] += total


def chunk_backward(
    pre_ref, rim_ref, scal_ref, rate_ref, taps_ref, marks_ref, docs_ref,
    x_ref, uw_ref, s_ref, d_ref, do_ref,
    gpre_ref, grim_ref, gscal_ref, gtaps_ref, grate_ref, ext_ref, gext_ref,
):
    inner = HEADS * DK
    ext_ref[0:HALO, :] = rim_ref[...].astype(f32)
    ext_ref[HALO:, :] = pre_ref[...].astype(f32)
    gext_ref[...] = jnp.zeros_like(gext_ref)

    @pl.when(pl.program_id(0) == 0)
    def _():
        gtaps_ref[...] = jnp.zeros_like(gtaps_ref)
        grate_ref[...] = jnp.zeros_like(grate_ref)

    marks = marks_ref[0]
    weights = taps_ref[...]
    scal = scal_ref[...]
    rates = rate_ref[...]
    strength, total, total_t, causal, below = decays(scal, rates, marks, docs_ref[0])
    rows, cols = iotas()
    reached, tail = marks[:, 3:4], marks[:, 4:5]
    grad_b = jnp.zeros((TOK, TOK), f32)
    grad_c = jnp.zeros((TOK, TOK), f32)
    for h in range(HEADS):
        convs, sigs, acts = [], [], []
        for c in range(3):
            conv = conv_parts(ext_ref, weights, marks, c * inner + h * DK)
            sig = sigmoid(conv)
            convs.append(conv)
            sigs.append(sig)
            acts.append(conv * sig)
        nq, nk = unit_scale(acts[0]), unit_scale(acts[1])
        q_hat, k_hat = acts[0] * nq, acts[1] * nk
        q, k, v = q_hat.astype(bf16), k_hat.astype(bf16), acts[2].astype(bf16)
        qf, kf, vf = q.astype(f32), k.astype(f32), v.astype(f32)
        c_col = total[:, HEADS + h : HEADS + h + 1]
        c_row = total_t[HEADS + h : HEADS + h + 1, :]
        decay = jnp.where(causal, jnp.exp(jnp.where(causal, c_col - c_row, 0.0)), 0.0)
        strict_decay = jnp.where(below, decay, 0.0)
        b = strength[:, h : h + 1]
        gram_decay = dot1(k, k, NT) * strict_decay
        scores = dot1(q, k, NT) * decay
        start = jnp.exp(c_col) * reached
        last = c_col[TOK - 1 : TOK, :]
        tail_decay = jnp.exp(last - c_col) * tail
        tail_k = kf * tail_decay
        carry = jnp.exp(last) * reached[TOK - 1 : TOK, :]
        state, adj = s_ref[h], d_ref[h]
        do = do_ref[:, h * DK : (h + 1) * DK].astype(bf16)
        fresh = uw_ref[h, :, :DK] - dot1(uw_ref[h, :, DK:], state, NT)
        fresh = fresh.astype(bf16)
        recalled = dot1(k, state, NT)
        d_fresh = dot1(scores, do, TN) + dot1(tail_k, adj, NT)
        d_scores = dot1(do, fresh, NT)
        score_pull = d_scores * scores
        d_qk = (d_scores * decay).astype(bf16)
        do_state = dot1(do, state)
        d_q = dot1(d_qk, k) + start * do_state
        d_start = jnp.sum(qf * do_state, axis=-1, keepdims=True)
        d_r = dot1(x_ref[h], d_fresh, TN)
        d_v = b * d_r
        d_b = jnp.sum(d_r * (vf - start * recalled), axis=-1, keepdims=True)
        d_start = d_start - jnp.sum(d_v * recalled, axis=-1, keepdims=True)
        d_k = -start * dot1(d_v, state)
        d_strict = -dot1(d_r, fresh, NT)
        strict_pull = d_strict * gram_decay
        d_b = d_b + jnp.sum(strict_pull, axis=-1, keepdims=True)
        d_gram = (d_strict * (b * strict_decay)).astype(bf16)
        d_k = d_k + dot1(d_gram, k) + dot1(d_gram, k, TN) + dot1(d_qk, q, TN)
        fresh_adj = dot1(fresh, adj)
        d_k = d_k + tail_decay * fresh_adj
        d_tail = jnp.sum(kf * fresh_adj, axis=-1, keepdims=True) * tail_decay
        d_carry = jnp.sum(
            jnp.sum(adj.astype(f32) * state.astype(f32), axis=-1, keepdims=True),
            axis=0, keepdims=True,
        )
        pull = score_pull + b * strict_pull
        d_c = jnp.sum(pull - jnp.transpose(pull), axis=-1, keepdims=True)
        d_c = d_c + d_start * start - d_tail
        d_last = d_carry * carry + jnp.sum(d_tail, axis=0, keepdims=True)
        d_c = d_c + jnp.where(rows[:, 0:1] == TOK - 1, d_last, 0.0)
        grad_b = jnp.where(cols == h, d_b, grad_b)
        grad_c = jnp.where(cols == HEADS + h, d_c, grad_c)
        d_acts = (
            nq * (d_q - q_hat * jnp.sum(d_q * q_hat, axis=-1, keepdims=True)),
            nk * (d_k - k_hat * jnp.sum(d_k * k_hat, axis=-1, keepdims=True)),
            d_v,
        )
        for c in range(3):
            lane = c * inner + h * DK
            d_conv = d_acts[c] * sigs[c] * (1.0 + convs[c] * (1.0 - sigs[c]))
            for tap in range(TAPS):
                kept = d_conv * marks[:, tap : tap + 1] if tap < TAPS - 1 else d_conv
                place = (pl.ds(HALO - TAPS + 1 + tap, TOK), pl.ds(lane, DK))
                gtaps_ref[tap : tap + 1, lane : lane + DK] += jnp.sum(
                    kept * ext_ref[place], axis=0, keepdims=True
                )
                gext_ref[place] += kept * weights[tap : tap + 1, lane : lane + DK]
    upper = (cols >= rows).astype(bf16)
    grad_ld = dot2(upper, grad_c)
    decay_side = -grad_ld * rates * sigmoid(scal)
    gscal_ref[...] = jnp.where(
        cols < HEADS,
        grad_b * strength * (1.0 - strength),
        jnp.where(cols < 2 * HEADS, decay_side, 0.0),
    ).astype(bf16)
    grate_ref[0:1, :] += -jnp.sum(grad_ld * softplus(scal), axis=0, keepdims=True)
    gpre_ref[...] = gext_ref[HALO:, :]
    grim_ref[...] = gext_ref[0:HALO, :].astype(bf16)


def cost(flops, moved):
    return pl.CostEstimate(flops=flops, bytes_accessed=moved, transcendentals=0)


def params():
    return pltpu.CompilerParams(vmem_limit_bytes=VMEM)


def whole(shape):
    return pl.BlockSpec(shape, lambda s: (0,) * len(shape))


def by_rows(rows, cols, base=0, lane=0):
    return pl.BlockSpec((rows, cols), lambda s: (base + s, lane))


def by_lead(*shape):
    return pl.BlockSpec(shape, lambda s: (s,) + (0,) * (len(shape) - 1))


def mixer_specs():
    wide = 3 * HEADS * DK
    return [
        by_rows(TOK, wide),
        by_rows(HALO, wide, 2 * TOK // HALO),
        by_rows(TOK, 128),
        whole((1, 128)),
        whole((TAPS, wide)),
        by_lead(1, TOK, 8),
        by_lead(1, 1, TOK),
    ]


def run_chunk_forward(pre, scal, rates, taps, marks, docs):
    quarter = DK // HEADS
    wide = 3 * HEADS * DK
    return pl.pallas_call(
        chunk_forward,
        grid=(2,),
        in_specs=mixer_specs(),
        out_specs=[
            by_lead(16, DK + quarter, DK),
            by_lead(HEADS, TOK, DK),
            by_lead(HEADS, TOK, DK),
            by_lead(HEADS, TOK, DK),
            by_lead(HEADS, TOK, 2 * DK),
        ],
        out_shape=[
            jax.ShapeDtypeStruct((SEQ, DK + quarter, DK), bf16),
            jax.ShapeDtypeStruct((8, TOK, DK), bf16),
            jax.ShapeDtypeStruct((8, TOK, DK), f32),
            jax.ShapeDtypeStruct((8, TOK, DK), bf16),
            jax.ShapeDtypeStruct((8, TOK, 2 * DK), f32),
        ],
        scratch_shapes=[pltpu.VMEM((HALO + TOK, wide), f32)],
        compiler_params=params(),
        cost_estimate=cost(10**10, 6 * 10**6),
    )(pre, pre, scal, rates, taps, marks, docs)


def run_scan_forward(got):
    return pl.pallas_call(
        scan_forward,
        out_shape=jax.ShapeDtypeStruct((SEQ, DK // HEADS, DK), bf16),
        compiler_params=params(),
        cost_estimate=cost(10**9, 3 * 10**6),
    )(got)


def run_scan_backward(got, local):
    return pl.pallas_call(
        scan_backward,
        out_shape=jax.ShapeDtypeStruct((SEQ, DK // HEADS, DK), bf16),
        compiler_params=params(),
        cost_estimate=cost(10**9, 3 * 10**6),
    )(got, local)


def run_gate_forward(p, z, state, og, gain):
    inner = HEADS * DK
    return pl.pallas_call(
        gate_forward,
        grid=(2,),
        in_specs=[
            by_lead(HEADS, TOK, DK),
            by_lead(HEADS, TOK, DK),
            by_lead(HEADS, DK, DK),
            by_rows(TOK, inner),
            whole((1, DK)),
        ],
        out_specs=[by_rows(TOK, inner), by_rows(TOK, inner)],
        out_shape=[
            jax.ShapeDtypeStruct((2 * TOK, inner), f32),
            jax.ShapeDtypeStruct((2 * TOK, inner), bf16),
        ],
        compiler_params=params(),
        cost_estimate=cost(10**9, 3 * 10**6),
    )(p, z, state, og, gain)


def run_gate_backward(gg, heads_out, og, gain, p):
    inner = HEADS * DK
    return pl.pallas_call(
        gate_backward,
        grid=(2,),
        in_specs=[
            by_rows(TOK, inner),
            by_rows(TOK, inner),
            by_rows(TOK, inner),
            whole((1, DK)),
            by_lead(HEADS, TOK, DK),
        ],
        out_specs=[
            by_rows(TOK, inner),
            by_rows(TOK, inner),
            by_lead(16, DK // HEADS, DK),
            whole((8, DK)),
        ],
        out_shape=[
            jax.ShapeDtypeStruct((2 * TOK, inner), f32),
            jax.ShapeDtypeStruct((2 * TOK, inner), bf16),
            jax.ShapeDtypeStruct((SEQ, DK // HEADS, DK), bf16),
            jax.ShapeDtypeStruct((8, DK), f32),
        ],
        compiler_params=params(),
        cost_estimate=cost(10**9, 3 * 10**6),
    )(gg, heads_out, og, gain, p)


def run_chunk_backward(pre, scal, rates, taps, marks, docs, x, uw, state, adj, do):
    inner = HEADS * DK
    wide = 3 * inner
    return pl.pallas_call(
        chunk_backward,
        grid=(2,),
        in_specs=mixer_specs()
        + [
            by_lead(HEADS, TOK, DK),
            by_lead(HEADS, TOK, 2 * DK),
            by_lead(HEADS, DK, DK),
            by_lead(HEADS, DK, DK),
            by_rows(TOK, inner),
        ],
        out_specs=[
            by_rows(TOK, wide),
            by_rows(HALO, wide),
            by_rows(TOK, 128),
            whole((TAPS, wide)),
            whole((8, 128)),
        ],
        out_shape=[
            jax.ShapeDtypeStruct((2 * TOK, wide), f32),
            jax.ShapeDtypeStruct((2 * HALO, wide), bf16),
            jax.ShapeDtypeStruct((2 * TOK, 128), bf16),
            jax.ShapeDtypeStruct((TAPS, wide), f32),
            jax.ShapeDtypeStruct((8, 128), f32),
        ],
        scratch_shapes=[
            pltpu.VMEM((HALO + TOK, wide), f32),
            pltpu.VMEM((HALO + TOK, wide), f32),
        ],
        compiler_params=params(),
        cost_estimate=cost(10**10, 10**7),
    )(pre, pre, scal, rates, taps, marks, docs, x, uw, state, adj, do)


def passed_along(array, by):
    pairs = [(i, i + by) for i in range(SEQ) if 0 <= i + by < SEQ]
    return lax.ppermute(array, "seq", pairs)


STRIDE = {"x": (8, 4), "z": (2, 4), "y": (1, 2)}


def along(array, axis, by):
    stride, count = STRIDE[axis]
    pairs = []
    for i in range(SEQ):
        place = (i // stride) % count
        pairs.append((i, i + ((place + by) % count - place) * stride))
    return lax.ppermute(array, "seq", pairs)


def place_of(axis):
    stride, count = STRIDE[axis]
    return (lax.axis_index("seq") // stride) % count


def gather_pair(array):
    other = along(array, "y", 1)
    first = place_of("y") == 0
    return jnp.concatenate(
        [jnp.where(first, array, other), jnp.where(first, other, array)], axis=0
    )


def gather_four(array, axis, dim):
    half = array.shape[0] // 2
    left = along(array, axis, 1)
    right = along(array, axis, -1)
    far = jnp.concatenate(
        [along(left[:half], axis, 1), along(right[half:], axis, -1)], axis=0
    )
    place = place_of(axis)
    shape = list(array.shape)
    shape.insert(dim, 4)
    out = jnp.zeros(shape, array.dtype)
    for offset, block in ((0, array), (-1, left), (-2, far), (1, right)):
        out = lax.dynamic_update_index_in_dim(out, block, (place + offset) % 4, dim)
    return out


def gather_rows(left, right):
    left, right = gather_pair(left), gather_pair(right)
    left = gather_four(left, "x", 0)
    right = gather_four(right, "z", 0)
    left = gather_four(left, "z", 1)
    right = gather_four(right, "x", 0)
    return (
        left.reshape(-1, left.shape[-1]),
        right.reshape(-1, right.shape[-1]),
    )


def exchange(array, axis):
    return lax.all_to_all(array, axis, split_axis=0, concat_axis=0, tiled=True)


def head_scatter(partial_rows):
    rows = partial_rows.shape[0] // 4
    got = exchange(partial_rows.astype(bf16).reshape(4, rows, -1), "head")
    return jnp.sum(got.astype(f32), axis=0)


def head_gather(rows):
    got = exchange(jnp.broadcast_to(rows[None], (4,) + rows.shape), "head")
    return got.reshape(4 * rows.shape[0], -1)


def seq_scatter(partial_rows):
    rows = partial_rows.shape[0] // SEQ
    got = exchange(partial_rows.reshape(SEQ, rows, -1), "seq")
    return jnp.sum(got.astype(f32), axis=0)


def mm(a, b, dims="ij,jk->ik"):
    return jnp.einsum(dims, a, b, preferred_element_type=f32)


def row_scale(x):
    return lax.rsqrt(jnp.mean(x * x, axis=-1, keepdims=True) + norm_eps)


def norm_pull(x, scale, gain, grad):
    unit = x * scale
    scaled = grad * gain
    back = scale * (scaled - unit * jnp.mean(scaled * unit, axis=-1, keepdims=True))
    return back, jnp.sum(grad * unit, axis=0)


def doc_tables(doc_lengths):
    first = lax.axis_index("seq") * TOK - (TAPS - 1)
    ends = jnp.cumsum(doc_lengths, axis=1)
    places = first + jnp.arange(TOK + TAPS - 1, dtype=jnp.int32)
    counted = jnp.sum((places[None, :, None] >= ends[:, None, :]).astype(jnp.int32), axis=2)
    ext = jnp.where(places[None, :] >= 0, counted, -1)
    local = ext[:, TAPS - 1 :]
    columns = [(ext[:, o : o + TOK] == local) for o in range(TAPS - 1)]
    columns.append(local == ext[:, TAPS - 2 : TAPS - 1])
    columns.append(local == local[:, -1:])
    columns.append(local)
    columns += [jnp.zeros_like(local)] * 2
    marks = jnp.stack([c.astype(f32) for c in columns], axis=-1)
    return marks, local.astype(f32)[:, None, :]


def body(
    inputs, doc_lengths, norm_in, query_weight, key_weight, value_weight, outgate_weight,
    scalar_weight, conv_kernel, decay_rate, head_norm, output_weight, norm_ffn, gate_weight,
    up_weight, down_weight, grad_out,
):
    width = inputs.shape[2]
    inner = HEADS * DK
    hidden = gate_weight.shape[1]
    head_index = lax.axis_index("head")
    quarter = 2 * TOK // HEADS

    gains = jnp.stack([norm_in, norm_ffn] + [jnp.zeros_like(norm_in)] * 14)
    gains = exchange(jnp.broadcast_to(gains[None], (SEQ,) + gains.shape), "seq")
    gain_in = gains[:, 0].reshape(1, width).astype(f32)
    gain_ffn = gains[:, 1].reshape(1, width).astype(f32)

    misc = jnp.pad(scalar_weight.reshape(-1, 2 * HEADS), ((0, 0), (0, 128 - 2 * HEADS)))
    w_left, w_right = gather_rows(
        jnp.concatenate([query_weight, key_weight, misc], axis=1),
        jnp.concatenate([value_weight, outgate_weight], axis=1),
    )
    packed = jnp.concatenate(
        [gate_weight, up_weight, down_weight.T, output_weight.T], axis=1
    )
    w_late = lax.all_gather(packed, "seq", axis=0, tiled=True)
    w_gateup = w_late[:, : 2 * hidden]
    w_down_t = w_late[:, 2 * hidden : 3 * hidden]
    w_out_t = w_late[:, 3 * hidden :]

    marks, docs_row = doc_tables(doc_lengths)
    taps = jnp.transpose(conv_kernel.astype(f32), (1, 0, 2)).reshape(TAPS, 3 * inner)
    rates = jnp.zeros((1, 128), f32)
    rates = rates.at[0, HEADS : 2 * HEADS].set(decay_rate.astype(f32))
    gain_head = head_norm.astype(f32).reshape(1, DK)

    halo = passed_along(inputs[:, TOK - HALO :], 1)
    tokens = inputs.reshape(2 * TOK, width)
    all_rows = jnp.concatenate([tokens, halo.reshape(2 * HALO, width)], axis=0).astype(f32)
    normed_all = (all_rows * row_scale(all_rows) * gain_in).astype(bf16)
    normed_in = normed_all[: 2 * TOK]

    qk_misc = mm(normed_all, w_left)
    v_gate = mm(normed_all, w_right)
    pre = jnp.concatenate(
        [qk_misc[:, : 2 * inner].astype(bf16), v_gate[:, :inner].astype(bf16)], axis=1
    )
    scal = qk_misc[: 2 * TOK, 2 * inner :]
    out_gate = v_gate[: 2 * TOK, inner:]

    send, p, z, x, uw = run_chunk_forward(pre, scal, rates, taps, marks, docs_row)
    got = exchange(send, "seq")
    state = exchange(run_scan_forward(got), "seq").reshape(8, DK, DK)
    heads_out, gated_rows = run_gate_forward(p, z, state, out_gate, gain_head)

    mine = partial(lax.dynamic_slice_in_dim, start_index=head_index * quarter, slice_size=quarter)
    residual = mine(tokens).astype(f32) + head_scatter(mm(gated_rows, w_out_t, "ij,kj->ik"))
    scale_ffn = row_scale(residual)
    normed_ffn = head_gather((residual * scale_ffn * gain_ffn).astype(bf16))

    grad_rows = grad_out.reshape(2 * TOK, width)
    grad_act = mm(grad_rows, w_down_t)
    gate_up = mm(normed_ffn, w_gateup)
    gate, up = gate_up[:, :hidden], gate_up[:, hidden:]
    sig = sigmoid(gate)
    silu = gate * sig
    product = (silu * up).astype(bf16)
    gu_grad = jnp.concatenate(
        [
            (grad_act * up * sig * (1.0 + gate * (1.0 - sig))).astype(bf16),
            (grad_act * silu).astype(bf16),
        ],
        axis=1,
    )
    grad_normed = head_scatter(mm(gu_grad, w_gateup, "ij,kj->ik"))
    back, part_gain_ffn = norm_pull(residual, scale_ffn, gain_ffn, grad_normed)
    grad_residual = mine(grad_rows).astype(f32) + back
    grad_mixer = head_gather(grad_residual.astype(bf16))

    outputs = residual + head_scatter(mm(product, w_down_t, "ij,kj->ik"))
    outputs = head_gather(outputs.astype(bf16))

    grad_gated = mm(grad_mixer, w_out_t)
    do, gate_grad_mix, local, part_gain_head = run_gate_backward(
        grad_gated, heads_out, out_gate, gain_head, p
    )
    adj = exchange(run_scan_backward(got, exchange(local, "seq")), "seq").reshape(8, DK, DK)
    gpre, grim, gscal, gtaps, grate = run_chunk_backward(
        pre, scal, rates, taps, marks, docs_row, x, uw, state, adj, do
    )
    rim = passed_along(grim, -1).astype(f32).reshape(2, HALO, 3 * inner)
    gpre = gpre.reshape(2, TOK, 3 * inner).at[:, TOK - HALO :].add(rim)
    gpre = gpre.astype(bf16).reshape(2 * TOK, 3 * inner)

    input_part = mm(
        jnp.concatenate([gpre[:, : 2 * inner], gscal], axis=1), w_left, "ij,kj->ik"
    ) + mm(jnp.concatenate([gpre[:, 2 * inner :], gate_grad_mix], axis=1), w_right, "ij,kj->ik")
    grad_normed_in = head_scatter(input_part)
    own = mine(tokens).astype(f32)
    back_in, part_gain_in = norm_pull(own, row_scale(own), gain_in, grad_normed_in)
    grad_in = head_gather((grad_residual + back_in).astype(bf16)).astype(f32)

    grad_down = seq_scatter(mm(grad_rows, product, "ti,tj->ij").astype(bf16))
    grad_gateup = seq_scatter(mm(normed_ffn, gu_grad, "ti,tj->ij").astype(bf16))
    grad_out_w = seq_scatter(mm(grad_mixer, gated_rows, "ti,tj->ij").astype(bf16))
    grad_mix = seq_scatter(
        mm(
            normed_in, jnp.concatenate([gpre, gate_grad_mix, gscal], axis=1), "ti,tj->ij"
        ).astype(bf16)
    )

    small = jnp.concatenate([gtaps.reshape(12, inner), jnp.zeros((4, inner), f32)], axis=0)
    tail = jnp.concatenate([part_gain_head[0], grate[0], jnp.zeros((inner - 256,), f32)])
    small = jnp.broadcast_to(small.at[12].set(tail)[None], (SEQ, 16, inner))
    own_gains = jnp.pad(
        jnp.stack([part_gain_in.reshape(SEQ, -1), part_gain_ffn.reshape(SEQ, -1)], axis=1),
        ((0, 0), (0, 0), (0, inner - width // SEQ)),
    )
    small = small.at[:, 13:15].set(own_gains)
    small = jnp.sum(exchange(small, "seq"), axis=0)
    across = jnp.pad(small[12:15], ((0, 5), (0, 0)))
    across = jnp.sum(exchange(jnp.broadcast_to(across[None], (4, 8, inner)), "head"), axis=0)
    grad_conv = jnp.transpose(small[:12].reshape(TAPS, 3, inner), (1, 0, 2))
    rows = width // SEQ
    return (
        outputs.reshape(inputs.shape),
        grad_in.reshape(inputs.shape),
        across[1, :rows],
        grad_mix[:, :inner],
        grad_mix[:, inner : 2 * inner],
        grad_mix[:, 2 * inner : 3 * inner],
        grad_mix[:, 3 * inner : 4 * inner],
        grad_mix[:, 4 * inner : 4 * inner + 2 * HEADS].reshape(rows, 2, HEADS),
        grad_conv,
        small[12, DK + HEADS : DK + 2 * HEADS],
        across[0, :DK],
        grad_out_w.T,
        across[2, :rows],
        grad_gateup[:, :hidden],
        grad_gateup[:, hidden:],
        grad_down.T,
    )


def solution(mesh):
    weight = P("seq", "head")
    weight_t = P("head", "seq")
    tokens = P(None, "seq", None)
    scalars = P("seq", None, "head")
    taps = P(None, None, "head")
    return jax.shard_map(
        body,
        mesh=mesh,
        in_specs=(
            tokens, P(), P("seq"), weight, weight, weight, weight, scalars, taps, P("head"), P(),
            weight_t, P("seq"), weight, weight, weight_t, tokens,
        ),
        out_specs=(
            tokens, tokens, P("seq"), weight, weight, weight, weight, scalars, taps, P("head"),
            P(), weight_t, P("seq"), weight, weight, weight_t,
        ),
        check_vma=False,
    )
```

```python
from functools import partial

import jax
import jax.numpy as jnp
from jax import lax
from jax.experimental import pallas as pl
from jax.experimental.pallas import tpu as pltpu
from jax.sharding import Mesh
from jax.sharding import PartitionSpec as P

f32 = jnp.float32
bf16 = jnp.bfloat16
norm_eps = 1e-06
head_eps = 1e-05
SEQ = 32
HEADS = 4
DK = 128
TOK = 128
TAPS = 4
HALO = 16
VMEM = 56 * 1024 * 1024

NN = (((1,), (0,)), ((), ()))
NT = (((1,), (1,)), ((), ()))
TN = (((0,), (0,)), ((), ()))


def dot1(a, b, dims=NN):
    return lax.dot_general(a.astype(bf16), b.astype(bf16), dims, preferred_element_type=f32)


def split(a):
    high = a.astype(bf16)
    return high, (a - high.astype(f32)).astype(bf16)


def dot3(a, b, dims=NN):
    ah, al = split(a)
    bh, bl = split(b)
    return dot1(ah, bh, dims) + (dot1(ah, bl, dims) + dot1(al, bh, dims))


def dot2(exact, b, dims=NN):
    high = b.astype(bf16)
    rest = b - high.astype(f32)
    mid = rest.astype(bf16)
    low = (rest - mid.astype(f32)).astype(bf16)
    return dot1(exact, high, dims) + (dot1(exact, mid, dims) + dot1(exact, low, dims))


def sigmoid(x):
    return 1.0 / (1.0 + jnp.exp(-x))


def softplus(x):
    return jnp.maximum(x, 0.0) + jnp.log1p(jnp.exp(-jnp.abs(x)))


def iotas():
    rows = lax.broadcasted_iota(jnp.int32, (TOK, TOK), 0)
    cols = lax.broadcasted_iota(jnp.int32, (TOK, TOK), 1)
    return rows, cols


def unit_inverses(stricts):
    rows, cols = iotas()
    eye = (rows == cols).astype(f32)
    apart = jnp.bitwise_xor(rows, cols)
    results = []
    first = (apart == 1) & (rows > cols)
    results = [eye - jnp.where(first, a, 0.0) for a in stricts]
    size = 2
    while size < TOK:
        corner = (apart >= size) & (apart < 2 * size) & (rows > cols)
        parts = [dot3(jnp.where(corner, a, 0.0), x) for a, x in zip(stricts, results)]
        results = [x - dot3(x, c) for x, c in zip(results, parts)]
        size *= 2
    return results


def decays(scal, rates, marks, docs_row):
    rows, cols = iotas()
    strength = sigmoid(scal)
    log_decay = -rates * softplus(scal)
    lower = (rows >= cols).astype(bf16)
    total = dot2(lower, log_decay)
    total_t = jnp.transpose(total)
    same = marks[:, 5:6] == docs_row
    causal = same & (rows >= cols)
    return strength, total, total_t, causal, rows > cols


def conv_parts(ext_ref, weights, marks, lane):
    out = None
    for tap in range(TAPS):
        piece = ext_ref[pl.ds(HALO - TAPS + 1 + tap, TOK), pl.ds(lane, DK)]
        if tap < TAPS - 1:
            piece = piece * marks[:, tap : tap + 1]
        piece = piece * weights[tap : tap + 1, lane : lane + DK]
        out = piece if out is None else out + piece
    return out


def unit_scale(x):
    return lax.rsqrt(jnp.sum(x * x, axis=-1, keepdims=True) + norm_eps)


def chunk_forward(
    pre_ref, rim_ref, scal_ref, rate_ref, taps_ref, marks_ref, docs_ref,
    send_ref, p_ref, z_ref, x_ref, uw_ref, ext_ref,
):
    inner = HEADS * DK
    ext_ref[0:HALO, :] = rim_ref[...].astype(f32)
    ext_ref[HALO:, :] = pre_ref[...].astype(f32)
    marks = marks_ref[0]
    weights = taps_ref[...]
    strength, total, total_t, causal, below = decays(
        scal_ref[...], rate_ref[...], marks, docs_ref[0]
    )
    rows, cols = iotas()
    reached, tail = marks[:, 3:4], marks[:, 4:5]
    heads = []
    for h in range(HEADS):
        acts = []
        for c in range(3):
            conv = conv_parts(ext_ref, weights, marks, c * inner + h * DK)
            acts.append(conv * sigmoid(conv))
        q = (acts[0] * unit_scale(acts[0])).astype(bf16)
        k = (acts[1] * unit_scale(acts[1])).astype(bf16)
        v = acts[2].astype(bf16)
        c_col = total[:, HEADS + h : HEADS + h + 1]
        c_row = total_t[HEADS + h : HEADS + h + 1, :]
        decay = jnp.where(causal, jnp.exp(jnp.where(causal, c_col - c_row, 0.0)), 0.0)
        b = strength[:, h : h + 1]
        gram = dot1(k, k, NT)
        strict = jnp.where(below, b * gram * decay, 0.0)
        heads.append((q, k, v, c_col, decay, b, strict))
    inverses = unit_inverses([head[6] for head in heads])
    for h in range(HEADS):
        q, k, v, c_col, decay, b, strict = heads[h]
        x = inverses[h]
        start = jnp.exp(c_col) * reached
        kf = k.astype(f32)
        uw = dot3(x, jnp.concatenate([b * v.astype(f32), (b * start) * kf], axis=1))
        scores = dot1(q, k, NT) * decay
        suw = dot3(scores, uw)
        last = c_col[TOK - 1 : TOK, :]
        tail_k = kf * (jnp.exp(last - c_col) * tail)
        carry = jnp.exp(last) * reached[TOK - 1 : TOK, :]
        u, w = uw[:, :DK], uw[:, DK:]
        move = jnp.where(rows == cols, carry, 0.0) - dot3(tail_k, w, TN)
        offset_t = dot3(u, tail_k, TN)
        p_ref[h] = (q.astype(f32) * start - suw[:, DK:]).astype(bf16)
        z_ref[h] = suw[:, :DK]
        x_ref[h] = x.astype(bf16)
        uw_ref[h] = uw
        quarter = DK // HEADS
        for j in range(HEADS):
            send_ref[HEADS * h + j, 0:DK, :] = move.astype(bf16)
            send_ref[HEADS * h + j, DK : DK + quarter, :] = offset_t[
                j * quarter : (j + 1) * quarter
            ].astype(bf16)


def scan_forward(got_ref, out_ref):
    state = jnp.zeros((DK // HEADS, DK), f32)
    for i in range(SEQ):
        out_ref[i] = state.astype(bf16)
        if i + 1 < SEQ:
            high, low = split(state)
            both = dot1(jnp.concatenate([high, low], axis=0), got_ref[i, 0:DK, :], NT)
            half = DK // HEADS
            state = both[:half] + both[half:] + got_ref[i, DK : DK + half, :].astype(f32)


def scan_backward(got_ref, local_ref, out_ref):
    state = jnp.zeros((DK // HEADS, DK), f32)
    for i in range(SEQ - 1, -1, -1):
        out_ref[i] = state.astype(bf16)
        if i > 0:
            high, low = split(state)
            both = dot1(jnp.concatenate([high, low], axis=0), got_ref[i, 0:DK, :])
            half = DK // HEADS
            state = both[:half] + both[half:] + local_ref[i].astype(f32)


def gate_forward(p_ref, z_ref, s_ref, og_ref, gain_ref, heads_ref, gated_ref):
    gain = gain_ref[...]
    for h in range(HEADS):
        lanes = slice(h * DK, (h + 1) * DK)
        out = dot1(p_ref[h], s_ref[h], NT) + z_ref[h]
        heads_ref[:, lanes] = out
        r = lax.rsqrt(jnp.mean(out * out, axis=-1, keepdims=True) + head_eps)
        og = og_ref[:, lanes]
        gated_ref[:, lanes] = (out * r * gain * (og * sigmoid(og))).astype(bf16)


def gate_backward(
    gg_ref, heads_ref, og_ref, gain_ref, p_ref, do_ref, mix_ref, local_ref, gain_out_ref
):
    gain = gain_ref[...]
    total = jnp.zeros((1, DK), f32)
    quarter = DK // HEADS
    for h in range(HEADS):
        lanes = slice(h * DK, (h + 1) * DK)
        out = heads_ref[:, lanes]
        og = og_ref[:, lanes]
        gg = gg_ref[:, lanes]
        r = lax.rsqrt(jnp.mean(out * out, axis=-1, keepdims=True) + head_eps)
        u = out * r
        sig = sigmoid(og)
        w = og * sig
        ggw = gg * w
        g = ggw * gain
        total = total + jnp.sum(ggw * u, axis=0, keepdims=True)
        grad = r * (g - u * jnp.mean(g * u, axis=-1, keepdims=True))
        do_ref[:, lanes] = grad
        mix_ref[:, lanes] = (gg * gain * u * sig * (1.0 + og * (1.0 - sig))).astype(bf16)
        local = dot1(grad, p_ref[h], TN).astype(bf16)
        for j in range(HEADS):
            local_ref[HEADS * h + j] = local[j * quarter : (j + 1) * quarter]

    @pl.when(pl.program_id(0) == 0)
    def _():
        gain_out_ref[...] = jnp.zeros_like(gain_out_ref)

    gain_out_ref[0:1, :] += total


def conv_acts(ext_ref, weights, marks, lane):
    conv = conv_parts(ext_ref, weights, marks, lane)
    sig = sigmoid(conv)
    return conv, sig, conv * sig


def conv_pull(d_act, conv, sig, ext_ref, gext_ref, gtaps_ref, weights, marks, lane):
    d_conv = d_act * sig * (1.0 + conv * (1.0 - sig))
    for tap in range(TAPS):
        kept = d_conv * marks[:, tap : tap + 1] if tap < TAPS - 1 else d_conv
        place = (pl.ds(HALO - TAPS + 1 + tap, TOK), pl.ds(lane, DK))
        gtaps_ref[tap : tap + 1, lane : lane + DK] += jnp.sum(
            kept * ext_ref[place], axis=0, keepdims=True
        )
        gext_ref[place] += kept * weights[tap : tap + 1, lane : lane + DK]


def store_rows(gpre_ref, gext_ref):
    s = pl.program_id(0)
    gpre_ref[pl.ds(pl.multiple_of(s * TOK, TOK), TOK), :] = gext_ref[HALO:, :].astype(bf16)
    halo = pl.multiple_of(2 * TOK + s * HALO, HALO)
    gpre_ref[pl.ds(halo, HALO), :] = gext_ref[0:HALO, :].astype(bf16)


def unit_pull(d, hat, scale):
    return scale * (d - hat * jnp.sum(d * hat, axis=-1, keepdims=True))


def chunk_backward_early(
    pre_ref, rim_ref, scal_ref, rate_ref, taps_ref, marks_ref, docs_ref,
    uw_ref, s_ref, do_ref,
    gpre_ref, gtaps_ref, fresh_ref, recalled_ref, df_ref, dk_ref, dc_ref, ext_ref, gext_ref,
):
    inner = HEADS * DK
    ext_ref[0:HALO, :] = rim_ref[...].astype(f32)
    ext_ref[HALO:, :] = pre_ref[...].astype(f32)
    gext_ref[...] = jnp.zeros_like(gext_ref)

    @pl.when(pl.program_id(0) == 0)
    def _():
        gtaps_ref[...] = jnp.zeros_like(gtaps_ref)

    marks = marks_ref[0]
    weights = taps_ref[...]
    strength, total, total_t, causal, below = decays(
        scal_ref[...], rate_ref[...], marks, docs_ref[0]
    )
    rows, cols = iotas()
    reached = marks[:, 3:4]
    grad_c = jnp.zeros((TOK, TOK), f32)
    for h in range(HEADS):
        conv, sig, act = conv_acts(ext_ref, weights, marks, h * DK)
        act_k = conv_acts(ext_ref, weights, marks, inner + h * DK)[2]
        nq = unit_scale(act)
        q_hat = act * nq
        q, k = q_hat.astype(bf16), (act_k * unit_scale(act_k)).astype(bf16)
        c_col = total[:, HEADS + h : HEADS + h + 1]
        c_row = total_t[HEADS + h : HEADS + h + 1, :]
        decay = jnp.where(causal, jnp.exp(jnp.where(causal, c_col - c_row, 0.0)), 0.0)
        scores = dot1(q, k, NT) * decay
        start = jnp.exp(c_col) * reached
        state = s_ref[h]
        do = do_ref[:, h * DK : (h + 1) * DK].astype(bf16)
        fresh = uw_ref[h, :, :DK] - dot1(uw_ref[h, :, DK:], state, NT)
        fresh = fresh.astype(bf16)
        fresh_ref[h] = fresh
        recalled_ref[h] = dot1(k, state, NT)
        df_ref[h] = dot1(scores, do, TN)
        d_scores = dot1(do, fresh, NT)
        pull = d_scores * scores
        d_qk = (d_scores * decay).astype(bf16)
        dk_ref[h] = dot1(d_qk, q, TN)
        do_state = dot1(do, state)
        d_q = dot1(d_qk, k) + start * do_state
        d_start = jnp.sum(q.astype(f32) * do_state, axis=-1, keepdims=True)
        d_c = jnp.sum(pull - jnp.transpose(pull), axis=-1, keepdims=True) + d_start * start
        grad_c = jnp.where(cols == HEADS + h, d_c, grad_c)
        conv_pull(
            unit_pull(d_q, q_hat, nq), conv, sig, ext_ref, gext_ref, gtaps_ref, weights, marks,
            h * DK,
        )
    dc_ref[...] = grad_c
    store_rows(gpre_ref, gext_ref)


def chunk_backward_late(
    pre_ref, rim_ref, scal_ref, rate_ref, taps_ref, marks_ref, docs_ref,
    x_ref, s_ref, d_ref, fresh_ref, recalled_ref, df_ref, dk_ref, dc_ref,
    gpre_ref, gscal_ref, gtaps_ref, grate_ref, ext_ref, gext_ref,
):
    inner = HEADS * DK
    ext_ref[0:HALO, :] = rim_ref[:, inner:].astype(f32)
    ext_ref[HALO:, :] = pre_ref[:, inner:].astype(f32)
    gext_ref[...] = jnp.zeros_like(gext_ref)

    @pl.when(pl.program_id(0) == 0)
    def _():
        gtaps_ref[...] = jnp.zeros_like(gtaps_ref)
        grate_ref[...] = jnp.zeros_like(grate_ref)

    marks = marks_ref[0]
    weights = taps_ref[:, inner:]
    scal = scal_ref[...]
    rates = rate_ref[...]
    strength, total, total_t, causal, below = decays(scal, rates, marks, docs_ref[0])
    rows, cols = iotas()
    reached, tail = marks[:, 3:4], marks[:, 4:5]
    grad_b = jnp.zeros((TOK, TOK), f32)
    grad_c = jnp.zeros((TOK, TOK), f32)
    for h in range(HEADS):
        conv_k, sig_k, act_k = conv_acts(ext_ref, weights, marks, h * DK)
        conv_v, sig_v, act_v = conv_acts(ext_ref, weights, marks, inner + h * DK)
        nk = unit_scale(act_k)
        k_hat = act_k * nk
        k, v = k_hat.astype(bf16), act_v.astype(bf16)
        kf, vf = k.astype(f32), v.astype(f32)
        c_col = total[:, HEADS + h : HEADS + h + 1]
        c_row = total_t[HEADS + h : HEADS + h + 1, :]
        strict = causal & below
        strict_decay = jnp.where(strict, jnp.exp(jnp.where(strict, c_col - c_row, 0.0)), 0.0)
        b = strength[:, h : h + 1]
        gram_decay = dot1(k, k, NT) * strict_decay
        start = jnp.exp(c_col) * reached
        last = c_col[TOK - 1 : TOK, :]
        tail_decay = jnp.exp(last - c_col) * tail
        carry = jnp.exp(last) * reached[TOK - 1 : TOK, :]
        state, adj = s_ref[h], d_ref[h]
        fresh, recalled = fresh_ref[h], recalled_ref[h]
        d_fresh = df_ref[h] + dot1(kf * tail_decay, adj, NT)
        d_r = dot1(x_ref[h], d_fresh, TN)
        d_v = b * d_r
        d_b = jnp.sum(d_r * (vf - start * recalled), axis=-1, keepdims=True)
        d_start = -jnp.sum(d_v * recalled, axis=-1, keepdims=True)
        d_strict = -dot1(d_r, fresh, NT)
        strict_pull = d_strict * gram_decay
        d_b = d_b + jnp.sum(strict_pull, axis=-1, keepdims=True)
        d_gram = (d_strict * (b * strict_decay)).astype(bf16)
        d_k = dk_ref[h] - start * dot1(d_v, state) + dot1(d_gram, k) + dot1(d_gram, k, TN)
        fresh_adj = dot1(fresh, adj)
        d_k = d_k + tail_decay * fresh_adj
        d_tail = jnp.sum(kf * fresh_adj, axis=-1, keepdims=True) * tail_decay
        d_carry = jnp.sum(
            jnp.sum(adj.astype(f32) * state.astype(f32), axis=-1, keepdims=True),
            axis=0, keepdims=True,
        )
        pull = b * strict_pull
        d_c = jnp.sum(pull - jnp.transpose(pull), axis=-1, keepdims=True)
        d_c = d_c + d_start * start - d_tail
        d_last = d_carry * carry + jnp.sum(d_tail, axis=0, keepdims=True)
        d_c = d_c + jnp.where(rows[:, 0:1] == TOK - 1, d_last, 0.0)
        grad_b = jnp.where(cols == h, d_b, grad_b)
        grad_c = jnp.where(cols == HEADS + h, d_c, grad_c)
        conv_pull(
            unit_pull(d_k, k_hat, nk), conv_k, sig_k, ext_ref, gext_ref, gtaps_ref, weights,
            marks, h * DK,
        )
        conv_pull(
            d_v, conv_v, sig_v, ext_ref, gext_ref, gtaps_ref, weights, marks, inner + h * DK
        )
    upper = (cols >= rows).astype(bf16)
    grad_ld = dot2(upper, grad_c + dc_ref[...])
    decay_side = -grad_ld * rates * sigmoid(scal)
    gscal_ref[...] = jnp.where(
        cols < HEADS,
        grad_b * strength * (1.0 - strength),
        jnp.where(cols < 2 * HEADS, decay_side, 0.0),
    ).astype(bf16)
    grate_ref[0:1, :] += -jnp.sum(grad_ld * softplus(scal), axis=0, keepdims=True)
    store_rows(gpre_ref, gext_ref)


def row_grads(groups, lhs_count, rhs_count, *refs):
    out_ref = refs[-1]
    lhs = [refs[i][...] for i in range(lhs_count)]
    rhs = refs[lhs_count : lhs_count + rhs_count]
    lane = 0
    for group in groups:
        total = None
        for i, j in group:
            part = dot1(lhs[i][: rhs[j].shape[0]], rhs[j][...], TN)
            total = part if total is None else total + part
        out_ref[:, lane : lane + total.shape[1]] = total.astype(bf16)
        lane += total.shape[1]


def mixer_grads(
    offsets, place_ref, normed_ref, mixer_ref, og_ref, gq_ref, gkv_ref, gscal_ref, gated_ref, *outs
):
    width = normed_ref.shape[1]
    part = HEADS * DK // 2
    tokens = 2 * TOK

    def rows_x(ref, offset):
        place = lax.rem(place_ref[0] + offset, 4)
        return ref[:, pl.ds(pl.multiple_of(place * (width // 4), 128), width // 4)]

    def rows_z(ref, offset):
        place = lax.rem(place_ref[1] + offset, 4)
        cut = width // 16
        pieces = [
            ref[:, pl.ds(pl.multiple_of((j * 4 + place) * cut, 128), cut)] for j in range(4)
        ]
        return jnp.concatenate(pieces, axis=1)

    def store(outs, columns):
        lane = 0
        for column in columns:
            column = column.astype(bf16)
            lanes = slice(lane, lane + column.shape[1])
            rows = column.shape[0] // len(outs)
            for i, out in enumerate(outs):
                out[:, lanes] = column[i * rows : (i + 1) * rows]
            lane += column.shape[1]

    count = len(outs) // (2 * len(offsets))
    for i, offset in enumerate(offsets):
        normed = rows_x(normed_ref, offset)
        store(
            outs[i * count : (i + 1) * count],
            [
                dot1(normed[:tokens], og_ref[...], TN),
                dot1(normed, gq_ref[...], TN),
                dot1(normed[:tokens], gscal_ref[...], TN),
                dot1(normed, gkv_ref[:, :part], TN),
            ],
        )
        normed = rows_z(normed_ref, offset)
        i += len(offsets)
        store(
            outs[i * count : (i + 1) * count],
            [
                dot1(normed, gkv_ref[:, part:], TN),
                dot1(rows_z(mixer_ref, offset), gated_ref[...], TN),
            ],
        )


def input_grads(
    rim_ref, gq_ref, gkv_ref, gscal_ref, og_ref, left_ref, right_ref, out_ref, first_ref, second_ref
):
    inner = HEADS * DK
    part = inner // 2
    tokens = 2 * TOK

    @pl.when(pl.program_id(0) == 0)
    def _():
        first_ref[:, :inner] = gq_ref[:tokens, :]
        first_ref[:, inner : inner + 128] = gscal_ref[...]
        first_ref[:, inner + 128 : inner + 128 + part] = gkv_ref[:tokens, :part]
        first_ref[:, inner + 128 + part :] = og_ref[...]
        second_ref[...] = gkv_ref[:tokens, part:]
        for s in range(2):
            rows = slice((s + 1) * TOK - HALO, (s + 1) * TOK)
            rim = rim_ref[s * HALO : (s + 1) * HALO, :].astype(f32)

            def put(ref, lanes, came):
                ref[rows, lanes] = (ref[rows, lanes].astype(f32) + came).astype(bf16)

            put(first_ref, slice(0, inner), rim[:, :inner])
            put(
                first_ref,
                slice(inner + 128, inner + 128 + part),
                rim[:, inner : inner + part],
            )
            put(second_ref, slice(0, inner + part), rim[:, inner + part :])

    total = dot1(first_ref[...], left_ref[...], NT)
    total = total + dot1(second_ref[...], right_ref[:, : inner + part], NT)
    out_ref[...] = total.astype(bf16)


def ignoring(kernel, at, count):
    def inner_kernel(*refs):
        kernel(*refs[:at], *refs[at + count :])

    return inner_kernel


def dep_specs(deps):
    return [pl.BlockSpec(memory_space=pl.ANY) for _ in deps]


def cost(flops, moved):
    return pl.CostEstimate(flops=flops, bytes_accessed=moved, transcendentals=0)


def params():
    return pltpu.CompilerParams(vmem_limit_bytes=VMEM)


def whole(shape):
    return pl.BlockSpec(shape, lambda s: (0,) * len(shape))


def by_rows(rows, cols, base=0, lane=0):
    return pl.BlockSpec((rows, cols), lambda s: (base + s, lane))


def by_lead(*shape):
    return pl.BlockSpec(shape, lambda s: (s,) + (0,) * (len(shape) - 1))


def mixer_specs():
    wide = 3 * HEADS * DK
    return [
        by_rows(TOK, wide),
        by_rows(HALO, wide, 2 * TOK // HALO),
        by_rows(TOK, 128),
        whole((1, 128)),
        whole((TAPS, wide)),
        by_lead(1, TOK, 8),
        by_lead(1, 1, TOK),
    ]


def run_chunk_forward(pre, scal, rates, taps, marks, docs):
    quarter = DK // HEADS
    wide = 3 * HEADS * DK
    return pl.pallas_call(
        chunk_forward,
        grid=(2,),
        in_specs=mixer_specs(),
        out_specs=[
            by_lead(16, DK + quarter, DK),
            by_lead(HEADS, TOK, DK),
            by_lead(HEADS, TOK, DK),
            by_lead(HEADS, TOK, DK),
            by_lead(HEADS, TOK, 2 * DK),
        ],
        out_shape=[
            jax.ShapeDtypeStruct((SEQ, DK + quarter, DK), bf16),
            jax.ShapeDtypeStruct((8, TOK, DK), bf16),
            jax.ShapeDtypeStruct((8, TOK, DK), f32),
            jax.ShapeDtypeStruct((8, TOK, DK), bf16),
            jax.ShapeDtypeStruct((8, TOK, 2 * DK), f32),
        ],
        scratch_shapes=[pltpu.VMEM((HALO + TOK, wide), f32)],
        compiler_params=params(),
        cost_estimate=cost(10**10, 6 * 10**6),
    )(pre, pre, scal, rates, taps, marks, docs)


def run_scan_forward(got):
    return pl.pallas_call(
        scan_forward,
        out_shape=jax.ShapeDtypeStruct((SEQ, DK // HEADS, DK), bf16),
        compiler_params=params(),
        cost_estimate=cost(10**9, 3 * 10**6),
    )(got)


def run_scan_backward(got, local, deps):
    vmem = pl.BlockSpec(memory_space=pltpu.VMEM)
    return pl.pallas_call(
        ignoring(scan_backward, 2, len(deps)),
        in_specs=[vmem, vmem] + dep_specs(deps),
        out_specs=vmem,
        out_shape=jax.ShapeDtypeStruct((SEQ, DK // HEADS, DK), bf16),
        compiler_params=params(),
        cost_estimate=cost(10**9, 3 * 10**6),
    )(got, local, *deps)


def run_gate_forward(p, z, state, og, gain, deps):
    inner = HEADS * DK
    return pl.pallas_call(
        ignoring(gate_forward, 5, len(deps)),
        grid=(2,),
        in_specs=[
            by_lead(HEADS, TOK, DK),
            by_lead(HEADS, TOK, DK),
            by_lead(HEADS, DK, DK),
            by_rows(TOK, inner),
            whole((1, DK)),
        ]
        + dep_specs(deps),
        out_specs=[by_rows(TOK, inner), by_rows(TOK, inner)],
        out_shape=[
            jax.ShapeDtypeStruct((2 * TOK, inner), f32),
            jax.ShapeDtypeStruct((2 * TOK, inner), bf16),
        ],
        compiler_params=params(),
        cost_estimate=cost(10**9, 3 * 10**6),
    )(p, z, state, og, gain, *deps)


def run_gate_backward(gg, heads_out, og, gain, p):
    inner = HEADS * DK
    return pl.pallas_call(
        gate_backward,
        grid=(2,),
        in_specs=[
            by_rows(TOK, inner),
            by_rows(TOK, inner),
            by_rows(TOK, inner),
            whole((1, DK)),
            by_lead(HEADS, TOK, DK),
        ],
        out_specs=[
            by_rows(TOK, inner),
            by_rows(TOK, inner),
            by_lead(16, DK // HEADS, DK),
            whole((8, DK)),
        ],
        out_shape=[
            jax.ShapeDtypeStruct((2 * TOK, inner), f32),
            jax.ShapeDtypeStruct((2 * TOK, inner), bf16),
            jax.ShapeDtypeStruct((SEQ, DK // HEADS, DK), bf16),
            jax.ShapeDtypeStruct((8, DK), f32),
        ],
        compiler_params=params(),
        cost_estimate=cost(10**9, 3 * 10**6),
    )(gg, heads_out, og, gain, p)


def run_chunk_backward_early(pre, scal, rates, taps, marks, docs, uw, state, do):
    inner = HEADS * DK
    wide = 3 * inner
    square = jax.ShapeDtypeStruct((8, TOK, DK), f32)
    return pl.pallas_call(
        chunk_backward_early,
        grid=(2,),
        in_specs=mixer_specs()
        + [
            by_lead(HEADS, TOK, 2 * DK),
            by_lead(HEADS, DK, DK),
            by_rows(TOK, inner),
        ],
        out_specs=[
            whole((2 * (TOK + HALO), inner)),
            whole((TAPS, inner)),
            by_lead(HEADS, TOK, DK),
            by_lead(HEADS, TOK, DK),
            by_lead(HEADS, TOK, DK),
            by_lead(HEADS, TOK, DK),
            by_rows(TOK, 128),
        ],
        out_shape=[
            jax.ShapeDtypeStruct((2 * (TOK + HALO), inner), bf16),
            jax.ShapeDtypeStruct((TAPS, inner), f32),
            jax.ShapeDtypeStruct((8, TOK, DK), bf16),
            square,
            square,
            square,
            jax.ShapeDtypeStruct((2 * TOK, 128), f32),
        ],
        scratch_shapes=[
            pltpu.VMEM((HALO + TOK, wide), f32),
            pltpu.VMEM((HALO + TOK, inner), f32),
        ],
        compiler_params=params(),
        cost_estimate=cost(5 * 10**9, 10**7),
    )(pre, pre, scal, rates, taps, marks, docs, uw, state, do)


def run_chunk_backward_late(
    pre, scal, rates, taps, marks, docs, x, state, adj, early, deps
):
    inner = HEADS * DK
    wide = 3 * inner
    return pl.pallas_call(
        ignoring(chunk_backward_late, 15, len(deps)),
        grid=(2,),
        in_specs=mixer_specs()
        + [
            by_lead(HEADS, TOK, DK),
            by_lead(HEADS, DK, DK),
            by_lead(HEADS, DK, DK),
            by_lead(HEADS, TOK, DK),
            by_lead(HEADS, TOK, DK),
            by_lead(HEADS, TOK, DK),
            by_lead(HEADS, TOK, DK),
            by_rows(TOK, 128),
        ]
        + dep_specs(deps),
        out_specs=[
            whole((2 * (TOK + HALO), 2 * inner)),
            by_rows(TOK, 128),
            whole((TAPS, 2 * inner)),
            whole((8, 128)),
        ],
        out_shape=[
            jax.ShapeDtypeStruct((2 * (TOK + HALO), 2 * inner), bf16),
            jax.ShapeDtypeStruct((2 * TOK, 128), bf16),
            jax.ShapeDtypeStruct((TAPS, 2 * inner), f32),
            jax.ShapeDtypeStruct((8, 128), f32),
        ],
        scratch_shapes=[
            pltpu.VMEM((HALO + TOK, 2 * inner), f32),
            pltpu.VMEM((HALO + TOK, 2 * inner), f32),
        ],
        compiler_params=params(),
        cost_estimate=cost(5 * 10**9, 10**7),
    )(pre, pre, scal, rates, taps, marks, docs, x, state, adj, *early, *deps)


def run_row_grads(lhs, rhs, groups, deps=()):
    width = lhs[0].shape[1]
    cols = sum(rhs[group[0][1]].shape[1] for group in groups)
    return pl.pallas_call(
        partial(row_grads, groups, len(lhs), len(rhs)),
        grid=(4,),
        in_specs=[pl.BlockSpec((m.shape[0], width // 4), lambda s: (0, s)) for m in lhs]
        + [whole(m.shape) for m in rhs]
        + dep_specs(deps),
        out_specs=pl.BlockSpec((width // 4, cols), lambda s: (s, 0)),
        out_shape=jax.ShapeDtypeStruct((width, cols), bf16),
        compiler_params=params(),
        cost_estimate=cost(2 * rhs[0].shape[0] * width * cols, 2 * width * cols),
    )(*lhs, *rhs, *deps)


def run_mixer_grads(offsets, halves, *arrays, deps=()):
    width = arrays[0].shape[1]
    inner = HEADS * DK
    vmem = pl.BlockSpec(memory_space=pltpu.VMEM)
    place = jnp.stack([place_of("x"), place_of("z")]).astype(jnp.int32)
    shapes = [
        (width // 4 // halves, cols)
        for cols in (2 * inner + inner // 2 + 128, 2 * inner + inner // 2)
        for _ in range(halves * len(offsets))
    ]
    return pl.pallas_call(
        ignoring(partial(mixer_grads, offsets), 8, len(deps)),
        in_specs=[pl.BlockSpec(memory_space=pltpu.SMEM)] + [vmem] * 7 + dep_specs(deps),
        out_specs=[vmem] * len(shapes),
        out_shape=[jax.ShapeDtypeStruct(shape, bf16) for shape in shapes],
        compiler_params=params(),
        cost_estimate=cost(2 * 256 * width * 5 * inner, 2 * width * 5 * inner),
    )(place, *arrays, *deps)


def run_input_grads(rim, gq, gkv, gscal, og, left, right):
    inner = HEADS * DK
    width = left.shape[0]
    tokens = 2 * TOK
    cut = width // 4
    return pl.pallas_call(
        input_grads,
        grid=(4,),
        in_specs=[whole(m.shape) for m in (rim, gq, gkv, gscal, og)]
        + [
            by_rows(cut, left.shape[1]),
            by_rows(cut, right.shape[1]),
        ],
        out_specs=pl.BlockSpec((tokens, cut), lambda s: (0, s)),
        out_shape=jax.ShapeDtypeStruct((tokens, width), bf16),
        scratch_shapes=[
            pltpu.VMEM((tokens, left.shape[1]), bf16),
            pltpu.VMEM((tokens, inner + inner // 2), bf16),
        ],
        compiler_params=params(),
        cost_estimate=cost(2 * tokens * width * 5 * inner, 2 * width * 5 * inner),
    )(rim, gq, gkv, gscal, og, left, right)


SEQ_AXES = ("x", "z", "y")
GROUP_AXES = ("y", "head")


def passed_along(array, by):
    pairs = [(i, i + by) for i in range(SEQ) if 0 <= i + by < SEQ]
    return lax.ppermute(array, SEQ_AXES, pairs)


def along(array, axis, by):
    count = lax.axis_size(axis)
    return lax.ppermute(array, axis, [(i, (i + by) % count) for i in range(count)])


def place_of(axis):
    return lax.axis_index(axis)


def flipped(array, axes, mask):
    count = lax.axis_size(axes)
    return lax.ppermute(array, axes, [(i, i ^ mask) for i in range(count)])


def pick(array, index, dim):
    return lax.dynamic_index_in_dim(array, index, dim, keepdims=False)


def ordered(mine, other, place, axis=0):
    first = place == 0
    return jnp.concatenate(
        [jnp.where(first, mine, other), jnp.where(first, other, mine)], axis=axis
    )


def later(array, *deps):
    for dep in deps:
        first = lax.slice(dep, (0,) * dep.ndim, (1,) * dep.ndim).reshape(())
        array = array + (first * 0).astype(array.dtype)
    return array


def gather_last(first, second):
    near, far, halfway = near_and_far(first, second, ("z", "x"))
    outs = []
    for i, (array, axis, dim) in enumerate(((first, "z", 1), (second, "x", 0))):
        place = place_of(axis)
        shape = list(array.shape)
        shape.insert(dim, 4)
        out = jnp.zeros(shape, array.dtype)
        block = jnp.concatenate(far[2 * i : 2 * i + 2], axis=0)
        for offset, block in ((0, array), (-1, near[2 * i]), (-2, block), (1, near[2 * i + 1])):
            out = lax.dynamic_update_index_in_dim(out, block, (place + offset) % 4, dim)
        outs.append(out.reshape(-1, array.shape[-1]))
    return outs[0], outs[1], halfway


def exchange(array, axis):
    return lax.all_to_all(array, axis, split_axis=0, concat_axis=0, tiled=True)


def head_place():
    index = lax.axis_index("head")
    return index // 2, index % 2


def core_scatter(partial_rows):
    core = head_place()[1]
    rows = partial_rows.shape[0] // HEADS
    blocks = partial_rows.astype(bf16).reshape(2, 2, rows, -1)
    got = flipped(pick(blocks, 1 - core, 1), "head", 1)
    return pick(blocks, core, 1).astype(f32) + got.astype(f32), got


def chip_scatter(both, *gates):
    chip = head_place()[0]
    got = flipped(later(pick(both, 1 - chip, 0), *gates).astype(bf16), "head", 2)
    return pick(both, chip, 0) + got.astype(f32)


def head_gather(rows):
    chip, core = head_place()
    got = flipped(rows, "head", 2)
    first = chip == 0
    chips = jnp.stack([jnp.where(first, rows, got), jnp.where(first, got, rows)])
    got = flipped(chips, "head", 1)
    first = core == 0
    cores = [jnp.where(first, chips, got), jnp.where(first, got, chips)]
    return jnp.stack(cores, axis=1).reshape(HEADS * rows.shape[0], -1)


def group_scatter(partial_rows):
    chip, core = head_place()
    place = place_of("y") * 2 + chip
    blocks = partial_rows.astype(bf16).reshape(4, 2, -1, partial_rows.shape[1])
    got = flipped(pick(blocks, 1 - core, 1), GROUP_AXES, 1)
    both = pick(blocks, core, 1).astype(f32) + got.astype(f32)
    total = pick(both, place, 0)
    for mask in (2, 1, 3):
        part = pick(both, jnp.bitwise_xor(place, mask), 0).astype(bf16)
        total = total + flipped(part, GROUP_AXES, 2 * mask).astype(f32)
    return total, got


def group_gather(rows):
    chip, core = head_place()
    place = place_of("y") * 2 + chip
    out = jnp.zeros((4,) + rows.shape, rows.dtype)
    for mask in (2, 1, 3, 0):
        got = flipped(rows, GROUP_AXES, 2 * mask) if mask else rows
        out = lax.dynamic_update_index_in_dim(out, got, jnp.bitwise_xor(place, mask), 0)
    got = flipped(out, GROUP_AXES, 1)
    first = core == 0
    cores = [jnp.where(first, out, got), jnp.where(first, got, out)]
    return jnp.stack(cores, axis=1).reshape(8 * rows.shape[0], -1)


def in_vmem(kernel, shapes, place, *arrays, deps=()):
    vmem = pl.BlockSpec(memory_space=pltpu.VMEM)
    moved = sum(2 * a.size for a in arrays)
    return pl.pallas_call(
        ignoring(kernel, 1 + len(arrays), len(deps)),
        in_specs=[pl.BlockSpec(memory_space=pltpu.SMEM)] + [vmem] * len(arrays) + dep_specs(deps),
        out_specs=[vmem] * len(shapes),
        out_shape=[jax.ShapeDtypeStruct(shape, kind) for shape, kind in shapes],
        compiler_params=params(),
        cost_estimate=cost(moved, moved),
    )(place, *arrays, *deps)


def add_far(place_ref, *refs):
    for i in range(2):
        right, left, ahead, behind = refs[4 * i : 4 * i + 4]
        right_out, left_out = refs[8 + 2 * i : 10 + 2 * i]
        half = ahead.shape[0]
        total = right[:half].astype(f32) + ahead[...].astype(f32)
        right_out[:half] = total.astype(bf16)
        right_out[half:] = right[half:]
        left_out[:half] = left[:half]
        total = left[half:].astype(f32) + behind[...].astype(f32)
        left_out[half:] = total.astype(bf16)


def add_and_cut(place_ref, *refs):
    for i in range(2):
        members = refs[3 * i : 3 * i + 3]
        outs = refs[6 + 4 * i : 10 + 4 * i]
        rows = members[0].shape[0] // 4
        for out, by in zip(outs, (0, 2, 1, 3)):
            start = pl.multiple_of(lax.rem(place_ref[1 - i] + by, 4) * rows, rows)
            total = members[0][pl.ds(start, rows), :].astype(f32)
            for member in members[1:]:
                total = total + member[pl.ds(start, rows), :].astype(f32)
            out[...] = total.astype(bf16)


def add_and_halve(place_ref, *refs):
    kept, sent = refs[8:]
    rows = kept.shape[0]
    lane = 0
    for i in range(2):
        parts = refs[4 * i : 4 * i + 4]
        lanes = slice(lane, lane + parts[0].shape[1])
        lane += parts[0].shape[1]
        for out, at in ((kept, place_ref[2]), (sent, 1 - place_ref[2])):
            start = pl.multiple_of(at * rows, rows)
            total = parts[0][pl.ds(start, rows), :].astype(f32)
            for part in parts[1:]:
                total = total + part[pl.ds(start, rows), :].astype(f32)
            out[:, lanes] = total.astype(out.dtype)


def places():
    return jnp.stack([place_of(axis) for axis in SEQ_AXES]).astype(jnp.int32)


def reduce_near(owns, arrays, deps):
    shapes = [(arrays[i].shape, bf16) for i in (0, 1, 4, 5)]
    sums = in_vmem(add_far, shapes, places(), *arrays, deps=deps)
    gate = sums[0]
    arrays = []
    for i, axis in enumerate(("x", "z")):
        arrays += [owns[i], along(sums[2 * i], axis, 1), along(sums[2 * i + 1], axis, -1)]
    return arrays, gate


def reduce_cross(arrays, deps):
    shapes = []
    for own in (arrays[0], arrays[3]):
        shapes += [((own.shape[0] // 4, own.shape[1]), bf16)] * 4
    cut = in_vmem(add_and_cut, shapes, places(), *arrays, deps=deps)
    arrays = []
    for i, axis in enumerate(("z", "x")):
        own, two, one, three = cut[4 * i : 4 * i + 4]
        arrays += [own, along(two, axis, 2), along(one, axis, 1), along(three, axis, -1)]
    return arrays, cut[0]


def reduce_end(arrays, deps):
    rows, cols = arrays[0].shape[0] // 2, arrays[0].shape[1] + arrays[4].shape[1]
    shapes = [((rows, cols), f32), ((rows, cols), bf16)]
    kept, sent = in_vmem(add_and_halve, shapes, places(), *arrays, deps=deps)
    return kept + along(sent, "y", 1).astype(f32)


def pair_up(place_ref, left, left_other, right, right_other, left_out, right_out):
    rows = left.shape[0]
    mine = pl.multiple_of(place_ref[2] * rows, rows)
    other = pl.multiple_of((1 - place_ref[2]) * rows, rows)
    left_out[pl.ds(mine, rows), :] = left[...]
    left_out[pl.ds(other, rows), :] = left_other[...]
    right_out[pl.ds(mine, rows), :] = right[...]
    right_out[pl.ds(other, rows), :] = right_other[...]


def pass_on(place_ref, *refs):
    for i in range(2):
        half = refs[4 + 2 * i].shape[0]
        refs[4 + 2 * i][...] = refs[2 * i][:half]
        refs[5 + 2 * i][...] = refs[2 * i + 1][half:]


def put_in_place(axes, place_ref, *refs):
    for i in range(2):
        out = refs[10 + i]
        own, left, right, far_a, far_b = refs[5 * i : 5 * i + 5]
        place = place_ref[axes[i]]
        half = far_a.shape[0]
        out[place] = own[...]
        out[lax.rem(place + 3, 4)] = left[...]
        out[lax.rem(place + 1, 4)] = right[...]
        out[lax.rem(place + 2, 4), :half] = far_a[...]
        out[lax.rem(place + 2, 4), half:] = far_b[...]


def near_and_far(first, second, axes):
    near = []
    for array, axis in ((first, axes[0]), (second, axes[1])):
        near += [along(array, axis, 1), along(array, axis, -1)]
    shapes = []
    for array in (first, second):
        shapes += [((array.shape[0] // 2,) + array.shape[1:], bf16)] * 2
    halves = in_vmem(pass_on, shapes, places(), *near)
    far = []
    for i in range(2):
        far += [along(halves[2 * i], axes[i], 1), along(halves[2 * i + 1], axes[i], -1)]
    return near, far, halves[0]


def sum_along(array, axis):
    total = array
    for by in range(1, lax.axis_size(axis)):
        total = total + along(array, axis, by)
    return total


def mm(a, b, dims="ij,jk->ik"):
    return jnp.einsum(dims, a, b, preferred_element_type=f32)


def row_scale(x):
    return lax.rsqrt(jnp.mean(x * x, axis=-1, keepdims=True) + norm_eps)


def norm_pull(x, scale, gain, grad):
    unit = x * scale
    scaled = grad * gain
    return scale * (scaled - unit * jnp.mean(scaled * unit, axis=-1, keepdims=True))


def doc_tables(doc_lengths):
    first = lax.axis_index(SEQ_AXES) * TOK - (TAPS - 1)
    ends = jnp.cumsum(doc_lengths, axis=1)
    places = first + jnp.arange(TOK + TAPS - 1, dtype=jnp.int32)
    counted = jnp.sum((places[None, :, None] >= ends[:, None, :]).astype(jnp.int32), axis=2)
    ext = jnp.where(places[None, :] >= 0, counted, -1)
    local = ext[:, TAPS - 1 :]
    columns = [(ext[:, o : o + TOK] == local) for o in range(TAPS - 1)]
    columns.append(local == ext[:, TAPS - 2 : TAPS - 1])
    columns.append(local == local[:, -1:])
    columns.append(local)
    columns += [jnp.zeros_like(local)] * 2
    marks = jnp.stack([c.astype(f32) for c in columns], axis=-1)
    return marks, local.astype(f32)[:, None, :]


def body(
    inputs, doc_lengths, norm_in, query_weight, key_weight, value_weight, outgate_weight,
    scalar_weight, conv_kernel, decay_rate, head_norm, output_weight, norm_ffn, gate_weight,
    up_weight, down_weight, grad_out,
):
    width = inputs.shape[2]
    inner = HEADS * DK
    hidden = gate_weight.shape[1]
    head_index = lax.axis_index("head")
    quarter = 2 * TOK // HEADS

    gains = jnp.stack([norm_in, norm_ffn], axis=1)
    misc = jnp.concatenate([scalar_weight.reshape(-1, 2 * HEADS), gains], axis=1)
    misc = jnp.pad(misc, ((0, 0), (0, 128 - misc.shape[1])))
    part = inner // 2
    left = jnp.concatenate([query_weight, misc, key_weight[:, :part], outgate_weight], axis=1)
    right = jnp.concatenate([key_weight[:, part:], value_weight, output_weight.T], axis=1)
    y_place = place_of("y")
    rows = left.shape[0]
    left, right = in_vmem(
        pair_up,
        [((2 * rows, left.shape[1]), bf16), ((2 * rows, right.shape[1]), bf16)],
        places(),
        left, along(left, "y", 1), right, along(right, "y", 1),
    )
    near, far, _ = near_and_far(left, right, ("x", "z"))
    left, right = in_vmem(
        partial(put_in_place, (0, 1)),
        [((4, 2 * rows, part.shape[1]), bf16) for part in (left, right)],
        places(),
        left, *near[:2], *far[:2], right, *near[2:], *far[2:],
    )
    all_left, all_right, halfway = gather_last(left, right)
    w_gate, w_out_t = all_left[:, -inner:], all_right[:, -inner:]
    w_left, w_right = all_left[:, :-inner], all_right[:, :-inner]
    gains = w_left[:, inner : inner + 128].T[2 * HEADS : 2 * HEADS + 2].astype(f32)
    gain_in, gain_ffn = gains[0:1], gains[1:2]

    units = hidden // 2
    span = -(-units // 128) * 128

    def in_halves(weight):
        halves = weight.reshape(weight.shape[0], 2, units)
        return jnp.pad(halves, ((0, 0), (0, 0), (0, span - units)))

    packed = jnp.concatenate(
        [in_halves(gate_weight), in_halves(up_weight), in_halves(down_weight.T)], axis=2
    )
    other = along(later(pick(packed, 1 - y_place, 1), left), "y", 1)
    packed = later(ordered(pick(packed, y_place, 1), other, y_place), halfway)
    w_ffn = lax.all_gather(packed, ("x", "z"), axis=0, tiled=True)
    w_gateup = w_ffn[:, : 2 * span]
    w_down_t = w_ffn[:, 2 * span :]

    marks, docs_row = doc_tables(doc_lengths)
    taps = jnp.transpose(conv_kernel.astype(f32), (1, 0, 2)).reshape(TAPS, 3 * inner)
    rates = jnp.zeros((1, 128), f32)
    rates = rates.at[0, HEADS : 2 * HEADS].set(decay_rate.astype(f32))
    gain_head = head_norm.astype(f32).reshape(1, DK)

    halo = passed_along(inputs[:, TOK - HALO :], 1)
    tokens = inputs.reshape(2 * TOK, width)
    all_rows = jnp.concatenate([tokens, halo.reshape(2 * HALO, width)], axis=0).astype(f32)
    scale_in = row_scale(all_rows)
    normed_all = (all_rows * scale_in * gain_in).astype(bf16)
    normed_in = normed_all[: 2 * TOK]

    left = mm(normed_all, w_left)
    right = mm(normed_all, w_right)
    pre = jnp.concatenate(
        [left[:, :inner].astype(bf16), left[:, inner + 128 :].astype(bf16), right.astype(bf16)],
        axis=1,
    )
    scal = left[: 2 * TOK, inner : inner + 128]

    grad_rows = grad_out.reshape(2 * TOK, width)
    grad_other = along(grad_rows, "y", 1)
    send, p, z, x, uw = run_chunk_forward(pre, scal, rates, taps, marks, docs_row)
    out_gate = mm(normed_in, w_gate)
    got = exchange(send, SEQ_AXES)
    state = exchange(run_scan_forward(got), SEQ_AXES).reshape(8, DK, DK)
    heads_out, gated_rows = run_gate_forward(
        p, z, state, out_gate, gain_head, (grad_other,)
    )

    mine = partial(lax.dynamic_slice_in_dim, start_index=head_index * quarter, slice_size=quarter)
    residual = mine(tokens).astype(f32) + chip_scatter(
        core_scatter(mm(gated_rows, w_out_t, "ij,kj->ik"))[0]
    )
    scale_ffn = row_scale(residual)
    normed_ffn = group_gather((residual * scale_ffn * gain_ffn).astype(bf16))

    group_grads = ordered(grad_rows, grad_other, y_place)
    grad_act = mm(group_grads, w_down_t)
    gate_up = mm(normed_ffn, w_gateup)
    gate, up = gate_up[:, :span], gate_up[:, span:]
    sig = sigmoid(gate)
    silu = gate * sig
    product = (silu * up).astype(bf16)
    gu_grad = jnp.concatenate(
        [
            (grad_act * up * sig * (1.0 + gate * (1.0 - sig))).astype(bf16),
            (grad_act * silu).astype(bf16),
        ],
        axis=1,
    )
    ffn_part = mm(gu_grad, w_gateup, "ij,kj->ik").astype(bf16)
    grad_normed = group_scatter(ffn_part)[0]
    back = norm_pull(residual, scale_ffn, gain_ffn, grad_normed)
    grad_residual = mine(grad_rows).astype(f32) + back
    grad_mixer = head_gather(grad_residual.astype(bf16))

    grad_gated = mm(grad_mixer, w_out_t)
    do, gate_grad_mix, local, part_gain_head = run_gate_backward(
        grad_gated, heads_out, out_gate, gain_head, p
    )
    local_got = exchange(local, SEQ_AXES)
    early = run_chunk_backward_early(pre, scal, rates, taps, marks, docs_row, uw, state, do)
    gq, gtaps_q = early[:2]
    ffn_all = run_row_grads(
        [normed_ffn, group_grads], [gu_grad, product], (((0, 0),), ((1, 1),)), (gq,)
    )
    ffn = lax.psum_scatter(ffn_all, ("x", "z"), scatter_dimension=0, tiled=True)
    adj_out = run_scan_backward(got, local_got, (ffn_all,))
    ffn_out, ffn_got = group_scatter(mm(later(product, local), w_down_t, "ij,kj->ik"))
    adj = exchange(adj_out, SEQ_AXES).reshape(8, DK, DK)
    gkv, gscal, gtaps_kv, grate = run_chunk_backward_late(
        pre, scal, rates, taps, marks, docs_row, x, state, adj, early[2:], (ffn_got,)
    )

    arrays = (normed_all, grad_mixer, gate_grad_mix, gq, gkv, gscal, gated_rows)
    far = run_mixer_grads((2,), 2, *arrays, deps=(ffn_out,))
    blocks = run_mixer_grads((1, 3, 0), 1, *arrays, deps=(far[0],))
    owns, partials = (blocks[2], blocks[5]), []
    for i, axis in enumerate(("x", "z")):
        partials += blocks[3 * i : 3 * i + 2]
        partials += [along(far[2 * i], axis, 1), along(far[2 * i + 1], axis, -1)]

    gtaps = jnp.concatenate([gtaps_q, gtaps_kv], axis=1).reshape(12, inner)
    tail = jnp.concatenate([part_gain_head[:1], grate[:1]], axis=1)
    tail = jnp.pad(tail, ((0, 3), (0, inner - tail.shape[1])))
    small = sum_along(jnp.concatenate([gtaps, tail], axis=0), "x")
    rim = jnp.concatenate([gq[2 * TOK :], gkv[2 * TOK :]], axis=1)
    rim = passed_along(later(rim, blocks[0]), -1)
    input_sent = run_input_grads(
        rim, gq, gkv, gscal, gate_grad_mix, all_left, all_right
    )
    partials, near_gate = reduce_near(owns, partials, (small, input_sent))
    small = sum_along(later(small, near_gate), "z")
    by_core = core_scatter(later(input_sent, near_gate))[0]
    grad_normed_in = chip_scatter(by_core)
    own = mine(tokens).astype(f32)
    back_in = norm_pull(own, row_scale(own), gain_in, grad_normed_in)
    both = jnp.concatenate([residual + ffn_out, grad_residual + back_in], axis=1)
    both = both.astype(bf16)
    partials, cross_gate = reduce_cross(partials, (both, small, ffn))
    small = sum_along(later(small, cross_gate), "y")
    mixer_w = reduce_end(partials, ())
    both = head_gather(later(both, cross_gate))
    outputs, grad_in = both[:, :width], both[:, width:].astype(f32)

    ffn = ffn.reshape(2, -1, 3, span)[..., :units]
    ffn_other = along(pick(ffn, 1 - y_place, 0), "y", 1)
    ffn = ordered(pick(ffn, y_place, 0), ffn_other, y_place, 2).astype(f32)

    rows = width // SEQ
    key_at = 2 * inner + 128
    grad_conv = jnp.transpose(small[:12].reshape(TAPS, 3, inner), (1, 0, 2))

    def gain_grad(gain, weights, grads):
        total = 0.0
        for weight, grad in zip(weights, grads):
            total = total + jnp.sum(weight.astype(f32) * grad, axis=1)
        return total / gain.astype(f32)

    grad_scalar = mixer_w[:, 2 * inner : 2 * inner + 2 * HEADS]
    gain_parts = jnp.concatenate(
        [
            gain_grad(
                norm_in,
                (outgate_weight, query_weight, scalar_weight.reshape(rows, -1), key_weight, value_weight),
                (
                    mixer_w[:, :inner],
                    mixer_w[:, inner : 2 * inner],
                    grad_scalar,
                    mixer_w[:, key_at : key_at + inner],
                    mixer_w[:, key_at + inner : key_at + 2 * inner],
                ),
            ),
            gain_grad(norm_ffn, (gate_weight, up_weight), (ffn[:, 0], ffn[:, 1])),
            small[12, :DK],
        ]
    )
    shared = sum_along(gain_parts[None], "head")[0]
    return (
        outputs.reshape(inputs.shape),
        grad_in.reshape(inputs.shape),
        shared[:rows],
        mixer_w[:, inner : 2 * inner],
        mixer_w[:, key_at : key_at + inner],
        mixer_w[:, key_at + inner : key_at + 2 * inner],
        mixer_w[:, :inner],
        grad_scalar.reshape(rows, 2, HEADS),
        grad_conv,
        small[12, DK + HEADS : DK + 2 * HEADS],
        shared[2 * rows :],
        mixer_w[:, key_at + 2 * inner :].T,
        shared[rows : 2 * rows],
        ffn[:, 0],
        ffn[:, 1],
        ffn[:, 2].T,
    )


def solution(mesh):
    mesh = Mesh(mesh.devices.reshape(4, 4, 2, HEADS), ("x", "z", "y", "head"))
    seq = SEQ_AXES
    weight = P(seq, "head")
    weight_t = P("head", seq)
    tokens = P(None, seq, None)
    scalars = P(seq, None, "head")
    taps = P(None, None, "head")
    return jax.shard_map(
        body,
        mesh=mesh,
        in_specs=(
            tokens, P(), P(seq), weight, weight, weight, weight, scalars, taps, P("head"), P(),
            weight_t, P(seq), weight, weight, weight_t, tokens,
        ),
        out_specs=(
            tokens, tokens, P(seq), weight, weight, weight, weight, scalars, taps, P("head"),
            P(), weight_t, P(seq), weight, weight, weight_t,
        ),
        check_vma=False,
    )
```

```python
from functools import partial

import jax
import jax.numpy as jnp
from jax import lax
from jax.experimental import pallas as pl
from jax.experimental.pallas import tpu as pltpu
from jax.sharding import Mesh
from jax.sharding import PartitionSpec as P

f32 = jnp.float32
bf16 = jnp.bfloat16
norm_eps = 1e-06
head_eps = 1e-05
SEQ = 32
HEADS = 4
DK = 128
TOK = 128
TAPS = 4
HALO = 16
VMEM = 56 * 1024 * 1024

NN = (((1,), (0,)), ((), ()))
NT = (((1,), (1,)), ((), ()))
TN = (((0,), (0,)), ((), ()))


def dot1(a, b, dims=NN):
    return lax.dot_general(a.astype(bf16), b.astype(bf16), dims, preferred_element_type=f32)


def split(a):
    high = a.astype(bf16)
    return high, (a - high.astype(f32)).astype(bf16)


def dot3(a, b, dims=NN):
    ah, al = split(a)
    bh, bl = split(b)
    return dot1(ah, bh, dims) + (dot1(ah, bl, dims) + dot1(al, bh, dims))


def dot2(exact, b, dims=NN):
    high = b.astype(bf16)
    rest = b - high.astype(f32)
    mid = rest.astype(bf16)
    low = (rest - mid.astype(f32)).astype(bf16)
    return dot1(exact, high, dims) + (dot1(exact, mid, dims) + dot1(exact, low, dims))


def sigmoid(x):
    return 1.0 / (1.0 + jnp.exp(-x))


def softplus(x):
    return jnp.maximum(x, 0.0) + jnp.log1p(jnp.exp(-jnp.abs(x)))


def iotas():
    rows = lax.broadcasted_iota(jnp.int32, (TOK, TOK), 0)
    cols = lax.broadcasted_iota(jnp.int32, (TOK, TOK), 1)
    return rows, cols


def unit_inverses(stricts):
    rows, cols = iotas()
    eye = (rows == cols).astype(f32)
    apart = jnp.bitwise_xor(rows, cols)
    results = []
    first = (apart == 1) & (rows > cols)
    results = [eye - jnp.where(first, a, 0.0) for a in stricts]
    size = 2
    while size < TOK:
        corner = (apart >= size) & (apart < 2 * size) & (rows > cols)
        parts = [dot3(jnp.where(corner, a, 0.0), x) for a, x in zip(stricts, results)]
        results = [x - dot3(x, c) for x, c in zip(results, parts)]
        size *= 2
    return results


def decays(scal, rates, marks, docs_row):
    rows, cols = iotas()
    strength = sigmoid(scal)
    log_decay = -rates * softplus(scal)
    lower = (rows >= cols).astype(bf16)
    total = dot2(lower, log_decay)
    total_t = jnp.transpose(total)
    same = marks[:, 5:6] == docs_row
    causal = same & (rows >= cols)
    return strength, total, total_t, causal, rows > cols


def conv_parts(ext_ref, weights, marks, lane):
    out = None
    for tap in range(TAPS):
        piece = ext_ref[pl.ds(HALO - TAPS + 1 + tap, TOK), pl.ds(lane, DK)]
        if tap < TAPS - 1:
            piece = piece * marks[:, tap : tap + 1]
        piece = piece * weights[tap : tap + 1, lane : lane + DK]
        out = piece if out is None else out + piece
    return out


def unit_scale(x):
    return lax.rsqrt(jnp.sum(x * x, axis=-1, keepdims=True) + norm_eps)


def chunk_forward(
    pre_ref, rim_ref, scal_ref, rate_ref, taps_ref, marks_ref, docs_ref,
    send_ref, p_ref, z_ref, x_ref, uw_ref, ext_ref,
):
    inner = HEADS * DK
    ext_ref[0:HALO, :] = rim_ref[...].astype(f32)
    ext_ref[HALO:, :] = pre_ref[...].astype(f32)
    marks = marks_ref[0]
    weights = taps_ref[...]
    strength, total, total_t, causal, below = decays(
        scal_ref[...], rate_ref[...], marks, docs_ref[0]
    )
    rows, cols = iotas()
    reached, tail = marks[:, 3:4], marks[:, 4:5]
    heads = []
    for h in range(HEADS):
        acts = []
        for c in range(3):
            conv = conv_parts(ext_ref, weights, marks, c * inner + h * DK)
            acts.append(conv * sigmoid(conv))
        q = (acts[0] * unit_scale(acts[0])).astype(bf16)
        k = (acts[1] * unit_scale(acts[1])).astype(bf16)
        v = acts[2].astype(bf16)
        c_col = total[:, HEADS + h : HEADS + h + 1]
        c_row = total_t[HEADS + h : HEADS + h + 1, :]
        decay = jnp.where(causal, jnp.exp(jnp.where(causal, c_col - c_row, 0.0)), 0.0)
        b = strength[:, h : h + 1]
        gram = dot1(k, k, NT)
        strict = jnp.where(below, b * gram * decay, 0.0)
        heads.append((q, k, v, c_col, decay, b, strict))
    inverses = unit_inverses([head[6] for head in heads])
    for h in range(HEADS):
        q, k, v, c_col, decay, b, strict = heads[h]
        x = inverses[h]
        start = jnp.exp(c_col) * reached
        kf = k.astype(f32)
        uw = dot3(x, jnp.concatenate([b * v.astype(f32), (b * start) * kf], axis=1))
        scores = dot1(q, k, NT) * decay
        suw = dot3(scores, uw)
        last = c_col[TOK - 1 : TOK, :]
        tail_k = kf * (jnp.exp(last - c_col) * tail)
        carry = jnp.exp(last) * reached[TOK - 1 : TOK, :]
        u, w = uw[:, :DK], uw[:, DK:]
        move = jnp.where(rows == cols, carry, 0.0) - dot3(tail_k, w, TN)
        offset_t = dot3(u, tail_k, TN)
        p_ref[h] = (q.astype(f32) * start - suw[:, DK:]).astype(bf16)
        z_ref[h] = suw[:, :DK]
        x_ref[h] = x.astype(bf16)
        uw_ref[h] = uw
        quarter = DK // HEADS
        for j in range(HEADS):
            send_ref[HEADS * h + j, 0:DK, :] = move.astype(bf16)
            send_ref[HEADS * h + j, DK : DK + quarter, :] = offset_t[
                j * quarter : (j + 1) * quarter
            ].astype(bf16)


def scan_forward(got_ref, out_ref):
    state = jnp.zeros((DK // HEADS, DK), f32)
    for i in range(SEQ):
        out_ref[i] = state.astype(bf16)
        if i + 1 < SEQ:
            high, low = split(state)
            both = dot1(jnp.concatenate([high, low], axis=0), got_ref[i, 0:DK, :], NT)
            half = DK // HEADS
            state = both[:half] + both[half:] + got_ref[i, DK : DK + half, :].astype(f32)


def scan_backward(got_ref, local_ref, out_ref):
    state = jnp.zeros((DK // HEADS, DK), f32)
    for i in range(SEQ - 1, -1, -1):
        out_ref[i] = state.astype(bf16)
        if i > 0:
            high, low = split(state)
            both = dot1(jnp.concatenate([high, low], axis=0), got_ref[i, 0:DK, :])
            half = DK // HEADS
            state = both[:half] + both[half:] + local_ref[i].astype(f32)


def gate_forward(p_ref, z_ref, s_ref, og_ref, gain_ref, heads_ref, gated_ref):
    gain = gain_ref[...]
    for h in range(HEADS):
        lanes = slice(h * DK, (h + 1) * DK)
        out = dot1(p_ref[h], s_ref[h], NT) + z_ref[h]
        heads_ref[:, lanes] = out
        r = lax.rsqrt(jnp.mean(out * out, axis=-1, keepdims=True) + head_eps)
        og = og_ref[:, lanes]
        gated_ref[:, lanes] = (out * r * gain * (og * sigmoid(og))).astype(bf16)


def gate_backward(
    gg_ref, heads_ref, og_ref, gain_ref, p_ref, do_ref, mix_ref, local_ref, gain_out_ref
):
    gain = gain_ref[...]
    total = jnp.zeros((1, DK), f32)
    quarter = DK // HEADS
    for h in range(HEADS):
        lanes = slice(h * DK, (h + 1) * DK)
        out = heads_ref[:, lanes]
        og = og_ref[:, lanes]
        gg = gg_ref[:, lanes]
        r = lax.rsqrt(jnp.mean(out * out, axis=-1, keepdims=True) + head_eps)
        u = out * r
        sig = sigmoid(og)
        w = og * sig
        ggw = gg * w
        g = ggw * gain
        total = total + jnp.sum(ggw * u, axis=0, keepdims=True)
        grad = r * (g - u * jnp.mean(g * u, axis=-1, keepdims=True))
        do_ref[:, lanes] = grad
        mix_ref[:, lanes] = (gg * gain * u * sig * (1.0 + og * (1.0 - sig))).astype(bf16)
        local = dot1(grad, p_ref[h], TN).astype(bf16)
        for j in range(HEADS):
            local_ref[HEADS * h + j] = local[j * quarter : (j + 1) * quarter]

    @pl.when(pl.program_id(0) == 0)
    def _():
        gain_out_ref[...] = jnp.zeros_like(gain_out_ref)

    gain_out_ref[0:1, :] += total


def conv_acts(ext_ref, weights, marks, lane):
    conv = conv_parts(ext_ref, weights, marks, lane)
    sig = sigmoid(conv)
    return conv, sig, conv * sig


def conv_pull(d_act, conv, sig, ext_ref, gext_ref, gtaps_ref, weights, marks, lane):
    d_conv = d_act * sig * (1.0 + conv * (1.0 - sig))
    for tap in range(TAPS):
        kept = d_conv * marks[:, tap : tap + 1] if tap < TAPS - 1 else d_conv
        place = (pl.ds(HALO - TAPS + 1 + tap, TOK), pl.ds(lane, DK))
        gtaps_ref[tap : tap + 1, lane : lane + DK] += jnp.sum(
            kept * ext_ref[place], axis=0, keepdims=True
        )
        gext_ref[place] += kept * weights[tap : tap + 1, lane : lane + DK]


def store_rows(gpre_ref, gext_ref):
    s = pl.program_id(0)
    gpre_ref[pl.ds(pl.multiple_of(s * TOK, TOK), TOK), :] = gext_ref[HALO:, :].astype(bf16)
    halo = pl.multiple_of(2 * TOK + s * HALO, HALO)
    gpre_ref[pl.ds(halo, HALO), :] = gext_ref[0:HALO, :].astype(bf16)


def unit_pull(d, hat, scale):
    return scale * (d - hat * jnp.sum(d * hat, axis=-1, keepdims=True))


def chunk_backward_early(
    pre_ref, rim_ref, scal_ref, rate_ref, taps_ref, marks_ref, docs_ref,
    uw_ref, s_ref, do_ref,
    gpre_ref, gtaps_ref, fresh_ref, recalled_ref, df_ref, dk_ref, dc_ref, ext_ref, gext_ref,
):
    inner = HEADS * DK
    ext_ref[0:HALO, :] = rim_ref[...].astype(f32)
    ext_ref[HALO:, :] = pre_ref[...].astype(f32)
    gext_ref[...] = jnp.zeros_like(gext_ref)

    @pl.when(pl.program_id(0) == 0)
    def _():
        gtaps_ref[...] = jnp.zeros_like(gtaps_ref)

    marks = marks_ref[0]
    weights = taps_ref[...]
    strength, total, total_t, causal, below = decays(
        scal_ref[...], rate_ref[...], marks, docs_ref[0]
    )
    rows, cols = iotas()
    reached = marks[:, 3:4]
    grad_c = jnp.zeros((TOK, TOK), f32)
    for h in range(HEADS):
        conv, sig, act = conv_acts(ext_ref, weights, marks, h * DK)
        act_k = conv_acts(ext_ref, weights, marks, inner + h * DK)[2]
        nq = unit_scale(act)
        q_hat = act * nq
        q, k = q_hat.astype(bf16), (act_k * unit_scale(act_k)).astype(bf16)
        c_col = total[:, HEADS + h : HEADS + h + 1]
        c_row = total_t[HEADS + h : HEADS + h + 1, :]
        decay = jnp.where(causal, jnp.exp(jnp.where(causal, c_col - c_row, 0.0)), 0.0)
        scores = dot1(q, k, NT) * decay
        start = jnp.exp(c_col) * reached
        state = s_ref[h]
        do = do_ref[:, h * DK : (h + 1) * DK].astype(bf16)
        fresh = uw_ref[h, :, :DK] - dot1(uw_ref[h, :, DK:], state, NT)
        fresh = fresh.astype(bf16)
        fresh_ref[h] = fresh
        recalled_ref[h] = dot1(k, state, NT)
        df_ref[h] = dot1(scores, do, TN)
        d_scores = dot1(do, fresh, NT)
        pull = d_scores * scores
        d_qk = (d_scores * decay).astype(bf16)
        dk_ref[h] = dot1(d_qk, q, TN)
        do_state = dot1(do, state)
        d_q = dot1(d_qk, k) + start * do_state
        d_start = jnp.sum(q.astype(f32) * do_state, axis=-1, keepdims=True)
        d_c = jnp.sum(pull - jnp.transpose(pull), axis=-1, keepdims=True) + d_start * start
        grad_c = jnp.where(cols == HEADS + h, d_c, grad_c)
        conv_pull(
            unit_pull(d_q, q_hat, nq), conv, sig, ext_ref, gext_ref, gtaps_ref, weights, marks,
            h * DK,
        )
    dc_ref[...] = grad_c
    store_rows(gpre_ref, gext_ref)


def chunk_backward_late(
    pre_ref, rim_ref, scal_ref, rate_ref, taps_ref, marks_ref, docs_ref,
    x_ref, s_ref, d_ref, fresh_ref, recalled_ref, df_ref, dk_ref, dc_ref,
    gpre_ref, gscal_ref, gtaps_ref, grate_ref, ext_ref, gext_ref,
):
    inner = HEADS * DK
    ext_ref[0:HALO, :] = rim_ref[:, inner:].astype(f32)
    ext_ref[HALO:, :] = pre_ref[:, inner:].astype(f32)
    gext_ref[...] = jnp.zeros_like(gext_ref)

    @pl.when(pl.program_id(0) == 0)
    def _():
        gtaps_ref[...] = jnp.zeros_like(gtaps_ref)
        grate_ref[...] = jnp.zeros_like(grate_ref)

    marks = marks_ref[0]
    weights = taps_ref[:, inner:]
    scal = scal_ref[...]
    rates = rate_ref[...]
    strength, total, total_t, causal, below = decays(scal, rates, marks, docs_ref[0])
    rows, cols = iotas()
    reached, tail = marks[:, 3:4], marks[:, 4:5]
    grad_b = jnp.zeros((TOK, TOK), f32)
    grad_c = jnp.zeros((TOK, TOK), f32)
    for h in range(HEADS):
        conv_k, sig_k, act_k = conv_acts(ext_ref, weights, marks, h * DK)
        conv_v, sig_v, act_v = conv_acts(ext_ref, weights, marks, inner + h * DK)
        nk = unit_scale(act_k)
        k_hat = act_k * nk
        k, v = k_hat.astype(bf16), act_v.astype(bf16)
        kf, vf = k.astype(f32), v.astype(f32)
        c_col = total[:, HEADS + h : HEADS + h + 1]
        c_row = total_t[HEADS + h : HEADS + h + 1, :]
        strict = causal & below
        strict_decay = jnp.where(strict, jnp.exp(jnp.where(strict, c_col - c_row, 0.0)), 0.0)
        b = strength[:, h : h + 1]
        gram_decay = dot1(k, k, NT) * strict_decay
        start = jnp.exp(c_col) * reached
        last = c_col[TOK - 1 : TOK, :]
        tail_decay = jnp.exp(last - c_col) * tail
        carry = jnp.exp(last) * reached[TOK - 1 : TOK, :]
        state, adj = s_ref[h], d_ref[h]
        fresh, recalled = fresh_ref[h], recalled_ref[h]
        d_fresh = df_ref[h] + dot1(kf * tail_decay, adj, NT)
        d_r = dot1(x_ref[h], d_fresh, TN)
        d_v = b * d_r
        d_b = jnp.sum(d_r * (vf - start * recalled), axis=-1, keepdims=True)
        d_start = -jnp.sum(d_v * recalled, axis=-1, keepdims=True)
        d_strict = -dot1(d_r, fresh, NT)
        strict_pull = d_strict * gram_decay
        d_b = d_b + jnp.sum(strict_pull, axis=-1, keepdims=True)
        d_gram = (d_strict * (b * strict_decay)).astype(bf16)
        d_k = dk_ref[h] - start * dot1(d_v, state) + dot1(d_gram, k) + dot1(d_gram, k, TN)
        fresh_adj = dot1(fresh, adj)
        d_k = d_k + tail_decay * fresh_adj
        d_tail = jnp.sum(kf * fresh_adj, axis=-1, keepdims=True) * tail_decay
        d_carry = jnp.sum(
            jnp.sum(adj.astype(f32) * state.astype(f32), axis=-1, keepdims=True),
            axis=0, keepdims=True,
        )
        pull = b * strict_pull
        d_c = jnp.sum(pull - jnp.transpose(pull), axis=-1, keepdims=True)
        d_c = d_c + d_start * start - d_tail
        d_last = d_carry * carry + jnp.sum(d_tail, axis=0, keepdims=True)
        d_c = d_c + jnp.where(rows[:, 0:1] == TOK - 1, d_last, 0.0)
        grad_b = jnp.where(cols == h, d_b, grad_b)
        grad_c = jnp.where(cols == HEADS + h, d_c, grad_c)
        conv_pull(
            unit_pull(d_k, k_hat, nk), conv_k, sig_k, ext_ref, gext_ref, gtaps_ref, weights,
            marks, h * DK,
        )
        conv_pull(
            d_v, conv_v, sig_v, ext_ref, gext_ref, gtaps_ref, weights, marks, inner + h * DK
        )
    upper = (cols >= rows).astype(bf16)
    grad_ld = dot2(upper, grad_c + dc_ref[...])
    decay_side = -grad_ld * rates * sigmoid(scal)
    gscal_ref[...] = jnp.where(
        cols < HEADS,
        grad_b * strength * (1.0 - strength),
        jnp.where(cols < 2 * HEADS, decay_side, 0.0),
    ).astype(bf16)
    grate_ref[0:1, :] += -jnp.sum(grad_ld * softplus(scal), axis=0, keepdims=True)
    store_rows(gpre_ref, gext_ref)


def row_grads(groups, lhs_count, rhs_count, *refs):
    out_ref = refs[-1]
    lhs = [refs[i][...] for i in range(lhs_count)]
    rhs = refs[lhs_count : lhs_count + rhs_count]
    lane = 0
    for group in groups:
        total = None
        for i, j in group:
            part = dot1(lhs[i][: rhs[j].shape[0]], rhs[j][...], TN)
            total = part if total is None else total + part
        out_ref[:, lane : lane + total.shape[1]] = total.astype(bf16)
        lane += total.shape[1]


def mixer_grads(
    offsets, place_ref, normed_ref, mixer_ref, og_ref, gq_ref, gkv_ref, gscal_ref, gated_ref, *outs
):
    width = normed_ref.shape[1]
    part = HEADS * DK // 2
    tokens = 2 * TOK

    def rows_x(ref, offset):
        place = lax.rem(place_ref[0] + offset, 4)
        return ref[:, pl.ds(pl.multiple_of(place * (width // 4), 128), width // 4)]

    def rows_z(ref, offset):
        place = lax.rem(place_ref[1] + offset, 4)
        cut = width // 16
        pieces = [
            ref[:, pl.ds(pl.multiple_of((j * 4 + place) * cut, 128), cut)] for j in range(4)
        ]
        return jnp.concatenate(pieces, axis=1)

    def store(outs, columns):
        lane = 0
        for column in columns:
            column = column.astype(bf16)
            lanes = slice(lane, lane + column.shape[1])
            rows = column.shape[0] // len(outs)
            for i, out in enumerate(outs):
                out[:, lanes] = column[i * rows : (i + 1) * rows]
            lane += column.shape[1]

    count = len(outs) // (2 * len(offsets))
    for i, offset in enumerate(offsets):
        normed = rows_x(normed_ref, offset)
        store(
            outs[i * count : (i + 1) * count],
            [
                dot1(normed[:tokens], og_ref[...], TN),
                dot1(normed, gq_ref[...], TN),
                dot1(normed[:tokens], gscal_ref[...], TN),
                dot1(normed, gkv_ref[:, :part], TN),
            ],
        )
        normed = rows_z(normed_ref, offset)
        i += len(offsets)
        store(
            outs[i * count : (i + 1) * count],
            [
                dot1(normed, gkv_ref[:, part:], TN),
                dot1(rows_z(mixer_ref, offset), gated_ref[...], TN),
            ],
        )


def input_grads(
    rim_ref, gq_ref, gkv_ref, gscal_ref, og_ref, left_ref, right_ref, out_ref, first_ref, second_ref
):
    inner = HEADS * DK
    part = inner // 2
    tokens = 2 * TOK

    @pl.when(pl.program_id(0) == 0)
    def _():
        first_ref[:, :inner] = gq_ref[:tokens, :]
        first_ref[:, inner : inner + 128] = gscal_ref[...]
        first_ref[:, inner + 128 : inner + 128 + part] = gkv_ref[:tokens, :part]
        first_ref[:, inner + 128 + part :] = og_ref[...]
        second_ref[...] = gkv_ref[:tokens, part:]
        for s in range(2):
            rows = slice((s + 1) * TOK - HALO, (s + 1) * TOK)
            rim = rim_ref[s * HALO : (s + 1) * HALO, :].astype(f32)

            def put(ref, lanes, came):
                ref[rows, lanes] = (ref[rows, lanes].astype(f32) + came).astype(bf16)

            put(first_ref, slice(0, inner), rim[:, :inner])
            put(
                first_ref,
                slice(inner + 128, inner + 128 + part),
                rim[:, inner : inner + part],
            )
            put(second_ref, slice(0, inner + part), rim[:, inner + part :])

    total = dot1(first_ref[...], left_ref[...], NT)
    total = total + dot1(second_ref[...], right_ref[:, : inner + part], NT)
    out_ref[...] = total.astype(bf16)


def ignoring(kernel, at, count):
    def inner_kernel(*refs):
        kernel(*refs[:at], *refs[at + count :])

    return inner_kernel


def dep_specs(deps):
    return [pl.BlockSpec(memory_space=pl.ANY) for _ in deps]


def cost(flops, moved):
    return pl.CostEstimate(flops=flops, bytes_accessed=moved, transcendentals=0)


def params():
    return pltpu.CompilerParams(vmem_limit_bytes=VMEM)


def whole(shape):
    return pl.BlockSpec(shape, lambda s: (0,) * len(shape))


def by_rows(rows, cols, base=0, lane=0):
    return pl.BlockSpec((rows, cols), lambda s: (base + s, lane))


def by_lead(*shape):
    return pl.BlockSpec(shape, lambda s: (s,) + (0,) * (len(shape) - 1))


def mixer_specs():
    wide = 3 * HEADS * DK
    return [
        by_rows(TOK, wide),
        by_rows(HALO, wide, 2 * TOK // HALO),
        by_rows(TOK, 128),
        whole((1, 128)),
        whole((TAPS, wide)),
        by_lead(1, TOK, 8),
        by_lead(1, 1, TOK),
    ]


def run_chunk_forward(pre, scal, rates, taps, marks, docs):
    quarter = DK // HEADS
    wide = 3 * HEADS * DK
    return pl.pallas_call(
        chunk_forward,
        grid=(2,),
        in_specs=mixer_specs(),
        out_specs=[
            by_lead(16, DK + quarter, DK),
            by_lead(HEADS, TOK, DK),
            by_lead(HEADS, TOK, DK),
            by_lead(HEADS, TOK, DK),
            by_lead(HEADS, TOK, 2 * DK),
        ],
        out_shape=[
            jax.ShapeDtypeStruct((SEQ, DK + quarter, DK), bf16),
            jax.ShapeDtypeStruct((8, TOK, DK), bf16),
            jax.ShapeDtypeStruct((8, TOK, DK), f32),
            jax.ShapeDtypeStruct((8, TOK, DK), bf16),
            jax.ShapeDtypeStruct((8, TOK, 2 * DK), f32),
        ],
        scratch_shapes=[pltpu.VMEM((HALO + TOK, wide), f32)],
        compiler_params=params(),
        cost_estimate=cost(10**10, 6 * 10**6),
    )(pre, pre, scal, rates, taps, marks, docs)


def run_scan_forward(got):
    return pl.pallas_call(
        scan_forward,
        out_shape=jax.ShapeDtypeStruct((SEQ, DK // HEADS, DK), bf16),
        compiler_params=params(),
        cost_estimate=cost(10**9, 3 * 10**6),
    )(got)


def run_scan_backward(got, local, deps):
    vmem = pl.BlockSpec(memory_space=pltpu.VMEM)
    return pl.pallas_call(
        ignoring(scan_backward, 2, len(deps)),
        in_specs=[vmem, vmem] + dep_specs(deps),
        out_specs=vmem,
        out_shape=jax.ShapeDtypeStruct((SEQ, DK // HEADS, DK), bf16),
        compiler_params=params(),
        cost_estimate=cost(10**9, 3 * 10**6),
    )(got, local, *deps)


def run_gate_forward(p, z, state, og, gain, deps):
    inner = HEADS * DK
    return pl.pallas_call(
        ignoring(gate_forward, 5, len(deps)),
        grid=(2,),
        in_specs=[
            by_lead(HEADS, TOK, DK),
            by_lead(HEADS, TOK, DK),
            by_lead(HEADS, DK, DK),
            by_rows(TOK, inner),
            whole((1, DK)),
        ]
        + dep_specs(deps),
        out_specs=[by_rows(TOK, inner), by_rows(TOK, inner)],
        out_shape=[
            jax.ShapeDtypeStruct((2 * TOK, inner), f32),
            jax.ShapeDtypeStruct((2 * TOK, inner), bf16),
        ],
        compiler_params=params(),
        cost_estimate=cost(10**9, 3 * 10**6),
    )(p, z, state, og, gain, *deps)


def run_gate_backward(gg, heads_out, og, gain, p):
    inner = HEADS * DK
    return pl.pallas_call(
        gate_backward,
        grid=(2,),
        in_specs=[
            by_rows(TOK, inner),
            by_rows(TOK, inner),
            by_rows(TOK, inner),
            whole((1, DK)),
            by_lead(HEADS, TOK, DK),
        ],
        out_specs=[
            by_rows(TOK, inner),
            by_rows(TOK, inner),
            by_lead(16, DK // HEADS, DK),
            whole((8, DK)),
        ],
        out_shape=[
            jax.ShapeDtypeStruct((2 * TOK, inner), f32),
            jax.ShapeDtypeStruct((2 * TOK, inner), bf16),
            jax.ShapeDtypeStruct((SEQ, DK // HEADS, DK), bf16),
            jax.ShapeDtypeStruct((8, DK), f32),
        ],
        compiler_params=params(),
        cost_estimate=cost(10**9, 3 * 10**6),
    )(gg, heads_out, og, gain, p)


def run_chunk_backward_early(pre, scal, rates, taps, marks, docs, uw, state, do, deps):
    inner = HEADS * DK
    wide = 3 * inner
    square = jax.ShapeDtypeStruct((8, TOK, DK), f32)
    return pl.pallas_call(
        ignoring(chunk_backward_early, 10, len(deps)),
        grid=(2,),
        in_specs=mixer_specs()
        + [
            by_lead(HEADS, TOK, 2 * DK),
            by_lead(HEADS, DK, DK),
            by_rows(TOK, inner),
        ]
        + dep_specs(deps),
        out_specs=[
            whole((2 * (TOK + HALO), inner)),
            whole((TAPS, inner)),
            by_lead(HEADS, TOK, DK),
            by_lead(HEADS, TOK, DK),
            by_lead(HEADS, TOK, DK),
            by_lead(HEADS, TOK, DK),
            by_rows(TOK, 128),
        ],
        out_shape=[
            jax.ShapeDtypeStruct((2 * (TOK + HALO), inner), bf16),
            jax.ShapeDtypeStruct((TAPS, inner), f32),
            jax.ShapeDtypeStruct((8, TOK, DK), bf16),
            square,
            square,
            square,
            jax.ShapeDtypeStruct((2 * TOK, 128), f32),
        ],
        scratch_shapes=[
            pltpu.VMEM((HALO + TOK, wide), f32),
            pltpu.VMEM((HALO + TOK, inner), f32),
        ],
        compiler_params=params(),
        cost_estimate=cost(5 * 10**9, 10**7),
    )(pre, pre, scal, rates, taps, marks, docs, uw, state, do, *deps)


def run_chunk_backward_late(
    pre, scal, rates, taps, marks, docs, x, state, adj, early, deps
):
    inner = HEADS * DK
    wide = 3 * inner
    return pl.pallas_call(
        ignoring(chunk_backward_late, 15, len(deps)),
        grid=(2,),
        in_specs=mixer_specs()
        + [
            by_lead(HEADS, TOK, DK),
            by_lead(HEADS, DK, DK),
            by_lead(HEADS, DK, DK),
            by_lead(HEADS, TOK, DK),
            by_lead(HEADS, TOK, DK),
            by_lead(HEADS, TOK, DK),
            by_lead(HEADS, TOK, DK),
            by_rows(TOK, 128),
        ]
        + dep_specs(deps),
        out_specs=[
            whole((2 * (TOK + HALO), 2 * inner)),
            by_rows(TOK, 128),
            whole((TAPS, 2 * inner)),
            whole((8, 128)),
        ],
        out_shape=[
            jax.ShapeDtypeStruct((2 * (TOK + HALO), 2 * inner), bf16),
            jax.ShapeDtypeStruct((2 * TOK, 128), bf16),
            jax.ShapeDtypeStruct((TAPS, 2 * inner), f32),
            jax.ShapeDtypeStruct((8, 128), f32),
        ],
        scratch_shapes=[
            pltpu.VMEM((HALO + TOK, 2 * inner), f32),
            pltpu.VMEM((HALO + TOK, 2 * inner), f32),
        ],
        compiler_params=params(),
        cost_estimate=cost(5 * 10**9, 10**7),
    )(pre, pre, scal, rates, taps, marks, docs, x, state, adj, *early, *deps)


def run_row_grads(lhs, rhs, groups, deps=()):
    width = lhs[0].shape[1]
    cols = sum(rhs[group[0][1]].shape[1] for group in groups)
    return pl.pallas_call(
        partial(row_grads, groups, len(lhs), len(rhs)),
        grid=(4,),
        in_specs=[pl.BlockSpec((m.shape[0], width // 4), lambda s: (0, s)) for m in lhs]
        + [whole(m.shape) for m in rhs]
        + dep_specs(deps),
        out_specs=pl.BlockSpec((width // 4, cols), lambda s: (s, 0)),
        out_shape=jax.ShapeDtypeStruct((width, cols), bf16),
        compiler_params=params(),
        cost_estimate=cost(2 * rhs[0].shape[0] * width * cols, 2 * width * cols),
    )(*lhs, *rhs, *deps)


def run_mixer_grads(offsets, halves, *arrays, deps=()):
    width = arrays[0].shape[1]
    inner = HEADS * DK
    vmem = pl.BlockSpec(memory_space=pltpu.VMEM)
    place = jnp.stack([place_of("x"), place_of("z")]).astype(jnp.int32)
    shapes = [
        (width // 4 // halves, cols)
        for cols in (2 * inner + inner // 2 + 128, 2 * inner + inner // 2)
        for _ in range(halves * len(offsets))
    ]
    return pl.pallas_call(
        ignoring(partial(mixer_grads, offsets), 8, len(deps)),
        in_specs=[pl.BlockSpec(memory_space=pltpu.SMEM)] + [vmem] * 7 + dep_specs(deps),
        out_specs=[vmem] * len(shapes),
        out_shape=[jax.ShapeDtypeStruct(shape, bf16) for shape in shapes],
        compiler_params=params(),
        cost_estimate=cost(2 * 256 * width * 5 * inner, 2 * width * 5 * inner),
    )(place, *arrays, *deps)


def run_input_grads(rim, gq, gkv, gscal, og, left, right):
    inner = HEADS * DK
    width = left.shape[0]
    tokens = 2 * TOK
    cut = width // 4
    return pl.pallas_call(
        input_grads,
        grid=(4,),
        in_specs=[whole(m.shape) for m in (rim, gq, gkv, gscal, og)]
        + [
            by_rows(cut, left.shape[1]),
            by_rows(cut, right.shape[1]),
        ],
        out_specs=pl.BlockSpec((tokens, cut), lambda s: (0, s)),
        out_shape=jax.ShapeDtypeStruct((tokens, width), bf16),
        scratch_shapes=[
            pltpu.VMEM((tokens, left.shape[1]), bf16),
            pltpu.VMEM((tokens, inner + inner // 2), bf16),
        ],
        compiler_params=params(),
        cost_estimate=cost(2 * tokens * width * 5 * inner, 2 * width * 5 * inner),
    )(rim, gq, gkv, gscal, og, left, right)


SEQ_AXES = ("x", "z", "y")
GROUP_AXES = ("y", "head")


def passed_along(array, by):
    pairs = [(i, i + by) for i in range(SEQ) if 0 <= i + by < SEQ]
    return lax.ppermute(array, SEQ_AXES, pairs)


def along(array, axis, by):
    count = lax.axis_size(axis)
    return lax.ppermute(array, axis, [(i, (i + by) % count) for i in range(count)])


def place_of(axis):
    return lax.axis_index(axis)


def flipped(array, axes, mask):
    count = lax.axis_size(axes)
    return lax.ppermute(array, axes, [(i, i ^ mask) for i in range(count)])


def pick(array, index, dim):
    return lax.dynamic_index_in_dim(array, index, dim, keepdims=False)


def ordered(mine, other, place, axis=0):
    first = place == 0
    return jnp.concatenate(
        [jnp.where(first, mine, other), jnp.where(first, other, mine)], axis=axis
    )


def later(array, *deps):
    for dep in deps:
        first = lax.slice(dep, (0,) * dep.ndim, (1,) * dep.ndim).reshape(())
        array = array + (first * 0).astype(array.dtype)
    return array


def gather_last(first, second):
    near, far, halfway = near_and_far(first, second, ("z", "x"))
    outs = []
    for i, (array, axis, dim) in enumerate(((first, "z", 1), (second, "x", 0))):
        place = place_of(axis)
        shape = list(array.shape)
        shape.insert(dim, 4)
        out = jnp.zeros(shape, array.dtype)
        block = jnp.concatenate(far[2 * i : 2 * i + 2], axis=0)
        for offset, block in ((0, array), (-1, near[2 * i]), (-2, block), (1, near[2 * i + 1])):
            out = lax.dynamic_update_index_in_dim(out, block, (place + offset) % 4, dim)
        outs.append(out.reshape(-1, array.shape[-1]))
    return outs[0], outs[1], halfway


def exchange(array, axis):
    return lax.all_to_all(array, axis, split_axis=0, concat_axis=0, tiled=True)


def head_place():
    index = lax.axis_index("head")
    return index // 2, index % 2


def core_scatter(partial_rows):
    core = head_place()[1]
    rows = partial_rows.shape[0] // HEADS
    blocks = partial_rows.astype(bf16).reshape(2, 2, rows, -1)
    got = flipped(pick(blocks, 1 - core, 1), "head", 1)
    return pick(blocks, core, 1).astype(f32) + got.astype(f32), got


def chip_scatter(both, *gates):
    chip = head_place()[0]
    got = flipped(later(pick(both, 1 - chip, 0), *gates).astype(bf16), "head", 2)
    return pick(both, chip, 0) + got.astype(f32)


def head_gather(rows):
    chip, core = head_place()
    got = flipped(rows, "head", 2)
    first = chip == 0
    chips = jnp.stack([jnp.where(first, rows, got), jnp.where(first, got, rows)])
    got = flipped(chips, "head", 1)
    first = core == 0
    cores = [jnp.where(first, chips, got), jnp.where(first, got, chips)]
    return jnp.stack(cores, axis=1).reshape(HEADS * rows.shape[0], -1)


def group_scatter(partial_rows):
    chip, core = head_place()
    place = place_of("y") * 2 + chip
    blocks = partial_rows.astype(bf16).reshape(4, 2, -1, partial_rows.shape[1])
    got = flipped(pick(blocks, 1 - core, 1), GROUP_AXES, 1)
    both = pick(blocks, core, 1).astype(f32) + got.astype(f32)
    total = pick(both, place, 0)
    for mask in (2, 1, 3):
        part = pick(both, jnp.bitwise_xor(place, mask), 0).astype(bf16)
        total = total + flipped(part, GROUP_AXES, 2 * mask).astype(f32)
    return total, got


def group_gather(rows):
    chip, core = head_place()
    place = place_of("y") * 2 + chip
    out = jnp.zeros((4,) + rows.shape, rows.dtype)
    for mask in (2, 1, 3, 0):
        got = flipped(rows, GROUP_AXES, 2 * mask) if mask else rows
        out = lax.dynamic_update_index_in_dim(out, got, jnp.bitwise_xor(place, mask), 0)
    got = flipped(out, GROUP_AXES, 1)
    first = core == 0
    cores = [jnp.where(first, out, got), jnp.where(first, got, out)]
    return jnp.stack(cores, axis=1).reshape(8 * rows.shape[0], -1)


def in_vmem(kernel, shapes, place, *arrays, deps=()):
    vmem = pl.BlockSpec(memory_space=pltpu.VMEM)
    moved = sum(2 * a.size for a in arrays)
    return pl.pallas_call(
        ignoring(kernel, 1 + len(arrays), len(deps)),
        in_specs=[pl.BlockSpec(memory_space=pltpu.SMEM)] + [vmem] * len(arrays) + dep_specs(deps),
        out_specs=[vmem] * len(shapes),
        out_shape=[jax.ShapeDtypeStruct(shape, kind) for shape, kind in shapes],
        compiler_params=params(),
        cost_estimate=cost(moved, moved),
    )(place, *arrays, *deps)


def add_far(place_ref, *refs):
    for i in range(2):
        right, left, ahead, behind = refs[4 * i : 4 * i + 4]
        right_out, left_out = refs[8 + 2 * i : 10 + 2 * i]
        half = ahead.shape[0]
        total = right[:half].astype(f32) + ahead[...].astype(f32)
        right_out[:half] = total.astype(bf16)
        right_out[half:] = right[half:]
        left_out[:half] = left[:half]
        total = left[half:].astype(f32) + behind[...].astype(f32)
        left_out[half:] = total.astype(bf16)


def add_and_cut(place_ref, *refs):
    for i in range(2):
        members = refs[3 * i : 3 * i + 3]
        outs = refs[6 + 4 * i : 10 + 4 * i]
        rows = members[0].shape[0] // 4
        for out, by in zip(outs, (0, 2, 1, 3)):
            start = pl.multiple_of(lax.rem(place_ref[1 - i] + by, 4) * rows, rows)
            total = members[0][pl.ds(start, rows), :].astype(f32)
            for member in members[1:]:
                total = total + member[pl.ds(start, rows), :].astype(f32)
            out[...] = total.astype(bf16)


def add_and_halve(place_ref, *refs):
    kept, sent = refs[8:]
    rows = kept.shape[0]
    lane = 0
    for i in range(2):
        parts = refs[4 * i : 4 * i + 4]
        lanes = slice(lane, lane + parts[0].shape[1])
        lane += parts[0].shape[1]
        for out, at in ((kept, place_ref[2]), (sent, 1 - place_ref[2])):
            start = pl.multiple_of(at * rows, rows)
            total = parts[0][pl.ds(start, rows), :].astype(f32)
            for part in parts[1:]:
                total = total + part[pl.ds(start, rows), :].astype(f32)
            out[:, lanes] = total.astype(out.dtype)


def places():
    return jnp.stack([place_of(axis) for axis in SEQ_AXES]).astype(jnp.int32)


def reduce_near(owns, arrays, deps):
    shapes = [(arrays[i].shape, bf16) for i in (0, 1, 4, 5)]
    sums = in_vmem(add_far, shapes, places(), *arrays, deps=deps)
    gate = sums[0]
    arrays = []
    for i, axis in enumerate(("x", "z")):
        arrays += [owns[i], along(sums[2 * i], axis, 1), along(sums[2 * i + 1], axis, -1)]
    return arrays, gate


def reduce_cross(arrays, deps):
    shapes = []
    for own in (arrays[0], arrays[3]):
        shapes += [((own.shape[0] // 4, own.shape[1]), bf16)] * 4
    cut = in_vmem(add_and_cut, shapes, places(), *arrays, deps=deps)
    arrays = []
    for i, axis in enumerate(("z", "x")):
        own, two, one, three = cut[4 * i : 4 * i + 4]
        arrays += [own, along(two, axis, 2), along(one, axis, 1), along(three, axis, -1)]
    return arrays, cut[0]


def reduce_end(arrays, deps):
    rows, cols = arrays[0].shape[0] // 2, arrays[0].shape[1] + arrays[4].shape[1]
    shapes = [((rows, cols), f32), ((rows, cols), bf16)]
    kept, sent = in_vmem(add_and_halve, shapes, places(), *arrays, deps=deps)
    return kept + along(sent, "y", 1).astype(f32), sent


def pair_up(place_ref, left, left_other, right, right_other, left_out, right_out):
    rows = left.shape[0]
    mine = pl.multiple_of(place_ref[2] * rows, rows)
    other = pl.multiple_of((1 - place_ref[2]) * rows, rows)
    left_out[pl.ds(mine, rows), :] = left[...]
    left_out[pl.ds(other, rows), :] = left_other[...]
    right_out[pl.ds(mine, rows), :] = right[...]
    right_out[pl.ds(other, rows), :] = right_other[...]


def pass_on(place_ref, *refs):
    for i in range(2):
        half = refs[4 + 2 * i].shape[0]
        refs[4 + 2 * i][...] = refs[2 * i][:half]
        refs[5 + 2 * i][...] = refs[2 * i + 1][half:]


def put_in_place(axes, place_ref, *refs):
    for i in range(2):
        out = refs[10 + i]
        own, left, right, far_a, far_b = refs[5 * i : 5 * i + 5]
        place = place_ref[axes[i]]
        half = far_a.shape[0]
        out[place] = own[...]
        out[lax.rem(place + 3, 4)] = left[...]
        out[lax.rem(place + 1, 4)] = right[...]
        out[lax.rem(place + 2, 4), :half] = far_a[...]
        out[lax.rem(place + 2, 4), half:] = far_b[...]


def near_and_far(first, second, axes):
    near = []
    for array, axis in ((first, axes[0]), (second, axes[1])):
        near += [along(array, axis, 1), along(array, axis, -1)]
    shapes = []
    for array in (first, second):
        shapes += [((array.shape[0] // 2,) + array.shape[1:], bf16)] * 2
    halves = in_vmem(pass_on, shapes, places(), *near)
    far = []
    for i in range(2):
        far += [along(halves[2 * i], axes[i], 1), along(halves[2 * i + 1], axes[i], -1)]
    return near, far, halves[0]


def sum_along(array, axis):
    total = array
    for by in range(1, lax.axis_size(axis)):
        total = total + along(array, axis, by)
    return total


def mm(a, b, dims="ij,jk->ik"):
    return jnp.einsum(dims, a, b, preferred_element_type=f32)


def row_scale(x):
    return lax.rsqrt(jnp.mean(x * x, axis=-1, keepdims=True) + norm_eps)


def norm_pull(x, scale, gain, grad):
    unit = x * scale
    scaled = grad * gain
    return scale * (scaled - unit * jnp.mean(scaled * unit, axis=-1, keepdims=True))


def doc_tables(doc_lengths):
    first = lax.axis_index(SEQ_AXES) * TOK - (TAPS - 1)
    ends = jnp.cumsum(doc_lengths, axis=1)
    places = first + jnp.arange(TOK + TAPS - 1, dtype=jnp.int32)
    counted = jnp.sum((places[None, :, None] >= ends[:, None, :]).astype(jnp.int32), axis=2)
    ext = jnp.where(places[None, :] >= 0, counted, -1)
    local = ext[:, TAPS - 1 :]
    columns = [(ext[:, o : o + TOK] == local) for o in range(TAPS - 1)]
    columns.append(local == ext[:, TAPS - 2 : TAPS - 1])
    columns.append(local == local[:, -1:])
    columns.append(local)
    columns += [jnp.zeros_like(local)] * 2
    marks = jnp.stack([c.astype(f32) for c in columns], axis=-1)
    return marks, local.astype(f32)[:, None, :]


def body(
    inputs, doc_lengths, norm_in, query_weight, key_weight, value_weight, outgate_weight,
    scalar_weight, conv_kernel, decay_rate, head_norm, output_weight, norm_ffn, gate_weight,
    up_weight, down_weight, grad_out,
):
    width = inputs.shape[2]
    inner = HEADS * DK
    hidden = gate_weight.shape[1]
    head_index = lax.axis_index("head")
    quarter = 2 * TOK // HEADS

    gains = jnp.stack([norm_in, norm_ffn], axis=1)
    misc = jnp.concatenate([scalar_weight.reshape(-1, 2 * HEADS), gains], axis=1)
    misc = jnp.pad(misc, ((0, 0), (0, 128 - misc.shape[1])))
    part = inner // 2
    left = jnp.concatenate([query_weight, misc, key_weight[:, :part], outgate_weight], axis=1)
    right = jnp.concatenate([key_weight[:, part:], value_weight, output_weight.T], axis=1)
    y_place = place_of("y")
    rows = left.shape[0]
    left, right = in_vmem(
        pair_up,
        [((2 * rows, left.shape[1]), bf16), ((2 * rows, right.shape[1]), bf16)],
        places(),
        left, along(left, "y", 1), right, along(right, "y", 1),
    )
    near, far, _ = near_and_far(left, right, ("x", "z"))
    left, right = in_vmem(
        partial(put_in_place, (0, 1)),
        [((4, 2 * rows, part.shape[1]), bf16) for part in (left, right)],
        places(),
        left, *near[:2], *far[:2], right, *near[2:], *far[2:],
    )
    all_left, all_right, halfway = gather_last(left, right)
    w_gate, w_out_t = all_left[:, -inner:], all_right[:, -inner:]
    w_left, w_right = all_left[:, :-inner], all_right[:, :-inner]
    gains = w_left[:, inner : inner + 128].T[2 * HEADS : 2 * HEADS + 2].astype(f32)
    gain_in, gain_ffn = gains[0:1], gains[1:2]

    units = hidden // 2
    span = -(-units // 128) * 128

    def in_halves(weight):
        halves = weight.reshape(weight.shape[0], 2, units)
        return jnp.pad(halves, ((0, 0), (0, 0), (0, span - units)))

    packed = jnp.concatenate(
        [in_halves(gate_weight), in_halves(up_weight), in_halves(down_weight.T)], axis=2
    )
    other = along(later(pick(packed, 1 - y_place, 1), left), "y", 1)
    packed = later(ordered(pick(packed, y_place, 1), other, y_place), halfway)
    w_ffn = lax.all_gather(packed, ("x", "z"), axis=0, tiled=True)
    w_gateup = w_ffn[:, : 2 * span]
    w_down_t = w_ffn[:, 2 * span :]

    marks, docs_row = doc_tables(doc_lengths)
    taps = jnp.transpose(conv_kernel.astype(f32), (1, 0, 2)).reshape(TAPS, 3 * inner)
    rates = jnp.zeros((1, 128), f32)
    rates = rates.at[0, HEADS : 2 * HEADS].set(decay_rate.astype(f32))
    gain_head = head_norm.astype(f32).reshape(1, DK)

    halo = passed_along(inputs[:, TOK - HALO :], 1)
    tokens = inputs.reshape(2 * TOK, width)
    all_rows = jnp.concatenate([tokens, halo.reshape(2 * HALO, width)], axis=0).astype(f32)
    scale_in = row_scale(all_rows)
    normed_all = (all_rows * scale_in * gain_in).astype(bf16)
    normed_in = normed_all[: 2 * TOK]

    left = mm(normed_all, w_left)
    right = mm(normed_all, w_right)
    pre = jnp.concatenate(
        [left[:, :inner].astype(bf16), left[:, inner + 128 :].astype(bf16), right.astype(bf16)],
        axis=1,
    )
    scal = left[: 2 * TOK, inner : inner + 128]

    grad_rows = grad_out.reshape(2 * TOK, width)
    grad_other = along(grad_rows, "y", 1)
    send, p, z, x, uw = run_chunk_forward(pre, scal, rates, taps, marks, docs_row)
    out_gate = mm(normed_in, w_gate)
    got = exchange(send, SEQ_AXES)
    state = exchange(run_scan_forward(got), SEQ_AXES).reshape(8, DK, DK)
    heads_out, gated_rows = run_gate_forward(
        p, z, state, out_gate, gain_head, (grad_other,)
    )

    mine = partial(lax.dynamic_slice_in_dim, start_index=head_index * quarter, slice_size=quarter)
    residual = mine(tokens).astype(f32) + chip_scatter(
        core_scatter(mm(gated_rows, w_out_t, "ij,kj->ik"))[0]
    )
    scale_ffn = row_scale(residual)
    normed_ffn = group_gather((residual * scale_ffn * gain_ffn).astype(bf16))

    group_grads = ordered(grad_rows, grad_other, y_place)
    grad_act = mm(group_grads, w_down_t)
    gate_up = mm(normed_ffn, w_gateup)
    gate, up = gate_up[:, :span], gate_up[:, span:]
    sig = sigmoid(gate)
    silu = gate * sig
    product = (silu * up).astype(bf16)
    gu_grad = jnp.concatenate(
        [
            (grad_act * up * sig * (1.0 + gate * (1.0 - sig))).astype(bf16),
            (grad_act * silu).astype(bf16),
        ],
        axis=1,
    )
    ffn_part = mm(gu_grad, w_gateup, "ij,kj->ik").astype(bf16)
    grad_normed = group_scatter(ffn_part)[0]
    back = norm_pull(residual, scale_ffn, gain_ffn, grad_normed)
    grad_residual = mine(grad_rows).astype(f32) + back
    grad_mixer = head_gather(grad_residual.astype(bf16))

    grad_gated = mm(grad_mixer, w_out_t)
    do, gate_grad_mix, local, part_gain_head = run_gate_backward(
        grad_gated, heads_out, out_gate, gain_head, p
    )
    local_got = exchange(local, SEQ_AXES)
    early = run_chunk_backward_early(
        pre, scal, rates, taps, marks, docs_row, uw, state, do, ()
    )
    gq, gtaps_q = early[:2]
    ffn_all = run_row_grads(
        [normed_ffn, group_grads], [gu_grad, product], (((0, 0),), ((1, 1),)), (local,)
    )
    ffn = lax.psum_scatter(ffn_all, ("x", "z"), scatter_dimension=0, tiled=True)
    adj_out = run_scan_backward(got, local_got, (gq,))
    ffn_out, ffn_got = group_scatter(mm(later(product, local), w_down_t, "ij,kj->ik"))
    adj = exchange(adj_out, SEQ_AXES).reshape(8, DK, DK)
    gkv, gscal, gtaps_kv, grate = run_chunk_backward_late(
        pre, scal, rates, taps, marks, docs_row, x, state, adj, early[2:], (ffn_got,)
    )

    arrays = (normed_all, grad_mixer, gate_grad_mix, gq, gkv, gscal, gated_rows)
    far = run_mixer_grads((2,), 2, *arrays)
    blocks = run_mixer_grads((1, 3, 0), 1, *arrays, deps=(far[0], ffn_out))
    owns, partials = (blocks[2], blocks[5]), []
    for i, axis in enumerate(("x", "z")):
        partials += blocks[3 * i : 3 * i + 2]
        partials += [along(far[2 * i], axis, 1), along(far[2 * i + 1], axis, -1)]

    gtaps = jnp.concatenate([gtaps_q, gtaps_kv], axis=1).reshape(12, inner)
    tail = jnp.concatenate([part_gain_head[:1], grate[:1]], axis=1)
    tail = jnp.pad(tail, ((0, 3), (0, inner - tail.shape[1])))
    small = sum_along(later(jnp.concatenate([gtaps, tail], axis=0), blocks[0]), "x")
    rim = jnp.concatenate([gq[2 * TOK :], gkv[2 * TOK :]], axis=1)
    rim = passed_along(rim, -1)
    input_sent = run_input_grads(
        rim, gq, gkv, gscal, gate_grad_mix, all_left, all_right
    )
    partials, near_gate = reduce_near(owns, partials, (small, input_sent))
    ffn = ffn.reshape(2, -1, 3, span)[..., :units]
    ffn_other = along(later(pick(ffn, 1 - y_place, 0), near_gate), "y", 1)
    ffn = ordered(pick(ffn, y_place, 0), ffn_other, y_place, 2).astype(f32)
    by_core = core_scatter(later(input_sent, near_gate))[0]
    grad_normed_in = chip_scatter(by_core)
    own = mine(tokens).astype(f32)
    back_in = norm_pull(own, row_scale(own), gain_in, grad_normed_in)
    both = jnp.concatenate([residual + ffn_out, grad_residual + back_in], axis=1)
    both = both.astype(bf16)
    partials, cross_gate = reduce_cross(partials, (both, ffn_other))
    small = sum_along(later(small, cross_gate), "z")
    mixer_w, end_gate = reduce_end(partials, ())
    small = sum_along(later(small, end_gate), "y")
    both = head_gather(later(both, cross_gate))
    outputs, grad_in = both[:, :width], both[:, width:].astype(f32)

    rows = width // SEQ
    key_at = 2 * inner + 128
    grad_conv = jnp.transpose(small[:12].reshape(TAPS, 3, inner), (1, 0, 2))

    def gain_grad(gain, weights, grads):
        total = 0.0
        for weight, grad in zip(weights, grads):
            total = total + jnp.sum(weight.astype(f32) * grad, axis=1)
        return total / gain.astype(f32)

    grad_scalar = mixer_w[:, 2 * inner : 2 * inner + 2 * HEADS]
    gain_parts = jnp.concatenate(
        [
            gain_grad(
                norm_in,
                (outgate_weight, query_weight, scalar_weight.reshape(rows, -1), key_weight, value_weight),
                (
                    mixer_w[:, :inner],
                    mixer_w[:, inner : 2 * inner],
                    grad_scalar,
                    mixer_w[:, key_at : key_at + inner],
                    mixer_w[:, key_at + inner : key_at + 2 * inner],
                ),
            ),
            gain_grad(norm_ffn, (gate_weight, up_weight), (ffn[:, 0], ffn[:, 1])),
            small[12, :DK],
        ]
    )
    shared = sum_along(gain_parts[None], "head")[0]
    return (
        outputs.reshape(inputs.shape),
        grad_in.reshape(inputs.shape),
        shared[:rows],
        mixer_w[:, inner : 2 * inner],
        mixer_w[:, key_at : key_at + inner],
        mixer_w[:, key_at + inner : key_at + 2 * inner],
        mixer_w[:, :inner],
        grad_scalar.reshape(rows, 2, HEADS),
        grad_conv,
        small[12, DK + HEADS : DK + 2 * HEADS],
        shared[2 * rows :],
        mixer_w[:, key_at + 2 * inner :].T,
        shared[rows : 2 * rows],
        ffn[:, 0],
        ffn[:, 1],
        ffn[:, 2].T,
    )


def solution(mesh):
    mesh = Mesh(mesh.devices.reshape(4, 4, 2, HEADS), ("x", "z", "y", "head"))
    seq = SEQ_AXES
    weight = P(seq, "head")
    weight_t = P("head", seq)
    tokens = P(None, seq, None)
    scalars = P(seq, None, "head")
    taps = P(None, None, "head")
    return jax.shard_map(
        body,
        mesh=mesh,
        in_specs=(
            tokens, P(), P(seq), weight, weight, weight, weight, scalars, taps, P("head"), P(),
            weight_t, P(seq), weight, weight, weight_t, tokens,
        ),
        out_specs=(
            tokens, tokens, P(seq), weight, weight, weight, weight, scalars, taps, P("head"),
            P(), weight_t, P(seq), weight, weight, weight_t,
        ),
        check_vma=False,
    )
```

```python
from functools import partial

import jax
import jax.numpy as jnp
from jax import lax
from jax.experimental import pallas as pl
from jax.experimental.pallas import tpu as pltpu
from jax.sharding import Mesh
from jax.sharding import PartitionSpec as P

f32 = jnp.float32
bf16 = jnp.bfloat16
norm_eps = 1e-06
head_eps = 1e-05
SEQ = 32
HEADS = 4
DK = 128
TOK = 128
TAPS = 4
HALO = 16
VMEM = 56 * 1024 * 1024

NN = (((1,), (0,)), ((), ()))
NT = (((1,), (1,)), ((), ()))
TN = (((0,), (0,)), ((), ()))


def dot1(a, b, dims=NN):
    return lax.dot_general(a.astype(bf16), b.astype(bf16), dims, preferred_element_type=f32)


def split(a):
    high = a.astype(bf16)
    return high, (a - high.astype(f32)).astype(bf16)


def dot3(a, b, dims=NN):
    ah, al = split(a)
    bh, bl = split(b)
    return dot1(ah, bh, dims) + (dot1(ah, bl, dims) + dot1(al, bh, dims))


def dot2(exact, b, dims=NN):
    high = b.astype(bf16)
    rest = b - high.astype(f32)
    mid = rest.astype(bf16)
    low = (rest - mid.astype(f32)).astype(bf16)
    return dot1(exact, high, dims) + (dot1(exact, mid, dims) + dot1(exact, low, dims))


def sigmoid(x):
    return 1.0 / (1.0 + jnp.exp(-x))


def softplus(x):
    return jnp.maximum(x, 0.0) + jnp.log1p(jnp.exp(-jnp.abs(x)))


def iotas():
    rows = lax.broadcasted_iota(jnp.int32, (TOK, TOK), 0)
    cols = lax.broadcasted_iota(jnp.int32, (TOK, TOK), 1)
    return rows, cols


def unit_inverses(stricts):
    rows, cols = iotas()
    eye = (rows == cols).astype(f32)
    apart = jnp.bitwise_xor(rows, cols)
    results = []
    first = (apart == 1) & (rows > cols)
    results = [eye - jnp.where(first, a, 0.0) for a in stricts]
    size = 2
    while size < TOK:
        corner = (apart >= size) & (apart < 2 * size) & (rows > cols)
        parts = [dot3(jnp.where(corner, a, 0.0), x) for a, x in zip(stricts, results)]
        results = [x - dot3(x, c) for x, c in zip(results, parts)]
        size *= 2
    return results


def decays(scal, rates, marks, docs_row):
    rows, cols = iotas()
    strength = sigmoid(scal)
    log_decay = -rates * softplus(scal)
    lower = (rows >= cols).astype(bf16)
    total = dot2(lower, log_decay)
    total_t = jnp.transpose(total)
    same = marks[:, 5:6] == docs_row
    causal = same & (rows >= cols)
    return strength, total, total_t, causal, rows > cols


def conv_parts(ext_ref, weights, marks, lane):
    out = None
    for tap in range(TAPS):
        piece = ext_ref[pl.ds(HALO - TAPS + 1 + tap, TOK), pl.ds(lane, DK)]
        if tap < TAPS - 1:
            piece = piece * marks[:, tap : tap + 1]
        piece = piece * weights[tap : tap + 1, lane : lane + DK]
        out = piece if out is None else out + piece
    return out


def unit_scale(x):
    return lax.rsqrt(jnp.sum(x * x, axis=-1, keepdims=True) + norm_eps)


def chunk_forward(
    pre_ref, rim_ref, scal_ref, rate_ref, taps_ref, marks_ref, docs_ref,
    send_ref, p_ref, z_ref, x_ref, uw_ref, ext_ref,
):
    inner = HEADS * DK
    ext_ref[0:HALO, :] = rim_ref[...].astype(f32)
    ext_ref[HALO:, :] = pre_ref[...].astype(f32)
    marks = marks_ref[0]
    weights = taps_ref[...]
    strength, total, total_t, causal, below = decays(
        scal_ref[...], rate_ref[...], marks, docs_ref[0]
    )
    rows, cols = iotas()
    reached, tail = marks[:, 3:4], marks[:, 4:5]
    heads = []
    for h in range(HEADS):
        acts = []
        for c in range(3):
            conv = conv_parts(ext_ref, weights, marks, c * inner + h * DK)
            acts.append(conv * sigmoid(conv))
        q = (acts[0] * unit_scale(acts[0])).astype(bf16)
        k = (acts[1] * unit_scale(acts[1])).astype(bf16)
        v = acts[2].astype(bf16)
        c_col = total[:, HEADS + h : HEADS + h + 1]
        c_row = total_t[HEADS + h : HEADS + h + 1, :]
        decay = jnp.where(causal, jnp.exp(jnp.where(causal, c_col - c_row, 0.0)), 0.0)
        b = strength[:, h : h + 1]
        gram = dot1(k, k, NT)
        strict = jnp.where(below, b * gram * decay, 0.0)
        heads.append((q, k, v, c_col, decay, b, strict))
    inverses = unit_inverses([head[6] for head in heads])
    for h in range(HEADS):
        q, k, v, c_col, decay, b, strict = heads[h]
        x = inverses[h]
        start = jnp.exp(c_col) * reached
        kf = k.astype(f32)
        uw = dot3(x, jnp.concatenate([b * v.astype(f32), (b * start) * kf], axis=1))
        scores = dot1(q, k, NT) * decay
        suw = dot3(scores, uw)
        last = c_col[TOK - 1 : TOK, :]
        tail_k = kf * (jnp.exp(last - c_col) * tail)
        carry = jnp.exp(last) * reached[TOK - 1 : TOK, :]
        u, w = uw[:, :DK], uw[:, DK:]
        move = jnp.where(rows == cols, carry, 0.0) - dot3(tail_k, w, TN)
        offset_t = dot3(u, tail_k, TN)
        p_ref[h] = (q.astype(f32) * start - suw[:, DK:]).astype(bf16)
        z_ref[h] = suw[:, :DK]
        x_ref[h] = x.astype(bf16)
        uw_ref[h] = uw
        quarter = DK // HEADS
        for j in range(HEADS):
            send_ref[HEADS * h + j, 0:DK, :] = move.astype(bf16)
            send_ref[HEADS * h + j, DK : DK + quarter, :] = offset_t[
                j * quarter : (j + 1) * quarter
            ].astype(bf16)


def scan_forward(got_ref, out_ref):
    state = jnp.zeros((DK // HEADS, DK), f32)
    for i in range(SEQ):
        out_ref[i] = state.astype(bf16)
        if i + 1 < SEQ:
            high, low = split(state)
            both = dot1(jnp.concatenate([high, low], axis=0), got_ref[i, 0:DK, :], NT)
            half = DK // HEADS
            state = both[:half] + both[half:] + got_ref[i, DK : DK + half, :].astype(f32)


def scan_backward(got_ref, local_ref, out_ref):
    state = jnp.zeros((DK // HEADS, DK), f32)
    for i in range(SEQ - 1, -1, -1):
        out_ref[i] = state.astype(bf16)
        if i > 0:
            high, low = split(state)
            both = dot1(jnp.concatenate([high, low], axis=0), got_ref[i, 0:DK, :])
            half = DK // HEADS
            state = both[:half] + both[half:] + local_ref[i].astype(f32)


def gate_forward(p_ref, z_ref, s_ref, og_ref, gain_ref, heads_ref, gated_ref):
    gain = gain_ref[...]
    for h in range(HEADS):
        lanes = slice(h * DK, (h + 1) * DK)
        out = dot1(p_ref[h], s_ref[h], NT) + z_ref[h]
        heads_ref[:, lanes] = out
        r = lax.rsqrt(jnp.mean(out * out, axis=-1, keepdims=True) + head_eps)
        og = og_ref[:, lanes]
        gated_ref[:, lanes] = (out * r * gain * (og * sigmoid(og))).astype(bf16)


def gate_backward(
    gg_ref, heads_ref, og_ref, gain_ref, p_ref, do_ref, mix_ref, local_ref, gain_out_ref
):
    gain = gain_ref[...]
    total = jnp.zeros((1, DK), f32)
    quarter = DK // HEADS
    for h in range(HEADS):
        lanes = slice(h * DK, (h + 1) * DK)
        out = heads_ref[:, lanes]
        og = og_ref[:, lanes]
        gg = gg_ref[:, lanes]
        r = lax.rsqrt(jnp.mean(out * out, axis=-1, keepdims=True) + head_eps)
        u = out * r
        sig = sigmoid(og)
        w = og * sig
        ggw = gg * w
        g = ggw * gain
        total = total + jnp.sum(ggw * u, axis=0, keepdims=True)
        grad = r * (g - u * jnp.mean(g * u, axis=-1, keepdims=True))
        do_ref[:, lanes] = grad
        mix_ref[:, lanes] = (gg * gain * u * sig * (1.0 + og * (1.0 - sig))).astype(bf16)
        local = dot1(grad, p_ref[h], TN).astype(bf16)
        for j in range(HEADS):
            local_ref[HEADS * h + j] = local[j * quarter : (j + 1) * quarter]

    @pl.when(pl.program_id(0) == 0)
    def _():
        gain_out_ref[...] = jnp.zeros_like(gain_out_ref)

    gain_out_ref[0:1, :] += total


def conv_acts(ext_ref, weights, marks, lane):
    conv = conv_parts(ext_ref, weights, marks, lane)
    sig = sigmoid(conv)
    return conv, sig, conv * sig


def conv_pull(d_act, conv, sig, ext_ref, gext_ref, gtaps_ref, weights, marks, lane):
    d_conv = d_act * sig * (1.0 + conv * (1.0 - sig))
    for tap in range(TAPS):
        kept = d_conv * marks[:, tap : tap + 1] if tap < TAPS - 1 else d_conv
        place = (pl.ds(HALO - TAPS + 1 + tap, TOK), pl.ds(lane, DK))
        gtaps_ref[tap : tap + 1, lane : lane + DK] += jnp.sum(
            kept * ext_ref[place], axis=0, keepdims=True
        )
        gext_ref[place] += kept * weights[tap : tap + 1, lane : lane + DK]


def store_rows(gpre_ref, gext_ref):
    s = pl.program_id(0)
    gpre_ref[pl.ds(pl.multiple_of(s * TOK, TOK), TOK), :] = gext_ref[HALO:, :].astype(bf16)
    halo = pl.multiple_of(2 * TOK + s * HALO, HALO)
    gpre_ref[pl.ds(halo, HALO), :] = gext_ref[0:HALO, :].astype(bf16)


def unit_pull(d, hat, scale):
    return scale * (d - hat * jnp.sum(d * hat, axis=-1, keepdims=True))


def chunk_backward_early(
    pre_ref, rim_ref, scal_ref, rate_ref, taps_ref, marks_ref, docs_ref,
    uw_ref, s_ref, do_ref,
    gpre_ref, gtaps_ref, fresh_ref, recalled_ref, df_ref, dk_ref, dc_ref, ext_ref, gext_ref,
):
    inner = HEADS * DK
    ext_ref[0:HALO, :] = rim_ref[...].astype(f32)
    ext_ref[HALO:, :] = pre_ref[...].astype(f32)
    gext_ref[...] = jnp.zeros_like(gext_ref)

    @pl.when(pl.program_id(0) == 0)
    def _():
        gtaps_ref[...] = jnp.zeros_like(gtaps_ref)

    marks = marks_ref[0]
    weights = taps_ref[...]
    strength, total, total_t, causal, below = decays(
        scal_ref[...], rate_ref[...], marks, docs_ref[0]
    )
    rows, cols = iotas()
    reached = marks[:, 3:4]
    grad_c = jnp.zeros((TOK, TOK), f32)
    for h in range(HEADS):
        conv, sig, act = conv_acts(ext_ref, weights, marks, h * DK)
        act_k = conv_acts(ext_ref, weights, marks, inner + h * DK)[2]
        nq = unit_scale(act)
        q_hat = act * nq
        q, k = q_hat.astype(bf16), (act_k * unit_scale(act_k)).astype(bf16)
        c_col = total[:, HEADS + h : HEADS + h + 1]
        c_row = total_t[HEADS + h : HEADS + h + 1, :]
        decay = jnp.where(causal, jnp.exp(jnp.where(causal, c_col - c_row, 0.0)), 0.0)
        scores = dot1(q, k, NT) * decay
        start = jnp.exp(c_col) * reached
        state = s_ref[h]
        do = do_ref[:, h * DK : (h + 1) * DK].astype(bf16)
        fresh = uw_ref[h, :, :DK] - dot1(uw_ref[h, :, DK:], state, NT)
        fresh = fresh.astype(bf16)
        fresh_ref[h] = fresh
        recalled_ref[h] = dot1(k, state, NT)
        df_ref[h] = dot1(scores, do, TN)
        d_scores = dot1(do, fresh, NT)
        pull = d_scores * scores
        d_qk = (d_scores * decay).astype(bf16)
        dk_ref[h] = dot1(d_qk, q, TN)
        do_state = dot1(do, state)
        d_q = dot1(d_qk, k) + start * do_state
        d_start = jnp.sum(q.astype(f32) * do_state, axis=-1, keepdims=True)
        d_c = jnp.sum(pull - jnp.transpose(pull), axis=-1, keepdims=True) + d_start * start
        grad_c = jnp.where(cols == HEADS + h, d_c, grad_c)
        conv_pull(
            unit_pull(d_q, q_hat, nq), conv, sig, ext_ref, gext_ref, gtaps_ref, weights, marks,
            h * DK,
        )
    dc_ref[...] = grad_c
    store_rows(gpre_ref, gext_ref)


def chunk_backward_late(
    pre_ref, rim_ref, scal_ref, rate_ref, taps_ref, marks_ref, docs_ref,
    x_ref, s_ref, d_ref, fresh_ref, recalled_ref, df_ref, dk_ref, dc_ref,
    gpre_ref, gscal_ref, gtaps_ref, grate_ref, ext_ref, gext_ref,
):
    inner = HEADS * DK
    ext_ref[0:HALO, :] = rim_ref[:, inner:].astype(f32)
    ext_ref[HALO:, :] = pre_ref[:, inner:].astype(f32)
    gext_ref[...] = jnp.zeros_like(gext_ref)

    @pl.when(pl.program_id(0) == 0)
    def _():
        gtaps_ref[...] = jnp.zeros_like(gtaps_ref)
        grate_ref[...] = jnp.zeros_like(grate_ref)

    marks = marks_ref[0]
    weights = taps_ref[:, inner:]
    scal = scal_ref[...]
    rates = rate_ref[...]
    strength, total, total_t, causal, below = decays(scal, rates, marks, docs_ref[0])
    rows, cols = iotas()
    reached, tail = marks[:, 3:4], marks[:, 4:5]
    grad_b = jnp.zeros((TOK, TOK), f32)
    grad_c = jnp.zeros((TOK, TOK), f32)
    for h in range(HEADS):
        conv_k, sig_k, act_k = conv_acts(ext_ref, weights, marks, h * DK)
        conv_v, sig_v, act_v = conv_acts(ext_ref, weights, marks, inner + h * DK)
        nk = unit_scale(act_k)
        k_hat = act_k * nk
        k, v = k_hat.astype(bf16), act_v.astype(bf16)
        kf, vf = k.astype(f32), v.astype(f32)
        c_col = total[:, HEADS + h : HEADS + h + 1]
        c_row = total_t[HEADS + h : HEADS + h + 1, :]
        strict = causal & below
        strict_decay = jnp.where(strict, jnp.exp(jnp.where(strict, c_col - c_row, 0.0)), 0.0)
        b = strength[:, h : h + 1]
        gram_decay = dot1(k, k, NT) * strict_decay
        start = jnp.exp(c_col) * reached
        last = c_col[TOK - 1 : TOK, :]
        tail_decay = jnp.exp(last - c_col) * tail
        carry = jnp.exp(last) * reached[TOK - 1 : TOK, :]
        state, adj = s_ref[h], d_ref[h]
        fresh, recalled = fresh_ref[h], recalled_ref[h]
        d_fresh = df_ref[h] + dot1(kf * tail_decay, adj, NT)
        d_r = dot1(x_ref[h], d_fresh, TN)
        d_v = b * d_r
        d_b = jnp.sum(d_r * (vf - start * recalled), axis=-1, keepdims=True)
        d_start = -jnp.sum(d_v * recalled, axis=-1, keepdims=True)
        d_strict = -dot1(d_r, fresh, NT)
        strict_pull = d_strict * gram_decay
        d_b = d_b + jnp.sum(strict_pull, axis=-1, keepdims=True)
        d_gram = (d_strict * (b * strict_decay)).astype(bf16)
        d_k = dk_ref[h] - start * dot1(d_v, state) + dot1(d_gram, k) + dot1(d_gram, k, TN)
        fresh_adj = dot1(fresh, adj)
        d_k = d_k + tail_decay * fresh_adj
        d_tail = jnp.sum(kf * fresh_adj, axis=-1, keepdims=True) * tail_decay
        d_carry = jnp.sum(
            jnp.sum(adj.astype(f32) * state.astype(f32), axis=-1, keepdims=True),
            axis=0, keepdims=True,
        )
        pull = b * strict_pull
        d_c = jnp.sum(pull - jnp.transpose(pull), axis=-1, keepdims=True)
        d_c = d_c + d_start * start - d_tail
        d_last = d_carry * carry + jnp.sum(d_tail, axis=0, keepdims=True)
        d_c = d_c + jnp.where(rows[:, 0:1] == TOK - 1, d_last, 0.0)
        grad_b = jnp.where(cols == h, d_b, grad_b)
        grad_c = jnp.where(cols == HEADS + h, d_c, grad_c)
        conv_pull(
            unit_pull(d_k, k_hat, nk), conv_k, sig_k, ext_ref, gext_ref, gtaps_ref, weights,
            marks, h * DK,
        )
        conv_pull(
            d_v, conv_v, sig_v, ext_ref, gext_ref, gtaps_ref, weights, marks, inner + h * DK
        )
    upper = (cols >= rows).astype(bf16)
    grad_ld = dot2(upper, grad_c + dc_ref[...])
    decay_side = -grad_ld * rates * sigmoid(scal)
    gscal_ref[...] = jnp.where(
        cols < HEADS,
        grad_b * strength * (1.0 - strength),
        jnp.where(cols < 2 * HEADS, decay_side, 0.0),
    ).astype(bf16)
    grate_ref[0:1, :] += -jnp.sum(grad_ld * softplus(scal), axis=0, keepdims=True)
    store_rows(gpre_ref, gext_ref)


def row_grads(groups, lhs_count, rhs_count, *refs):
    out_ref = refs[-1]
    lhs = [refs[i][...] for i in range(lhs_count)]
    rhs = refs[lhs_count : lhs_count + rhs_count]
    lane = 0
    for group in groups:
        total = None
        for i, j in group:
            part = dot1(lhs[i][: rhs[j].shape[0]], rhs[j][...], TN)
            total = part if total is None else total + part
        out_ref[:, lane : lane + total.shape[1]] = total.astype(bf16)
        lane += total.shape[1]


def mixer_grads(
    offsets, place_ref, normed_ref, mixer_ref, og_ref, gq_ref, gkv_ref, gscal_ref, gated_ref, *outs
):
    width = normed_ref.shape[1]
    part = HEADS * DK // 2
    tokens = 2 * TOK

    def rows_x(ref, offset):
        place = lax.rem(place_ref[0] + offset, 4)
        return ref[:, pl.ds(pl.multiple_of(place * (width // 4), 128), width // 4)]

    def rows_z(ref, offset):
        place = lax.rem(place_ref[1] + offset, 4)
        cut = width // 16
        pieces = [
            ref[:, pl.ds(pl.multiple_of((j * 4 + place) * cut, 128), cut)] for j in range(4)
        ]
        return jnp.concatenate(pieces, axis=1)

    def store(outs, columns):
        lane = 0
        for column in columns:
            column = column.astype(bf16)
            lanes = slice(lane, lane + column.shape[1])
            rows = column.shape[0] // len(outs)
            for i, out in enumerate(outs):
                out[:, lanes] = column[i * rows : (i + 1) * rows]
            lane += column.shape[1]

    count = len(outs) // (2 * len(offsets))
    for i, offset in enumerate(offsets):
        normed = rows_x(normed_ref, offset)
        store(
            outs[i * count : (i + 1) * count],
            [
                dot1(normed[:tokens], og_ref[...], TN),
                dot1(normed, gq_ref[...], TN),
                dot1(normed[:tokens], gscal_ref[...], TN),
                dot1(normed, gkv_ref[:, :part], TN),
            ],
        )
        normed = rows_z(normed_ref, offset)
        i += len(offsets)
        store(
            outs[i * count : (i + 1) * count],
            [
                dot1(normed, gkv_ref[:, part:], TN),
                dot1(rows_z(mixer_ref, offset), gated_ref[...], TN),
            ],
        )


def input_grads(
    rim_ref, gq_ref, gkv_ref, gscal_ref, og_ref, left_ref, right_ref, out_ref, first_ref, second_ref
):
    inner = HEADS * DK
    part = inner // 2
    tokens = 2 * TOK

    @pl.when(pl.program_id(0) == 0)
    def _():
        first_ref[:, :inner] = gq_ref[:tokens, :]
        first_ref[:, inner : inner + 128] = gscal_ref[...]
        first_ref[:, inner + 128 : inner + 128 + part] = gkv_ref[:tokens, :part]
        first_ref[:, inner + 128 + part :] = og_ref[...]
        second_ref[...] = gkv_ref[:tokens, part:]
        for s in range(2):
            rows = slice((s + 1) * TOK - HALO, (s + 1) * TOK)
            rim = rim_ref[s * HALO : (s + 1) * HALO, :].astype(f32)

            def put(ref, lanes, came):
                ref[rows, lanes] = (ref[rows, lanes].astype(f32) + came).astype(bf16)

            put(first_ref, slice(0, inner), rim[:, :inner])
            put(
                first_ref,
                slice(inner + 128, inner + 128 + part),
                rim[:, inner : inner + part],
            )
            put(second_ref, slice(0, inner + part), rim[:, inner + part :])

    total = dot1(first_ref[...], left_ref[...], NT)
    total = total + dot1(second_ref[...], right_ref[:, : inner + part], NT)
    out_ref[...] = total.astype(bf16)


def ignoring(kernel, at, count):
    def inner_kernel(*refs):
        kernel(*refs[:at], *refs[at + count :])

    return inner_kernel


def dep_specs(deps):
    return [pl.BlockSpec(memory_space=pl.ANY) for _ in deps]


def cost(flops, moved):
    return pl.CostEstimate(flops=flops, bytes_accessed=moved, transcendentals=0)


def params():
    return pltpu.CompilerParams(vmem_limit_bytes=VMEM)


def whole(shape):
    return pl.BlockSpec(shape, lambda s: (0,) * len(shape))


def by_rows(rows, cols, base=0, lane=0):
    return pl.BlockSpec((rows, cols), lambda s: (base + s, lane))


def by_lead(*shape):
    return pl.BlockSpec(shape, lambda s: (s,) + (0,) * (len(shape) - 1))


def mixer_specs():
    wide = 3 * HEADS * DK
    return [
        by_rows(TOK, wide),
        by_rows(HALO, wide, 2 * TOK // HALO),
        by_rows(TOK, 128),
        whole((1, 128)),
        whole((TAPS, wide)),
        by_lead(1, TOK, 8),
        by_lead(1, 1, TOK),
    ]


def run_chunk_forward(pre, scal, rates, taps, marks, docs):
    quarter = DK // HEADS
    wide = 3 * HEADS * DK
    return pl.pallas_call(
        chunk_forward,
        grid=(2,),
        in_specs=mixer_specs(),
        out_specs=[
            by_lead(16, DK + quarter, DK),
            by_lead(HEADS, TOK, DK),
            by_lead(HEADS, TOK, DK),
            by_lead(HEADS, TOK, DK),
            by_lead(HEADS, TOK, 2 * DK),
        ],
        out_shape=[
            jax.ShapeDtypeStruct((SEQ, DK + quarter, DK), bf16),
            jax.ShapeDtypeStruct((8, TOK, DK), bf16),
            jax.ShapeDtypeStruct((8, TOK, DK), f32),
            jax.ShapeDtypeStruct((8, TOK, DK), bf16),
            jax.ShapeDtypeStruct((8, TOK, 2 * DK), f32),
        ],
        scratch_shapes=[pltpu.VMEM((HALO + TOK, wide), f32)],
        compiler_params=params(),
        cost_estimate=cost(10**10, 6 * 10**6),
    )(pre, pre, scal, rates, taps, marks, docs)


def run_scan_forward(got):
    return pl.pallas_call(
        scan_forward,
        out_shape=jax.ShapeDtypeStruct((SEQ, DK // HEADS, DK), bf16),
        compiler_params=params(),
        cost_estimate=cost(10**9, 3 * 10**6),
    )(got)


def run_scan_backward(got, local, deps):
    vmem = pl.BlockSpec(memory_space=pltpu.VMEM)
    return pl.pallas_call(
        ignoring(scan_backward, 2, len(deps)),
        in_specs=[vmem, vmem] + dep_specs(deps),
        out_specs=vmem,
        out_shape=jax.ShapeDtypeStruct((SEQ, DK // HEADS, DK), bf16),
        compiler_params=params(),
        cost_estimate=cost(10**9, 3 * 10**6),
    )(got, local, *deps)


def run_gate_forward(p, z, state, og, gain, deps):
    inner = HEADS * DK
    return pl.pallas_call(
        ignoring(gate_forward, 5, len(deps)),
        grid=(2,),
        in_specs=[
            by_lead(HEADS, TOK, DK),
            by_lead(HEADS, TOK, DK),
            by_lead(HEADS, DK, DK),
            by_rows(TOK, inner),
            whole((1, DK)),
        ]
        + dep_specs(deps),
        out_specs=[by_rows(TOK, inner), by_rows(TOK, inner)],
        out_shape=[
            jax.ShapeDtypeStruct((2 * TOK, inner), f32),
            jax.ShapeDtypeStruct((2 * TOK, inner), bf16),
        ],
        compiler_params=params(),
        cost_estimate=cost(10**9, 3 * 10**6),
    )(p, z, state, og, gain, *deps)


def run_gate_backward(gg, heads_out, og, gain, p):
    inner = HEADS * DK
    return pl.pallas_call(
        gate_backward,
        grid=(2,),
        in_specs=[
            by_rows(TOK, inner),
            by_rows(TOK, inner),
            by_rows(TOK, inner),
            whole((1, DK)),
            by_lead(HEADS, TOK, DK),
        ],
        out_specs=[
            by_rows(TOK, inner),
            by_rows(TOK, inner),
            by_lead(16, DK // HEADS, DK),
            whole((8, DK)),
        ],
        out_shape=[
            jax.ShapeDtypeStruct((2 * TOK, inner), f32),
            jax.ShapeDtypeStruct((2 * TOK, inner), bf16),
            jax.ShapeDtypeStruct((SEQ, DK // HEADS, DK), bf16),
            jax.ShapeDtypeStruct((8, DK), f32),
        ],
        compiler_params=params(),
        cost_estimate=cost(10**9, 3 * 10**6),
    )(gg, heads_out, og, gain, p)


def run_chunk_backward_early(pre, scal, rates, taps, marks, docs, uw, state, do, deps):
    inner = HEADS * DK
    wide = 3 * inner
    square = jax.ShapeDtypeStruct((8, TOK, DK), f32)
    return pl.pallas_call(
        ignoring(chunk_backward_early, 10, len(deps)),
        grid=(2,),
        in_specs=mixer_specs()
        + [
            by_lead(HEADS, TOK, 2 * DK),
            by_lead(HEADS, DK, DK),
            by_rows(TOK, inner),
        ]
        + dep_specs(deps),
        out_specs=[
            whole((2 * (TOK + HALO), inner)),
            whole((TAPS, inner)),
            by_lead(HEADS, TOK, DK),
            by_lead(HEADS, TOK, DK),
            by_lead(HEADS, TOK, DK),
            by_lead(HEADS, TOK, DK),
            by_rows(TOK, 128),
        ],
        out_shape=[
            jax.ShapeDtypeStruct((2 * (TOK + HALO), inner), bf16),
            jax.ShapeDtypeStruct((TAPS, inner), f32),
            jax.ShapeDtypeStruct((8, TOK, DK), bf16),
            square,
            square,
            square,
            jax.ShapeDtypeStruct((2 * TOK, 128), f32),
        ],
        scratch_shapes=[
            pltpu.VMEM((HALO + TOK, wide), f32),
            pltpu.VMEM((HALO + TOK, inner), f32),
        ],
        compiler_params=params(),
        cost_estimate=cost(5 * 10**9, 10**7),
    )(pre, pre, scal, rates, taps, marks, docs, uw, state, do, *deps)


def run_chunk_backward_late(
    pre, scal, rates, taps, marks, docs, x, state, adj, early, deps
):
    inner = HEADS * DK
    wide = 3 * inner
    return pl.pallas_call(
        ignoring(chunk_backward_late, 15, len(deps)),
        grid=(2,),
        in_specs=mixer_specs()
        + [
            by_lead(HEADS, TOK, DK),
            by_lead(HEADS, DK, DK),
            by_lead(HEADS, DK, DK),
            by_lead(HEADS, TOK, DK),
            by_lead(HEADS, TOK, DK),
            by_lead(HEADS, TOK, DK),
            by_lead(HEADS, TOK, DK),
            by_rows(TOK, 128),
        ]
        + dep_specs(deps),
        out_specs=[
            whole((2 * (TOK + HALO), 2 * inner)),
            by_rows(TOK, 128),
            whole((TAPS, 2 * inner)),
            whole((8, 128)),
        ],
        out_shape=[
            jax.ShapeDtypeStruct((2 * (TOK + HALO), 2 * inner), bf16),
            jax.ShapeDtypeStruct((2 * TOK, 128), bf16),
            jax.ShapeDtypeStruct((TAPS, 2 * inner), f32),
            jax.ShapeDtypeStruct((8, 128), f32),
        ],
        scratch_shapes=[
            pltpu.VMEM((HALO + TOK, 2 * inner), f32),
            pltpu.VMEM((HALO + TOK, 2 * inner), f32),
        ],
        compiler_params=params(),
        cost_estimate=cost(5 * 10**9, 10**7),
    )(pre, pre, scal, rates, taps, marks, docs, x, state, adj, *early, *deps)


def run_row_grads(lhs, rhs, groups, deps=()):
    width = lhs[0].shape[1]
    cols = sum(rhs[group[0][1]].shape[1] for group in groups)
    return pl.pallas_call(
        partial(row_grads, groups, len(lhs), len(rhs)),
        grid=(4,),
        in_specs=[pl.BlockSpec((m.shape[0], width // 4), lambda s: (0, s)) for m in lhs]
        + [whole(m.shape) for m in rhs]
        + dep_specs(deps),
        out_specs=pl.BlockSpec((width // 4, cols), lambda s: (s, 0)),
        out_shape=jax.ShapeDtypeStruct((width, cols), bf16),
        compiler_params=params(),
        cost_estimate=cost(2 * rhs[0].shape[0] * width * cols, 2 * width * cols),
    )(*lhs, *rhs, *deps)


def run_mixer_grads(offsets, halves, *arrays, deps=()):
    width = arrays[0].shape[1]
    inner = HEADS * DK
    vmem = pl.BlockSpec(memory_space=pltpu.VMEM)
    place = jnp.stack([place_of("x"), place_of("z")]).astype(jnp.int32)
    shapes = [
        (width // 4 // halves, cols)
        for cols in (2 * inner + inner // 2 + 128, 2 * inner + inner // 2)
        for _ in range(halves * len(offsets))
    ]
    return pl.pallas_call(
        ignoring(partial(mixer_grads, offsets), 8, len(deps)),
        in_specs=[pl.BlockSpec(memory_space=pltpu.SMEM)] + [vmem] * 7 + dep_specs(deps),
        out_specs=[vmem] * len(shapes),
        out_shape=[jax.ShapeDtypeStruct(shape, bf16) for shape in shapes],
        compiler_params=params(),
        cost_estimate=cost(2 * 256 * width * 5 * inner, 2 * width * 5 * inner),
    )(place, *arrays, *deps)


def run_input_grads(rim, gq, gkv, gscal, og, left, right, deps):
    inner = HEADS * DK
    width = left.shape[0]
    tokens = 2 * TOK
    cut = width // 4
    return pl.pallas_call(
        ignoring(input_grads, 7, len(deps)),
        grid=(4,),
        in_specs=[whole(m.shape) for m in (rim, gq, gkv, gscal, og)]
        + [
            by_rows(cut, left.shape[1]),
            by_rows(cut, right.shape[1]),
        ]
        + dep_specs(deps),
        out_specs=pl.BlockSpec((tokens, cut), lambda s: (0, s)),
        out_shape=jax.ShapeDtypeStruct((tokens, width), bf16),
        scratch_shapes=[
            pltpu.VMEM((tokens, left.shape[1]), bf16),
            pltpu.VMEM((tokens, inner + inner // 2), bf16),
        ],
        compiler_params=params(),
        cost_estimate=cost(2 * tokens * width * 5 * inner, 2 * width * 5 * inner),
    )(rim, gq, gkv, gscal, og, left, right, *deps)


SEQ_AXES = ("x", "z", "y")
GROUP_AXES = ("y", "head")


def passed_along(array, by):
    pairs = [(i, i + by) for i in range(SEQ) if 0 <= i + by < SEQ]
    return lax.ppermute(array, SEQ_AXES, pairs)


def along(array, axis, by):
    count = lax.axis_size(axis)
    return lax.ppermute(array, axis, [(i, (i + by) % count) for i in range(count)])


def place_of(axis):
    return lax.axis_index(axis)


def flipped(array, axes, mask):
    count = lax.axis_size(axes)
    return lax.ppermute(array, axes, [(i, i ^ mask) for i in range(count)])


def pick(array, index, dim):
    return lax.dynamic_index_in_dim(array, index, dim, keepdims=False)


def ordered(mine, other, place, axis=0):
    first = place == 0
    return jnp.concatenate(
        [jnp.where(first, mine, other), jnp.where(first, other, mine)], axis=axis
    )


def later(array, *deps):
    for dep in deps:
        first = lax.slice(dep, (0,) * dep.ndim, (1,) * dep.ndim).reshape(())
        array = array + (first * 0).astype(array.dtype)
    return array


def gather_last(first, second):
    near, far, halfway = near_and_far(first, second, ("z", "x"))
    outs = []
    for i, (array, axis, dim) in enumerate(((first, "z", 1), (second, "x", 0))):
        place = place_of(axis)
        shape = list(array.shape)
        shape.insert(dim, 4)
        out = jnp.zeros(shape, array.dtype)
        block = jnp.concatenate(far[2 * i : 2 * i + 2], axis=0)
        for offset, block in ((0, array), (-1, near[2 * i]), (-2, block), (1, near[2 * i + 1])):
            out = lax.dynamic_update_index_in_dim(out, block, (place + offset) % 4, dim)
        outs.append(out.reshape(-1, array.shape[-1]))
    return outs[0], outs[1], halfway


def exchange(array, axis):
    return lax.all_to_all(array, axis, split_axis=0, concat_axis=0, tiled=True)


def head_place():
    index = lax.axis_index("head")
    return index // 2, index % 2


def core_scatter(partial_rows):
    core = head_place()[1]
    rows = partial_rows.shape[0] // HEADS
    blocks = partial_rows.astype(bf16).reshape(2, 2, rows, -1)
    got = flipped(pick(blocks, 1 - core, 1), "head", 1)
    return pick(blocks, core, 1).astype(f32) + got.astype(f32), got


def chip_scatter(both, *gates):
    chip = head_place()[0]
    got = flipped(later(pick(both, 1 - chip, 0), *gates).astype(bf16), "head", 2)
    return pick(both, chip, 0) + got.astype(f32)


def head_gather(rows):
    chip, core = head_place()
    chip_got = flipped(rows, "head", 2)
    first = chip == 0
    chips = [jnp.where(first, rows, chip_got), jnp.where(first, chip_got, rows)]
    chips = jnp.stack(chips)
    got = flipped(chips, "head", 1)
    first = core == 0
    cores = [jnp.where(first, chips, got), jnp.where(first, got, chips)]
    return jnp.stack(cores, axis=1).reshape(HEADS * rows.shape[0], -1), chip_got


def group_scatter(partial_rows):
    chip, core = head_place()
    place = place_of("y") * 2 + chip
    blocks = partial_rows.astype(bf16).reshape(4, 2, -1, partial_rows.shape[1])
    got = flipped(pick(blocks, 1 - core, 1), GROUP_AXES, 1)
    both = pick(blocks, core, 1).astype(f32) + got.astype(f32)
    total = pick(both, place, 0)
    for mask in (2, 1, 3):
        part = pick(both, jnp.bitwise_xor(place, mask), 0).astype(bf16)
        total = total + flipped(part, GROUP_AXES, 2 * mask).astype(f32)
    return total, got


def group_gather(rows):
    chip, core = head_place()
    place = place_of("y") * 2 + chip
    out = jnp.zeros((4,) + rows.shape, rows.dtype)
    for mask in (2, 1, 3, 0):
        got = flipped(rows, GROUP_AXES, 2 * mask) if mask else rows
        out = lax.dynamic_update_index_in_dim(out, got, jnp.bitwise_xor(place, mask), 0)
    got = flipped(out, GROUP_AXES, 1)
    first = core == 0
    cores = [jnp.where(first, out, got), jnp.where(first, got, out)]
    return jnp.stack(cores, axis=1).reshape(8 * rows.shape[0], -1)


def in_vmem(kernel, shapes, place, *arrays, deps=()):
    vmem = pl.BlockSpec(memory_space=pltpu.VMEM)
    moved = sum(2 * a.size for a in arrays)
    return pl.pallas_call(
        ignoring(kernel, 1 + len(arrays), len(deps)),
        in_specs=[pl.BlockSpec(memory_space=pltpu.SMEM)] + [vmem] * len(arrays) + dep_specs(deps),
        out_specs=[vmem] * len(shapes),
        out_shape=[jax.ShapeDtypeStruct(shape, kind) for shape, kind in shapes],
        compiler_params=params(),
        cost_estimate=cost(moved, moved),
    )(place, *arrays, *deps)


def add_far(place_ref, *refs):
    for i in range(2):
        right, left, ahead, behind = refs[4 * i : 4 * i + 4]
        right_out, left_out = refs[8 + 2 * i : 10 + 2 * i]
        half = ahead.shape[0]
        total = right[:half].astype(f32) + ahead[...].astype(f32)
        right_out[:half] = total.astype(bf16)
        right_out[half:] = right[half:]
        left_out[:half] = left[:half]
        total = left[half:].astype(f32) + behind[...].astype(f32)
        left_out[half:] = total.astype(bf16)


def add_and_cut(place_ref, *refs):
    for i in range(2):
        members = refs[3 * i : 3 * i + 3]
        outs = refs[6 + 4 * i : 10 + 4 * i]
        rows = members[0].shape[0] // 4
        for out, by in zip(outs, (0, 2, 1, 3)):
            start = pl.multiple_of(lax.rem(place_ref[1 - i] + by, 4) * rows, rows)
            total = members[0][pl.ds(start, rows), :].astype(f32)
            for member in members[1:]:
                total = total + member[pl.ds(start, rows), :].astype(f32)
            out[...] = total.astype(bf16)


def add_and_halve(place_ref, *refs):
    kept, sent = refs[8:]
    rows = kept.shape[0]
    lane = 0
    for i in range(2):
        parts = refs[4 * i : 4 * i + 4]
        lanes = slice(lane, lane + parts[0].shape[1])
        lane += parts[0].shape[1]
        for out, at in ((kept, place_ref[2]), (sent, 1 - place_ref[2])):
            start = pl.multiple_of(at * rows, rows)
            total = parts[0][pl.ds(start, rows), :].astype(f32)
            for part in parts[1:]:
                total = total + part[pl.ds(start, rows), :].astype(f32)
            out[:, lanes] = total.astype(out.dtype)


def places():
    return jnp.stack([place_of(axis) for axis in SEQ_AXES]).astype(jnp.int32)


def reduce_near(owns, arrays, deps):
    shapes = [(arrays[i].shape, bf16) for i in (0, 1, 4, 5)]
    sums = in_vmem(add_far, shapes, places(), *arrays, deps=deps)
    gate = sums[0]
    arrays = []
    for i, axis in enumerate(("x", "z")):
        arrays += [owns[i], along(sums[2 * i], axis, 1), along(sums[2 * i + 1], axis, -1)]
    return arrays, gate


def reduce_cross(arrays, deps):
    shapes = []
    for own in (arrays[0], arrays[3]):
        shapes += [((own.shape[0] // 4, own.shape[1]), bf16)] * 4
    cut = in_vmem(add_and_cut, shapes, places(), *arrays, deps=deps)
    arrays = []
    for i, axis in enumerate(("z", "x")):
        own, two, one, three = cut[4 * i : 4 * i + 4]
        arrays += [own, along(two, axis, 2), along(one, axis, 1), along(three, axis, -1)]
    return arrays, cut[0]


def reduce_end(arrays, deps):
    rows, cols = arrays[0].shape[0] // 2, arrays[0].shape[1] + arrays[4].shape[1]
    shapes = [((rows, cols), f32), ((rows, cols), bf16)]
    kept, sent = in_vmem(add_and_halve, shapes, places(), *arrays, deps=deps)
    return kept + along(sent, "y", 1).astype(f32)


def pair_up(place_ref, left, left_other, right, right_other, left_out, right_out):
    rows = left.shape[0]
    mine = pl.multiple_of(place_ref[2] * rows, rows)
    other = pl.multiple_of((1 - place_ref[2]) * rows, rows)
    left_out[pl.ds(mine, rows), :] = left[...]
    left_out[pl.ds(other, rows), :] = left_other[...]
    right_out[pl.ds(mine, rows), :] = right[...]
    right_out[pl.ds(other, rows), :] = right_other[...]


def pass_on(place_ref, *refs):
    for i in range(2):
        half = refs[4 + 2 * i].shape[0]
        refs[4 + 2 * i][...] = refs[2 * i][:half]
        refs[5 + 2 * i][...] = refs[2 * i + 1][half:]


def put_in_place(axes, place_ref, *refs):
    for i in range(2):
        out = refs[10 + i]
        own, left, right, far_a, far_b = refs[5 * i : 5 * i + 5]
        place = place_ref[axes[i]]
        half = far_a.shape[0]
        out[place] = own[...]
        out[lax.rem(place + 3, 4)] = left[...]
        out[lax.rem(place + 1, 4)] = right[...]
        out[lax.rem(place + 2, 4), :half] = far_a[...]
        out[lax.rem(place + 2, 4), half:] = far_b[...]


def near_and_far(first, second, axes):
    near = []
    for array, axis in ((first, axes[0]), (second, axes[1])):
        near += [along(array, axis, 1), along(array, axis, -1)]
    shapes = []
    for array in (first, second):
        shapes += [((array.shape[0] // 2,) + array.shape[1:], bf16)] * 2
    halves = in_vmem(pass_on, shapes, places(), *near)
    far = []
    for i in range(2):
        far += [along(halves[2 * i], axes[i], 1), along(halves[2 * i + 1], axes[i], -1)]
    return near, far, halves[0]


def sum_along(array, axis):
    total = array
    for by in range(1, lax.axis_size(axis)):
        total = total + along(array, axis, by)
    return total


def mm(a, b, dims="ij,jk->ik"):
    return jnp.einsum(dims, a, b, preferred_element_type=f32)


def row_scale(x):
    return lax.rsqrt(jnp.mean(x * x, axis=-1, keepdims=True) + norm_eps)


def norm_pull(x, scale, gain, grad):
    unit = x * scale
    scaled = grad * gain
    return scale * (scaled - unit * jnp.mean(scaled * unit, axis=-1, keepdims=True))


def doc_tables(doc_lengths):
    first = lax.axis_index(SEQ_AXES) * TOK - (TAPS - 1)
    ends = jnp.cumsum(doc_lengths, axis=1)
    places = first + jnp.arange(TOK + TAPS - 1, dtype=jnp.int32)
    counted = jnp.sum((places[None, :, None] >= ends[:, None, :]).astype(jnp.int32), axis=2)
    ext = jnp.where(places[None, :] >= 0, counted, -1)
    local = ext[:, TAPS - 1 :]
    columns = [(ext[:, o : o + TOK] == local) for o in range(TAPS - 1)]
    columns.append(local == ext[:, TAPS - 2 : TAPS - 1])
    columns.append(local == local[:, -1:])
    columns.append(local)
    columns += [jnp.zeros_like(local)] * 2
    marks = jnp.stack([c.astype(f32) for c in columns], axis=-1)
    return marks, local.astype(f32)[:, None, :]


def body(
    inputs, doc_lengths, norm_in, query_weight, key_weight, value_weight, outgate_weight,
    scalar_weight, conv_kernel, decay_rate, head_norm, output_weight, norm_ffn, gate_weight,
    up_weight, down_weight, grad_out,
):
    width = inputs.shape[2]
    inner = HEADS * DK
    hidden = gate_weight.shape[1]
    head_index = lax.axis_index("head")
    quarter = 2 * TOK // HEADS

    gains = jnp.stack([norm_in, norm_ffn], axis=1)
    misc = jnp.concatenate([scalar_weight.reshape(-1, 2 * HEADS), gains], axis=1)
    misc = jnp.pad(misc, ((0, 0), (0, 128 - misc.shape[1])))
    part = inner // 2
    left = jnp.concatenate([query_weight, misc, key_weight[:, :part], outgate_weight], axis=1)
    right = jnp.concatenate([key_weight[:, part:], value_weight, output_weight.T], axis=1)
    y_place = place_of("y")
    rows = left.shape[0]
    left, right = in_vmem(
        pair_up,
        [((2 * rows, left.shape[1]), bf16), ((2 * rows, right.shape[1]), bf16)],
        places(),
        left, along(left, "y", 1), right, along(right, "y", 1),
    )
    near, far, _ = near_and_far(left, right, ("x", "z"))
    left, right = in_vmem(
        partial(put_in_place, (0, 1)),
        [((4, 2 * rows, part.shape[1]), bf16) for part in (left, right)],
        places(),
        left, *near[:2], *far[:2], right, *near[2:], *far[2:],
    )
    all_left, all_right, halfway = gather_last(left, right)
    w_gate, w_out_t = all_left[:, -inner:], all_right[:, -inner:]
    w_left, w_right = all_left[:, :-inner], all_right[:, :-inner]
    gains = w_left[:, inner : inner + 128].T[2 * HEADS : 2 * HEADS + 2].astype(f32)
    gain_in, gain_ffn = gains[0:1], gains[1:2]

    units = hidden // 2
    span = -(-units // 128) * 128

    def in_halves(weight):
        halves = weight.reshape(weight.shape[0], 2, units)
        return jnp.pad(halves, ((0, 0), (0, 0), (0, span - units)))

    packed = jnp.concatenate(
        [in_halves(gate_weight), in_halves(up_weight), in_halves(down_weight.T)], axis=2
    )
    other = along(later(pick(packed, 1 - y_place, 1), left), "y", 1)
    packed = later(ordered(pick(packed, y_place, 1), other, y_place), halfway)
    w_ffn = lax.all_gather(packed, ("x", "z"), axis=0, tiled=True)
    w_gateup = w_ffn[:, : 2 * span]
    w_down_t = w_ffn[:, 2 * span :]

    marks, docs_row = doc_tables(doc_lengths)
    taps = jnp.transpose(conv_kernel.astype(f32), (1, 0, 2)).reshape(TAPS, 3 * inner)
    rates = jnp.zeros((1, 128), f32)
    rates = rates.at[0, HEADS : 2 * HEADS].set(decay_rate.astype(f32))
    gain_head = head_norm.astype(f32).reshape(1, DK)

    halo = passed_along(inputs[:, TOK - HALO :], 1)
    tokens = inputs.reshape(2 * TOK, width)
    all_rows = jnp.concatenate([tokens, halo.reshape(2 * HALO, width)], axis=0).astype(f32)
    scale_in = row_scale(all_rows)
    normed_all = (all_rows * scale_in * gain_in).astype(bf16)
    normed_in = normed_all[: 2 * TOK]

    left = mm(normed_all, w_left)
    right = mm(normed_all, w_right)
    pre = jnp.concatenate(
        [left[:, :inner].astype(bf16), left[:, inner + 128 :].astype(bf16), right.astype(bf16)],
        axis=1,
    )
    scal = left[: 2 * TOK, inner : inner + 128]

    grad_rows = grad_out.reshape(2 * TOK, width)
    grad_other = along(grad_rows, "y", 1)
    send, p, z, x, uw = run_chunk_forward(pre, scal, rates, taps, marks, docs_row)
    out_gate = mm(normed_in, w_gate)
    got = exchange(send, SEQ_AXES)
    state = exchange(run_scan_forward(got), SEQ_AXES).reshape(8, DK, DK)
    heads_out, gated_rows = run_gate_forward(
        p, z, state, out_gate, gain_head, (grad_other,)
    )

    mine = partial(lax.dynamic_slice_in_dim, start_index=head_index * quarter, slice_size=quarter)
    residual = mine(tokens).astype(f32) + chip_scatter(
        core_scatter(mm(gated_rows, w_out_t, "ij,kj->ik"))[0]
    )
    scale_ffn = row_scale(residual)
    normed_ffn = group_gather((residual * scale_ffn * gain_ffn).astype(bf16))

    group_grads = ordered(grad_rows, grad_other, y_place)
    grad_act = mm(group_grads, w_down_t)
    gate_up = mm(normed_ffn, w_gateup)
    gate, up = gate_up[:, :span], gate_up[:, span:]
    sig = sigmoid(gate)
    silu = gate * sig
    product = (silu * up).astype(bf16)
    gu_grad = jnp.concatenate(
        [
            (grad_act * up * sig * (1.0 + gate * (1.0 - sig))).astype(bf16),
            (grad_act * silu).astype(bf16),
        ],
        axis=1,
    )
    ffn_part = mm(gu_grad, w_gateup, "ij,kj->ik").astype(bf16)
    grad_normed = group_scatter(ffn_part)[0]
    back = norm_pull(residual, scale_ffn, gain_ffn, grad_normed)
    grad_residual = mine(grad_rows).astype(f32) + back
    grad_mixer = head_gather(grad_residual.astype(bf16))[0]

    grad_gated = mm(grad_mixer, w_out_t)
    do, gate_grad_mix, local, part_gain_head = run_gate_backward(
        grad_gated, heads_out, out_gate, gain_head, p
    )
    local_got = exchange(local, SEQ_AXES)
    early = run_chunk_backward_early(
        pre, scal, rates, taps, marks, docs_row, uw, state, do, ()
    )
    gq, gtaps_q = early[:2]
    ffn_all = run_row_grads(
        [normed_ffn, group_grads], [gu_grad, product], (((0, 0),), ((1, 1),)), (local,)
    )
    ffn = lax.psum_scatter(ffn_all, ("x", "z"), scatter_dimension=0, tiled=True)
    adj_out = run_scan_backward(got, local_got, (gq,))
    ffn_out, ffn_got = group_scatter(mm(later(product, local), w_down_t, "ij,kj->ik"))
    adj = exchange(adj_out, SEQ_AXES).reshape(8, DK, DK)
    gkv, gscal, gtaps_kv, grate = run_chunk_backward_late(
        pre, scal, rates, taps, marks, docs_row, x, state, adj, early[2:], (ffn_got,)
    )

    arrays = (normed_all, grad_mixer, gate_grad_mix, gq, gkv, gscal, gated_rows)
    far = run_mixer_grads((2,), 2, *arrays)
    blocks = run_mixer_grads((1, 3, 0), 1, *arrays, deps=(far[0], ffn_out))
    owns, partials = (blocks[2], blocks[5]), []
    for i, axis in enumerate(("x", "z")):
        partials += blocks[3 * i : 3 * i + 2]
        partials += [along(far[2 * i], axis, 1), along(far[2 * i + 1], axis, -1)]

    gtaps = jnp.concatenate([gtaps_q, gtaps_kv], axis=1).reshape(12, inner)
    tail = jnp.concatenate([part_gain_head[:1], grate[:1]], axis=1)
    tail = jnp.pad(tail, ((0, 3), (0, inner - tail.shape[1])))
    small = jnp.concatenate([gtaps, tail], axis=0)
    rim = jnp.concatenate([gq[2 * TOK :], gkv[2 * TOK :]], axis=1)
    rim = passed_along(rim, -1)
    input_sent = run_input_grads(
        rim, gq, gkv, gscal, gate_grad_mix, all_left, all_right, (blocks[0],)
    )
    partials, near_gate = reduce_near(owns, partials, (input_sent,))
    ffn = ffn.reshape(2, -1, 3, span)[..., :units]
    ffn_other = along(later(pick(ffn, 1 - y_place, 0), near_gate), "y", 1)
    ffn = ordered(pick(ffn, y_place, 0), ffn_other, y_place, 2).astype(f32)
    by_core = core_scatter(later(input_sent, near_gate))[0]
    grad_normed_in = chip_scatter(by_core)
    own = mine(tokens).astype(f32)
    back_in = norm_pull(own, row_scale(own), gain_in, grad_normed_in)
    both = jnp.concatenate([residual + ffn_out, grad_residual + back_in], axis=1)
    both = both.astype(bf16)
    small = sum_along(later(small, ffn_other), "x")
    partials, cross_gate = reduce_cross(partials, (both, ffn_other, small))
    mixer_w = reduce_end(partials, ())
    both, chip_got = head_gather(later(both, cross_gate))
    small = sum_along(sum_along(later(small, chip_got), "z"), "y")
    outputs, grad_in = both[:, :width], both[:, width:].astype(f32)

    rows = width // SEQ
    key_at = 2 * inner + 128
    grad_conv = jnp.transpose(small[:12].reshape(TAPS, 3, inner), (1, 0, 2))

    def gain_grad(gain, weights, grads):
        total = 0.0
        for weight, grad in zip(weights, grads):
            total = total + jnp.sum(weight.astype(f32) * grad, axis=1)
        return total / gain.astype(f32)

    grad_scalar = mixer_w[:, 2 * inner : 2 * inner + 2 * HEADS]
    gain_parts = jnp.concatenate(
        [
            gain_grad(
                norm_in,
                (outgate_weight, query_weight, scalar_weight.reshape(rows, -1), key_weight, value_weight),
                (
                    mixer_w[:, :inner],
                    mixer_w[:, inner : 2 * inner],
                    grad_scalar,
                    mixer_w[:, key_at : key_at + inner],
                    mixer_w[:, key_at + inner : key_at + 2 * inner],
                ),
            ),
            gain_grad(norm_ffn, (gate_weight, up_weight), (ffn[:, 0], ffn[:, 1])),
            small[12, :DK],
        ]
    )
    shared = sum_along(gain_parts[None], "head")[0]
    return (
        outputs.reshape(inputs.shape),
        grad_in.reshape(inputs.shape),
        shared[:rows],
        mixer_w[:, inner : 2 * inner],
        mixer_w[:, key_at : key_at + inner],
        mixer_w[:, key_at + inner : key_at + 2 * inner],
        mixer_w[:, :inner],
        grad_scalar.reshape(rows, 2, HEADS),
        grad_conv,
        small[12, DK + HEADS : DK + 2 * HEADS],
        shared[2 * rows :],
        mixer_w[:, key_at + 2 * inner :].T,
        shared[rows : 2 * rows],
        ffn[:, 0],
        ffn[:, 1],
        ffn[:, 2].T,
    )


def solution(mesh):
    mesh = Mesh(mesh.devices.reshape(4, 4, 2, HEADS), ("x", "z", "y", "head"))
    seq = SEQ_AXES
    weight = P(seq, "head")
    weight_t = P("head", seq)
    tokens = P(None, seq, None)
    scalars = P(seq, None, "head")
    taps = P(None, None, "head")
    return jax.shard_map(
        body,
        mesh=mesh,
        in_specs=(
            tokens, P(), P(seq), weight, weight, weight, weight, scalars, taps, P("head"), P(),
            weight_t, P(seq), weight, weight, weight_t, tokens,
        ),
        out_specs=(
            tokens, tokens, P(seq), weight, weight, weight, weight, scalars, taps, P("head"),
            P(), weight_t, P(seq), weight, weight, weight_t,
        ),
        check_vma=False,
    )
```

```python
from functools import partial

import jax
import jax.numpy as jnp
from jax import lax
from jax.experimental import pallas as pl
from jax.experimental.pallas import tpu as pltpu
from jax.sharding import Mesh
from jax.sharding import PartitionSpec as P

f32 = jnp.float32
bf16 = jnp.bfloat16
norm_eps = 1e-06
head_eps = 1e-05
SEQ = 32
HEADS = 4
DK = 128
TOK = 128
TAPS = 4
HALO = 16
VMEM = 56 * 1024 * 1024

NN = (((1,), (0,)), ((), ()))
NT = (((1,), (1,)), ((), ()))
TN = (((0,), (0,)), ((), ()))


def dot1(a, b, dims=NN):
    return lax.dot_general(a.astype(bf16), b.astype(bf16), dims, preferred_element_type=f32)


def split(a):
    high = a.astype(bf16)
    return high, (a - high.astype(f32)).astype(bf16)


def dot3(a, b, dims=NN):
    ah, al = split(a)
    bh, bl = split(b)
    return dot1(ah, bh, dims) + (dot1(ah, bl, dims) + dot1(al, bh, dims))


def dot2(exact, b, dims=NN):
    high = b.astype(bf16)
    rest = b - high.astype(f32)
    mid = rest.astype(bf16)
    low = (rest - mid.astype(f32)).astype(bf16)
    return dot1(exact, high, dims) + (dot1(exact, mid, dims) + dot1(exact, low, dims))


def sigmoid(x):
    return 1.0 / (1.0 + jnp.exp(-x))


def softplus(x):
    return jnp.maximum(x, 0.0) + jnp.log1p(jnp.exp(-jnp.abs(x)))


def iotas():
    rows = lax.broadcasted_iota(jnp.int32, (TOK, TOK), 0)
    cols = lax.broadcasted_iota(jnp.int32, (TOK, TOK), 1)
    return rows, cols


def unit_inverses(stricts):
    rows, cols = iotas()
    eye = (rows == cols).astype(f32)
    apart = jnp.bitwise_xor(rows, cols)
    results = []
    first = (apart == 1) & (rows > cols)
    results = [eye - jnp.where(first, a, 0.0) for a in stricts]
    size = 2
    while size < TOK:
        corner = (apart >= size) & (apart < 2 * size) & (rows > cols)
        parts = [dot3(jnp.where(corner, a, 0.0), x) for a, x in zip(stricts, results)]
        results = [x - dot3(x, c) for x, c in zip(results, parts)]
        size *= 2
    return results


def decays(scal, rates, marks, docs_row):
    rows, cols = iotas()
    strength = sigmoid(scal)
    log_decay = -rates * softplus(scal)
    lower = (rows >= cols).astype(bf16)
    total = dot2(lower, log_decay)
    total_t = jnp.transpose(total)
    same = marks[:, 5:6] == docs_row
    causal = same & (rows >= cols)
    return strength, total, total_t, causal, rows > cols


def conv_parts(ext_ref, weights, marks, lane):
    out = None
    for tap in range(TAPS):
        piece = ext_ref[pl.ds(HALO - TAPS + 1 + tap, TOK), pl.ds(lane, DK)]
        if tap < TAPS - 1:
            piece = piece * marks[:, tap : tap + 1]
        piece = piece * weights[tap : tap + 1, lane : lane + DK]
        out = piece if out is None else out + piece
    return out


def unit_scale(x):
    return lax.rsqrt(jnp.sum(x * x, axis=-1, keepdims=True) + norm_eps)


def chunk_forward(
    pre_ref, rim_ref, scal_ref, rate_ref, taps_ref, marks_ref, docs_ref,
    send_ref, p_ref, z_ref, x_ref, uw_ref, ext_ref,
):
    inner = HEADS * DK
    ext_ref[0:HALO, :] = rim_ref[...].astype(f32)
    ext_ref[HALO:, :] = pre_ref[...].astype(f32)
    marks = marks_ref[0]
    weights = taps_ref[...]
    strength, total, total_t, causal, below = decays(
        scal_ref[...], rate_ref[...], marks, docs_ref[0]
    )
    rows, cols = iotas()
    reached, tail = marks[:, 3:4], marks[:, 4:5]
    heads = []
    for h in range(HEADS):
        acts = []
        for c in range(3):
            conv = conv_parts(ext_ref, weights, marks, c * inner + h * DK)
            acts.append(conv * sigmoid(conv))
        q = (acts[0] * unit_scale(acts[0])).astype(bf16)
        k = (acts[1] * unit_scale(acts[1])).astype(bf16)
        v = acts[2].astype(bf16)
        c_col = total[:, HEADS + h : HEADS + h + 1]
        c_row = total_t[HEADS + h : HEADS + h + 1, :]
        decay = jnp.where(causal, jnp.exp(jnp.where(causal, c_col - c_row, 0.0)), 0.0)
        b = strength[:, h : h + 1]
        gram = dot1(k, k, NT)
        strict = jnp.where(below, b * gram * decay, 0.0)
        heads.append((q, k, v, c_col, decay, b, strict))
    inverses = unit_inverses([head[6] for head in heads])
    for h in range(HEADS):
        q, k, v, c_col, decay, b, strict = heads[h]
        x = inverses[h]
        start = jnp.exp(c_col) * reached
        kf = k.astype(f32)
        uw = dot3(x, jnp.concatenate([b * v.astype(f32), (b * start) * kf], axis=1))
        scores = dot1(q, k, NT) * decay
        suw = dot3(scores, uw)
        last = c_col[TOK - 1 : TOK, :]
        tail_k = kf * (jnp.exp(last - c_col) * tail)
        carry = jnp.exp(last) * reached[TOK - 1 : TOK, :]
        u, w = uw[:, :DK], uw[:, DK:]
        move = jnp.where(rows == cols, carry, 0.0) - dot3(tail_k, w, TN)
        offset_t = dot3(u, tail_k, TN)
        p_ref[h] = (q.astype(f32) * start - suw[:, DK:]).astype(bf16)
        z_ref[h] = suw[:, :DK]
        x_ref[h] = x.astype(bf16)
        uw_ref[h] = uw
        quarter = DK // HEADS
        for j in range(HEADS):
            send_ref[HEADS * h + j, 0:DK, :] = move.astype(bf16)
            send_ref[HEADS * h + j, DK : DK + quarter, :] = offset_t[
                j * quarter : (j + 1) * quarter
            ].astype(bf16)


def scan_forward(got_ref, out_ref):
    state = jnp.zeros((DK // HEADS, DK), f32)
    for i in range(SEQ):
        out_ref[i] = state.astype(bf16)
        if i + 1 < SEQ:
            high, low = split(state)
            both = dot1(jnp.concatenate([high, low], axis=0), got_ref[i, 0:DK, :], NT)
            half = DK // HEADS
            state = both[:half] + both[half:] + got_ref[i, DK : DK + half, :].astype(f32)


def scan_backward(got_ref, local_ref, out_ref):
    state = jnp.zeros((DK // HEADS, DK), f32)
    for i in range(SEQ - 1, -1, -1):
        out_ref[i] = state.astype(bf16)
        if i > 0:
            high, low = split(state)
            both = dot1(jnp.concatenate([high, low], axis=0), got_ref[i, 0:DK, :])
            half = DK // HEADS
            state = both[:half] + both[half:] + local_ref[i].astype(f32)


def gate_forward(p_ref, z_ref, s_ref, og_ref, gain_ref, heads_ref, gated_ref):
    gain = gain_ref[...]
    for h in range(HEADS):
        lanes = slice(h * DK, (h + 1) * DK)
        out = dot1(p_ref[h], s_ref[h], NT) + z_ref[h]
        heads_ref[:, lanes] = out
        r = lax.rsqrt(jnp.mean(out * out, axis=-1, keepdims=True) + head_eps)
        og = og_ref[:, lanes]
        gated_ref[:, lanes] = (out * r * gain * (og * sigmoid(og))).astype(bf16)


def gate_backward(
    gg_ref, heads_ref, og_ref, gain_ref, p_ref, do_ref, mix_ref, local_ref, gain_out_ref
):
    gain = gain_ref[...]
    total = jnp.zeros((1, DK), f32)
    quarter = DK // HEADS
    for h in range(HEADS):
        lanes = slice(h * DK, (h + 1) * DK)
        out = heads_ref[:, lanes]
        og = og_ref[:, lanes]
        gg = gg_ref[:, lanes]
        r = lax.rsqrt(jnp.mean(out * out, axis=-1, keepdims=True) + head_eps)
        u = out * r
        sig = sigmoid(og)
        w = og * sig
        ggw = gg * w
        g = ggw * gain
        total = total + jnp.sum(ggw * u, axis=0, keepdims=True)
        grad = r * (g - u * jnp.mean(g * u, axis=-1, keepdims=True))
        do_ref[:, lanes] = grad
        mix_ref[:, lanes] = (gg * gain * u * sig * (1.0 + og * (1.0 - sig))).astype(bf16)
        local = dot1(grad, p_ref[h], TN).astype(bf16)
        for j in range(HEADS):
            local_ref[HEADS * h + j] = local[j * quarter : (j + 1) * quarter]

    @pl.when(pl.program_id(0) == 0)
    def _():
        gain_out_ref[...] = jnp.zeros_like(gain_out_ref)

    gain_out_ref[0:1, :] += total


def conv_acts(ext_ref, weights, marks, lane):
    conv = conv_parts(ext_ref, weights, marks, lane)
    sig = sigmoid(conv)
    return conv, sig, conv * sig


def conv_pull(d_act, conv, sig, ext_ref, gext_ref, gtaps_ref, weights, marks, lane):
    d_conv = d_act * sig * (1.0 + conv * (1.0 - sig))
    for tap in range(TAPS):
        kept = d_conv * marks[:, tap : tap + 1] if tap < TAPS - 1 else d_conv
        place = (pl.ds(HALO - TAPS + 1 + tap, TOK), pl.ds(lane, DK))
        gtaps_ref[tap : tap + 1, lane : lane + DK] += jnp.sum(
            kept * ext_ref[place], axis=0, keepdims=True
        )
        gext_ref[place] += kept * weights[tap : tap + 1, lane : lane + DK]


def store_rows(gpre_ref, gext_ref):
    s = pl.program_id(0)
    gpre_ref[pl.ds(pl.multiple_of(s * TOK, TOK), TOK), :] = gext_ref[HALO:, :].astype(bf16)
    halo = pl.multiple_of(2 * TOK + s * HALO, HALO)
    gpre_ref[pl.ds(halo, HALO), :] = gext_ref[0:HALO, :].astype(bf16)


def unit_pull(d, hat, scale):
    return scale * (d - hat * jnp.sum(d * hat, axis=-1, keepdims=True))


def chunk_backward_early(
    pre_ref, rim_ref, scal_ref, rate_ref, taps_ref, marks_ref, docs_ref,
    uw_ref, s_ref, do_ref,
    gpre_ref, gtaps_ref, fresh_ref, recalled_ref, df_ref, dk_ref, dc_ref, ext_ref, gext_ref,
):
    inner = HEADS * DK
    ext_ref[0:HALO, :] = rim_ref[...].astype(f32)
    ext_ref[HALO:, :] = pre_ref[...].astype(f32)
    gext_ref[...] = jnp.zeros_like(gext_ref)

    @pl.when(pl.program_id(0) == 0)
    def _():
        gtaps_ref[...] = jnp.zeros_like(gtaps_ref)

    marks = marks_ref[0]
    weights = taps_ref[...]
    strength, total, total_t, causal, below = decays(
        scal_ref[...], rate_ref[...], marks, docs_ref[0]
    )
    rows, cols = iotas()
    reached = marks[:, 3:4]
    grad_c = jnp.zeros((TOK, TOK), f32)
    for h in range(HEADS):
        conv, sig, act = conv_acts(ext_ref, weights, marks, h * DK)
        act_k = conv_acts(ext_ref, weights, marks, inner + h * DK)[2]
        nq = unit_scale(act)
        q_hat = act * nq
        q, k = q_hat.astype(bf16), (act_k * unit_scale(act_k)).astype(bf16)
        c_col = total[:, HEADS + h : HEADS + h + 1]
        c_row = total_t[HEADS + h : HEADS + h + 1, :]
        decay = jnp.where(causal, jnp.exp(jnp.where(causal, c_col - c_row, 0.0)), 0.0)
        scores = dot1(q, k, NT) * decay
        start = jnp.exp(c_col) * reached
        state = s_ref[h]
        do = do_ref[:, h * DK : (h + 1) * DK].astype(bf16)
        fresh = uw_ref[h, :, :DK] - dot1(uw_ref[h, :, DK:], state, NT)
        fresh = fresh.astype(bf16)
        fresh_ref[h] = fresh
        recalled_ref[h] = dot1(k, state, NT)
        df_ref[h] = dot1(scores, do, TN)
        d_scores = dot1(do, fresh, NT)
        pull = d_scores * scores
        d_qk = (d_scores * decay).astype(bf16)
        dk_ref[h] = dot1(d_qk, q, TN)
        do_state = dot1(do, state)
        d_q = dot1(d_qk, k) + start * do_state
        d_start = jnp.sum(q.astype(f32) * do_state, axis=-1, keepdims=True)
        d_c = jnp.sum(pull - jnp.transpose(pull), axis=-1, keepdims=True) + d_start * start
        grad_c = jnp.where(cols == HEADS + h, d_c, grad_c)
        conv_pull(
            unit_pull(d_q, q_hat, nq), conv, sig, ext_ref, gext_ref, gtaps_ref, weights, marks,
            h * DK,
        )
    dc_ref[...] = grad_c
    store_rows(gpre_ref, gext_ref)


def chunk_backward_late(
    pre_ref, rim_ref, scal_ref, rate_ref, taps_ref, marks_ref, docs_ref,
    x_ref, s_ref, d_ref, fresh_ref, recalled_ref, df_ref, dk_ref, dc_ref,
    gpre_ref, gscal_ref, gtaps_ref, grate_ref, ext_ref, gext_ref,
):
    inner = HEADS * DK
    ext_ref[0:HALO, :] = rim_ref[:, inner:].astype(f32)
    ext_ref[HALO:, :] = pre_ref[:, inner:].astype(f32)
    gext_ref[...] = jnp.zeros_like(gext_ref)

    @pl.when(pl.program_id(0) == 0)
    def _():
        gtaps_ref[...] = jnp.zeros_like(gtaps_ref)
        grate_ref[...] = jnp.zeros_like(grate_ref)

    marks = marks_ref[0]
    weights = taps_ref[:, inner:]
    scal = scal_ref[...]
    rates = rate_ref[...]
    strength, total, total_t, causal, below = decays(scal, rates, marks, docs_ref[0])
    rows, cols = iotas()
    reached, tail = marks[:, 3:4], marks[:, 4:5]
    grad_b = jnp.zeros((TOK, TOK), f32)
    grad_c = jnp.zeros((TOK, TOK), f32)
    for h in range(HEADS):
        conv_k, sig_k, act_k = conv_acts(ext_ref, weights, marks, h * DK)
        conv_v, sig_v, act_v = conv_acts(ext_ref, weights, marks, inner + h * DK)
        nk = unit_scale(act_k)
        k_hat = act_k * nk
        k, v = k_hat.astype(bf16), act_v.astype(bf16)
        kf, vf = k.astype(f32), v.astype(f32)
        c_col = total[:, HEADS + h : HEADS + h + 1]
        c_row = total_t[HEADS + h : HEADS + h + 1, :]
        strict = causal & below
        strict_decay = jnp.where(strict, jnp.exp(jnp.where(strict, c_col - c_row, 0.0)), 0.0)
        b = strength[:, h : h + 1]
        gram_decay = dot1(k, k, NT) * strict_decay
        start = jnp.exp(c_col) * reached
        last = c_col[TOK - 1 : TOK, :]
        tail_decay = jnp.exp(last - c_col) * tail
        carry = jnp.exp(last) * reached[TOK - 1 : TOK, :]
        state, adj = s_ref[h], d_ref[h]
        fresh, recalled = fresh_ref[h], recalled_ref[h]
        d_fresh = df_ref[h] + dot1(kf * tail_decay, adj, NT)
        d_r = dot1(x_ref[h], d_fresh, TN)
        d_v = b * d_r
        d_b = jnp.sum(d_r * (vf - start * recalled), axis=-1, keepdims=True)
        d_start = -jnp.sum(d_v * recalled, axis=-1, keepdims=True)
        d_strict = -dot1(d_r, fresh, NT)
        strict_pull = d_strict * gram_decay
        d_b = d_b + jnp.sum(strict_pull, axis=-1, keepdims=True)
        d_gram = (d_strict * (b * strict_decay)).astype(bf16)
        d_k = dk_ref[h] - start * dot1(d_v, state) + dot1(d_gram, k) + dot1(d_gram, k, TN)
        fresh_adj = dot1(fresh, adj)
        d_k = d_k + tail_decay * fresh_adj
        d_tail = jnp.sum(kf * fresh_adj, axis=-1, keepdims=True) * tail_decay
        d_carry = jnp.sum(
            jnp.sum(adj.astype(f32) * state.astype(f32), axis=-1, keepdims=True),
            axis=0, keepdims=True,
        )
        pull = b * strict_pull
        d_c = jnp.sum(pull - jnp.transpose(pull), axis=-1, keepdims=True)
        d_c = d_c + d_start * start - d_tail
        d_last = d_carry * carry + jnp.sum(d_tail, axis=0, keepdims=True)
        d_c = d_c + jnp.where(rows[:, 0:1] == TOK - 1, d_last, 0.0)
        grad_b = jnp.where(cols == h, d_b, grad_b)
        grad_c = jnp.where(cols == HEADS + h, d_c, grad_c)
        conv_pull(
            unit_pull(d_k, k_hat, nk), conv_k, sig_k, ext_ref, gext_ref, gtaps_ref, weights,
            marks, h * DK,
        )
        conv_pull(
            d_v, conv_v, sig_v, ext_ref, gext_ref, gtaps_ref, weights, marks, inner + h * DK
        )
    upper = (cols >= rows).astype(bf16)
    grad_ld = dot2(upper, grad_c + dc_ref[...])
    decay_side = -grad_ld * rates * sigmoid(scal)
    gscal_ref[...] = jnp.where(
        cols < HEADS,
        grad_b * strength * (1.0 - strength),
        jnp.where(cols < 2 * HEADS, decay_side, 0.0),
    ).astype(bf16)
    grate_ref[0:1, :] += -jnp.sum(grad_ld * softplus(scal), axis=0, keepdims=True)
    store_rows(gpre_ref, gext_ref)


def row_grads(groups, lhs_count, rhs_count, *refs):
    out_ref = refs[-1]
    lhs = [refs[i][...] for i in range(lhs_count)]
    rhs = refs[lhs_count : lhs_count + rhs_count]
    lane = 0
    for group in groups:
        total = None
        for i, j in group:
            part = dot1(lhs[i][: rhs[j].shape[0]], rhs[j][...], TN)
            total = part if total is None else total + part
        out_ref[:, lane : lane + total.shape[1]] = total.astype(bf16)
        lane += total.shape[1]


def mixer_grads(
    offsets, place_ref, normed_ref, mixer_ref, og_ref, gq_ref, gkv_ref, gscal_ref, gated_ref, *outs
):
    width = normed_ref.shape[1]
    part = HEADS * DK // 2
    tokens = 2 * TOK

    def rows_x(ref, offset):
        place = lax.rem(place_ref[0] + offset, 4)
        return ref[:, pl.ds(pl.multiple_of(place * (width // 4), 128), width // 4)]

    def rows_z(ref, offset):
        place = lax.rem(place_ref[1] + offset, 4)
        cut = width // 16
        pieces = [
            ref[:, pl.ds(pl.multiple_of((j * 4 + place) * cut, 128), cut)] for j in range(4)
        ]
        return jnp.concatenate(pieces, axis=1)

    def store(outs, columns):
        lane = 0
        for column in columns:
            column = column.astype(bf16)
            lanes = slice(lane, lane + column.shape[1])
            rows = column.shape[0] // len(outs)
            for i, out in enumerate(outs):
                out[:, lanes] = column[i * rows : (i + 1) * rows]
            lane += column.shape[1]

    count = len(outs) // (2 * len(offsets))
    for i, offset in enumerate(offsets):
        normed = rows_x(normed_ref, offset)
        store(
            outs[i * count : (i + 1) * count],
            [
                dot1(normed[:tokens], og_ref[...], TN),
                dot1(normed, gq_ref[...], TN),
                dot1(normed[:tokens], gscal_ref[...], TN),
                dot1(normed, gkv_ref[:, :part], TN),
            ],
        )
        normed = rows_z(normed_ref, offset)
        i += len(offsets)
        store(
            outs[i * count : (i + 1) * count],
            [
                dot1(normed, gkv_ref[:, part:], TN),
                dot1(rows_z(mixer_ref, offset), gated_ref[...], TN),
            ],
        )


def input_grads(
    rim_ref, gq_ref, gkv_ref, gscal_ref, og_ref, left_ref, right_ref, out_ref, first_ref, second_ref
):
    inner = HEADS * DK
    part = inner // 2
    tokens = 2 * TOK

    @pl.when(pl.program_id(0) == 0)
    def _():
        first_ref[:, :inner] = gq_ref[:tokens, :]
        first_ref[:, inner : inner + 128] = gscal_ref[...]
        first_ref[:, inner + 128 : inner + 128 + part] = gkv_ref[:tokens, :part]
        first_ref[:, inner + 128 + part :] = og_ref[...]
        second_ref[...] = gkv_ref[:tokens, part:]
        for s in range(2):
            rows = slice((s + 1) * TOK - HALO, (s + 1) * TOK)
            rim = rim_ref[s * HALO : (s + 1) * HALO, :].astype(f32)

            def put(ref, lanes, came):
                ref[rows, lanes] = (ref[rows, lanes].astype(f32) + came).astype(bf16)

            put(first_ref, slice(0, inner), rim[:, :inner])
            put(
                first_ref,
                slice(inner + 128, inner + 128 + part),
                rim[:, inner : inner + part],
            )
            put(second_ref, slice(0, inner + part), rim[:, inner + part :])

    total = dot1(first_ref[...], left_ref[...], NT)
    total = total + dot1(second_ref[...], right_ref[:, : inner + part], NT)
    out_ref[...] = total.astype(bf16)


def ignoring(kernel, at, count):
    def inner_kernel(*refs):
        kernel(*refs[:at], *refs[at + count :])

    return inner_kernel


def dep_specs(deps):
    return [pl.BlockSpec(memory_space=pl.ANY) for _ in deps]


def cost(flops, moved):
    return pl.CostEstimate(flops=flops, bytes_accessed=moved, transcendentals=0)


def params():
    return pltpu.CompilerParams(vmem_limit_bytes=VMEM)


def whole(shape):
    return pl.BlockSpec(shape, lambda s: (0,) * len(shape))


def by_rows(rows, cols, base=0, lane=0):
    return pl.BlockSpec((rows, cols), lambda s: (base + s, lane))


def by_lead(*shape):
    return pl.BlockSpec(shape, lambda s: (s,) + (0,) * (len(shape) - 1))


def mixer_specs():
    wide = 3 * HEADS * DK
    return [
        by_rows(TOK, wide),
        by_rows(HALO, wide, 2 * TOK // HALO),
        by_rows(TOK, 128),
        whole((1, 128)),
        whole((TAPS, wide)),
        by_lead(1, TOK, 8),
        by_lead(1, 1, TOK),
    ]


def run_chunk_forward(pre, scal, rates, taps, marks, docs):
    quarter = DK // HEADS
    wide = 3 * HEADS * DK
    return pl.pallas_call(
        chunk_forward,
        grid=(2,),
        in_specs=mixer_specs(),
        out_specs=[
            by_lead(16, DK + quarter, DK),
            by_lead(HEADS, TOK, DK),
            by_lead(HEADS, TOK, DK),
            by_lead(HEADS, TOK, DK),
            by_lead(HEADS, TOK, 2 * DK),
        ],
        out_shape=[
            jax.ShapeDtypeStruct((SEQ, DK + quarter, DK), bf16),
            jax.ShapeDtypeStruct((8, TOK, DK), bf16),
            jax.ShapeDtypeStruct((8, TOK, DK), f32),
            jax.ShapeDtypeStruct((8, TOK, DK), bf16),
            jax.ShapeDtypeStruct((8, TOK, 2 * DK), f32),
        ],
        scratch_shapes=[pltpu.VMEM((HALO + TOK, wide), f32)],
        compiler_params=params(),
        cost_estimate=cost(10**10, 6 * 10**6),
    )(pre, pre, scal, rates, taps, marks, docs)


def run_scan_forward(got):
    return pl.pallas_call(
        scan_forward,
        out_shape=jax.ShapeDtypeStruct((SEQ, DK // HEADS, DK), bf16),
        compiler_params=params(),
        cost_estimate=cost(10**9, 3 * 10**6),
    )(got)


def run_scan_backward(got, local, deps):
    vmem = pl.BlockSpec(memory_space=pltpu.VMEM)
    return pl.pallas_call(
        ignoring(scan_backward, 2, len(deps)),
        in_specs=[vmem, vmem] + dep_specs(deps),
        out_specs=vmem,
        out_shape=jax.ShapeDtypeStruct((SEQ, DK // HEADS, DK), bf16),
        compiler_params=params(),
        cost_estimate=cost(10**9, 3 * 10**6),
    )(got, local, *deps)


def run_gate_forward(p, z, state, og, gain, deps):
    inner = HEADS * DK
    return pl.pallas_call(
        ignoring(gate_forward, 5, len(deps)),
        grid=(2,),
        in_specs=[
            by_lead(HEADS, TOK, DK),
            by_lead(HEADS, TOK, DK),
            by_lead(HEADS, DK, DK),
            by_rows(TOK, inner),
            whole((1, DK)),
        ]
        + dep_specs(deps),
        out_specs=[by_rows(TOK, inner), by_rows(TOK, inner)],
        out_shape=[
            jax.ShapeDtypeStruct((2 * TOK, inner), f32),
            jax.ShapeDtypeStruct((2 * TOK, inner), bf16),
        ],
        compiler_params=params(),
        cost_estimate=cost(10**9, 3 * 10**6),
    )(p, z, state, og, gain, *deps)


def run_gate_backward(gg, heads_out, og, gain, p):
    inner = HEADS * DK
    return pl.pallas_call(
        gate_backward,
        grid=(2,),
        in_specs=[
            by_rows(TOK, inner),
            by_rows(TOK, inner),
            by_rows(TOK, inner),
            whole((1, DK)),
            by_lead(HEADS, TOK, DK),
        ],
        out_specs=[
            by_rows(TOK, inner),
            by_rows(TOK, inner),
            by_lead(16, DK // HEADS, DK),
            whole((8, DK)),
        ],
        out_shape=[
            jax.ShapeDtypeStruct((2 * TOK, inner), f32),
            jax.ShapeDtypeStruct((2 * TOK, inner), bf16),
            jax.ShapeDtypeStruct((SEQ, DK // HEADS, DK), bf16),
            jax.ShapeDtypeStruct((8, DK), f32),
        ],
        compiler_params=params(),
        cost_estimate=cost(10**9, 3 * 10**6),
    )(gg, heads_out, og, gain, p)


def run_chunk_backward_early(pre, scal, rates, taps, marks, docs, uw, state, do, deps):
    inner = HEADS * DK
    wide = 3 * inner
    square = jax.ShapeDtypeStruct((8, TOK, DK), f32)
    return pl.pallas_call(
        ignoring(chunk_backward_early, 10, len(deps)),
        grid=(2,),
        in_specs=mixer_specs()
        + [
            by_lead(HEADS, TOK, 2 * DK),
            by_lead(HEADS, DK, DK),
            by_rows(TOK, inner),
        ]
        + dep_specs(deps),
        out_specs=[
            whole((2 * (TOK + HALO), inner)),
            whole((TAPS, inner)),
            by_lead(HEADS, TOK, DK),
            by_lead(HEADS, TOK, DK),
            by_lead(HEADS, TOK, DK),
            by_lead(HEADS, TOK, DK),
            by_rows(TOK, 128),
        ],
        out_shape=[
            jax.ShapeDtypeStruct((2 * (TOK + HALO), inner), bf16),
            jax.ShapeDtypeStruct((TAPS, inner), f32),
            jax.ShapeDtypeStruct((8, TOK, DK), bf16),
            square,
            square,
            square,
            jax.ShapeDtypeStruct((2 * TOK, 128), f32),
        ],
        scratch_shapes=[
            pltpu.VMEM((HALO + TOK, wide), f32),
            pltpu.VMEM((HALO + TOK, inner), f32),
        ],
        compiler_params=params(),
        cost_estimate=cost(5 * 10**9, 10**7),
    )(pre, pre, scal, rates, taps, marks, docs, uw, state, do, *deps)


def run_chunk_backward_late(
    pre, scal, rates, taps, marks, docs, x, state, adj, early, deps
):
    inner = HEADS * DK
    wide = 3 * inner
    return pl.pallas_call(
        ignoring(chunk_backward_late, 15, len(deps)),
        grid=(2,),
        in_specs=mixer_specs()
        + [
            by_lead(HEADS, TOK, DK),
            by_lead(HEADS, DK, DK),
            by_lead(HEADS, DK, DK),
            by_lead(HEADS, TOK, DK),
            by_lead(HEADS, TOK, DK),
            by_lead(HEADS, TOK, DK),
            by_lead(HEADS, TOK, DK),
            by_rows(TOK, 128),
        ]
        + dep_specs(deps),
        out_specs=[
            whole((2 * (TOK + HALO), 2 * inner)),
            by_rows(TOK, 128),
            whole((TAPS, 2 * inner)),
            whole((8, 128)),
        ],
        out_shape=[
            jax.ShapeDtypeStruct((2 * (TOK + HALO), 2 * inner), bf16),
            jax.ShapeDtypeStruct((2 * TOK, 128), bf16),
            jax.ShapeDtypeStruct((TAPS, 2 * inner), f32),
            jax.ShapeDtypeStruct((8, 128), f32),
        ],
        scratch_shapes=[
            pltpu.VMEM((HALO + TOK, 2 * inner), f32),
            pltpu.VMEM((HALO + TOK, 2 * inner), f32),
        ],
        compiler_params=params(),
        cost_estimate=cost(5 * 10**9, 10**7),
    )(pre, pre, scal, rates, taps, marks, docs, x, state, adj, *early, *deps)


def run_row_grads(lhs, rhs, groups, deps=()):
    width = lhs[0].shape[1]
    cols = sum(rhs[group[0][1]].shape[1] for group in groups)
    return pl.pallas_call(
        partial(row_grads, groups, len(lhs), len(rhs)),
        grid=(4,),
        in_specs=[pl.BlockSpec((m.shape[0], width // 4), lambda s: (0, s)) for m in lhs]
        + [whole(m.shape) for m in rhs]
        + dep_specs(deps),
        out_specs=pl.BlockSpec((width // 4, cols), lambda s: (s, 0)),
        out_shape=jax.ShapeDtypeStruct((width, cols), bf16),
        compiler_params=params(),
        cost_estimate=cost(2 * rhs[0].shape[0] * width * cols, 2 * width * cols),
    )(*lhs, *rhs, *deps)


def run_mixer_grads(offsets, halves, *arrays, deps=()):
    width = arrays[0].shape[1]
    inner = HEADS * DK
    vmem = pl.BlockSpec(memory_space=pltpu.VMEM)
    place = jnp.stack([place_of("x"), place_of("z")]).astype(jnp.int32)
    shapes = [
        (width // 4 // halves, cols)
        for cols in (2 * inner + inner // 2 + 128, 2 * inner + inner // 2)
        for _ in range(halves * len(offsets))
    ]
    return pl.pallas_call(
        ignoring(partial(mixer_grads, offsets), 8, len(deps)),
        in_specs=[pl.BlockSpec(memory_space=pltpu.SMEM)] + [vmem] * 7 + dep_specs(deps),
        out_specs=[vmem] * len(shapes),
        out_shape=[jax.ShapeDtypeStruct(shape, bf16) for shape in shapes],
        compiler_params=params(),
        cost_estimate=cost(2 * 256 * width * 5 * inner, 2 * width * 5 * inner),
    )(place, *arrays, *deps)


def run_input_grads(rim, gq, gkv, gscal, og, left, right, deps):
    inner = HEADS * DK
    width = left.shape[0]
    tokens = 2 * TOK
    cut = width // 4
    return pl.pallas_call(
        ignoring(input_grads, 7, len(deps)),
        grid=(4,),
        in_specs=[whole(m.shape) for m in (rim, gq, gkv, gscal, og)]
        + [
            by_rows(cut, left.shape[1]),
            by_rows(cut, right.shape[1]),
        ]
        + dep_specs(deps),
        out_specs=pl.BlockSpec((tokens, cut), lambda s: (0, s)),
        out_shape=jax.ShapeDtypeStruct((tokens, width), bf16),
        scratch_shapes=[
            pltpu.VMEM((tokens, left.shape[1]), bf16),
            pltpu.VMEM((tokens, inner + inner // 2), bf16),
        ],
        compiler_params=params(),
        cost_estimate=cost(2 * tokens * width * 5 * inner, 2 * width * 5 * inner),
    )(rim, gq, gkv, gscal, og, left, right, *deps)


SEQ_AXES = ("x", "z", "y")
GROUP_AXES = ("y", "head")


def passed_along(array, by):
    pairs = [(i, i + by) for i in range(SEQ) if 0 <= i + by < SEQ]
    return lax.ppermute(array, SEQ_AXES, pairs)


def along(array, axis, by):
    count = lax.axis_size(axis)
    return lax.ppermute(array, axis, [(i, (i + by) % count) for i in range(count)])


def place_of(axis):
    return lax.axis_index(axis)


def flipped(array, axes, mask):
    count = lax.axis_size(axes)
    return lax.ppermute(array, axes, [(i, i ^ mask) for i in range(count)])


def pick(array, index, dim):
    return lax.dynamic_index_in_dim(array, index, dim, keepdims=False)


def ordered(mine, other, place, axis=0):
    first = place == 0
    return jnp.concatenate(
        [jnp.where(first, mine, other), jnp.where(first, other, mine)], axis=axis
    )


def later(array, *deps):
    for dep in deps:
        first = lax.slice(dep, (0,) * dep.ndim, (1,) * dep.ndim).reshape(())
        array = array + (first * 0).astype(array.dtype)
    return array


def gather_last(first, second):
    near, far, halfway = near_and_far(first, second, ("z", "x"))
    outs = []
    for i, (array, axis, dim) in enumerate(((first, "z", 1), (second, "x", 0))):
        place = place_of(axis)
        shape = list(array.shape)
        shape.insert(dim, 4)
        out = jnp.zeros(shape, array.dtype)
        block = jnp.concatenate(far[2 * i : 2 * i + 2], axis=0)
        for offset, block in ((0, array), (-1, near[2 * i]), (-2, block), (1, near[2 * i + 1])):
            out = lax.dynamic_update_index_in_dim(out, block, (place + offset) % 4, dim)
        outs.append(out.reshape(-1, array.shape[-1]))
    return outs[0], outs[1], halfway


def exchange(array, axis):
    return lax.all_to_all(array, axis, split_axis=0, concat_axis=0, tiled=True)


def head_place():
    index = lax.axis_index("head")
    return index // 2, index % 2


def core_scatter(partial_rows):
    core = head_place()[1]
    rows = partial_rows.shape[0] // HEADS
    blocks = partial_rows.astype(bf16).reshape(2, 2, rows, -1)
    got = flipped(pick(blocks, 1 - core, 1), "head", 1)
    return pick(blocks, core, 1).astype(f32) + got.astype(f32), got


def chip_scatter(both, *gates):
    chip = head_place()[0]
    got = flipped(later(pick(both, 1 - chip, 0), *gates).astype(bf16), "head", 2)
    return pick(both, chip, 0) + got.astype(f32)


def head_gather(rows):
    chip, core = head_place()
    chip_got = flipped(rows, "head", 2)
    first = chip == 0
    chips = [jnp.where(first, rows, chip_got), jnp.where(first, chip_got, rows)]
    chips = jnp.stack(chips)
    got = flipped(chips, "head", 1)
    first = core == 0
    cores = [jnp.where(first, chips, got), jnp.where(first, got, chips)]
    return jnp.stack(cores, axis=1).reshape(HEADS * rows.shape[0], -1), chip_got


def group_scatter(partial_rows):
    chip, core = head_place()
    place = place_of("y") * 2 + chip
    blocks = partial_rows.astype(bf16).reshape(4, 2, -1, partial_rows.shape[1])
    got = flipped(pick(blocks, 1 - core, 1), GROUP_AXES, 1)
    both = pick(blocks, core, 1).astype(f32) + got.astype(f32)
    total = pick(both, place, 0)
    for mask in (2, 1, 3):
        part = pick(both, jnp.bitwise_xor(place, mask), 0).astype(bf16)
        total = total + flipped(part, GROUP_AXES, 2 * mask).astype(f32)
    return total, got


def group_gather(rows):
    chip, core = head_place()
    place = place_of("y") * 2 + chip
    out = jnp.zeros((4,) + rows.shape, rows.dtype)
    for mask in (2, 1, 3, 0):
        got = flipped(rows, GROUP_AXES, 2 * mask) if mask else rows
        out = lax.dynamic_update_index_in_dim(out, got, jnp.bitwise_xor(place, mask), 0)
    got = flipped(out, GROUP_AXES, 1)
    first = core == 0
    cores = [jnp.where(first, out, got), jnp.where(first, got, out)]
    return jnp.stack(cores, axis=1).reshape(8 * rows.shape[0], -1)


def in_vmem(kernel, shapes, place, *arrays, deps=()):
    vmem = pl.BlockSpec(memory_space=pltpu.VMEM)
    moved = sum(2 * a.size for a in arrays)
    return pl.pallas_call(
        ignoring(kernel, 1 + len(arrays), len(deps)),
        in_specs=[pl.BlockSpec(memory_space=pltpu.SMEM)] + [vmem] * len(arrays) + dep_specs(deps),
        out_specs=[vmem] * len(shapes),
        out_shape=[jax.ShapeDtypeStruct(shape, kind) for shape, kind in shapes],
        compiler_params=params(),
        cost_estimate=cost(moved, moved),
    )(place, *arrays, *deps)


def add_far(place_ref, *refs):
    for i in range(2):
        right, left, ahead, behind = refs[4 * i : 4 * i + 4]
        right_out, left_out = refs[8 + 2 * i : 10 + 2 * i]
        half = ahead.shape[0]
        total = right[:half].astype(f32) + ahead[...].astype(f32)
        right_out[:half] = total.astype(bf16)
        right_out[half:] = right[half:]
        left_out[:half] = left[:half]
        total = left[half:].astype(f32) + behind[...].astype(f32)
        left_out[half:] = total.astype(bf16)


def add_and_cut(place_ref, *refs):
    for i in range(2):
        members = refs[3 * i : 3 * i + 3]
        outs = refs[6 + 4 * i : 10 + 4 * i]
        rows = members[0].shape[0] // 4
        for out, by in zip(outs, (0, 2, 1, 3)):
            start = pl.multiple_of(lax.rem(place_ref[1 - i] + by, 4) * rows, rows)
            total = members[0][pl.ds(start, rows), :].astype(f32)
            for member in members[1:]:
                total = total + member[pl.ds(start, rows), :].astype(f32)
            out[...] = total.astype(bf16)


def add_and_halve(place_ref, *refs):
    kept, sent = refs[8:]
    rows = kept.shape[0]
    lane = 0
    for i in range(2):
        parts = refs[4 * i : 4 * i + 4]
        lanes = slice(lane, lane + parts[0].shape[1])
        lane += parts[0].shape[1]
        for out, at in ((kept, place_ref[2]), (sent, 1 - place_ref[2])):
            start = pl.multiple_of(at * rows, rows)
            total = parts[0][pl.ds(start, rows), :].astype(f32)
            for part in parts[1:]:
                total = total + part[pl.ds(start, rows), :].astype(f32)
            out[:, lanes] = total.astype(out.dtype)


def places():
    return jnp.stack([place_of(axis) for axis in SEQ_AXES]).astype(jnp.int32)


def reduce_near(owns, arrays, deps):
    shapes = [(arrays[i].shape, bf16) for i in (0, 1, 4, 5)]
    sums = in_vmem(add_far, shapes, places(), *arrays, deps=deps)
    gate = sums[0]
    arrays = []
    for i, axis in enumerate(("x", "z")):
        arrays += [owns[i], along(sums[2 * i], axis, 1), along(sums[2 * i + 1], axis, -1)]
    return arrays, gate


def reduce_cross(arrays, deps):
    shapes = []
    for own in (arrays[0], arrays[3]):
        shapes += [((own.shape[0] // 4, own.shape[1]), bf16)] * 4
    cut = in_vmem(add_and_cut, shapes, places(), *arrays, deps=deps)
    arrays = []
    for i, axis in enumerate(("z", "x")):
        own, two, one, three = cut[4 * i : 4 * i + 4]
        arrays += [own, along(two, axis, 2), along(one, axis, 1), along(three, axis, -1)]
    return arrays, cut[0]


def reduce_end(arrays, deps):
    rows, cols = arrays[0].shape[0] // 2, arrays[0].shape[1] + arrays[4].shape[1]
    shapes = [((rows, cols), f32), ((rows, cols), bf16)]
    kept, sent = in_vmem(add_and_halve, shapes, places(), *arrays, deps=deps)
    return kept + along(sent, "y", 1).astype(f32), sent


def pair_up(place_ref, left, left_other, right, right_other, left_out, right_out):
    rows = left.shape[0]
    mine = pl.multiple_of(place_ref[2] * rows, rows)
    other = pl.multiple_of((1 - place_ref[2]) * rows, rows)
    left_out[pl.ds(mine, rows), :] = left[...]
    left_out[pl.ds(other, rows), :] = left_other[...]
    right_out[pl.ds(mine, rows), :] = right[...]
    right_out[pl.ds(other, rows), :] = right_other[...]


def pass_on(place_ref, *refs):
    for i in range(2):
        half = refs[4 + 2 * i].shape[0]
        refs[4 + 2 * i][...] = refs[2 * i][:half]
        refs[5 + 2 * i][...] = refs[2 * i + 1][half:]


def put_in_place(axes, place_ref, *refs):
    for i in range(2):
        out = refs[10 + i]
        own, left, right, far_a, far_b = refs[5 * i : 5 * i + 5]
        place = place_ref[axes[i]]
        half = far_a.shape[0]
        out[place] = own[...]
        out[lax.rem(place + 3, 4)] = left[...]
        out[lax.rem(place + 1, 4)] = right[...]
        out[lax.rem(place + 2, 4), :half] = far_a[...]
        out[lax.rem(place + 2, 4), half:] = far_b[...]


def near_and_far(first, second, axes):
    near = []
    for array, axis in ((first, axes[0]), (second, axes[1])):
        near += [along(array, axis, 1), along(array, axis, -1)]
    shapes = []
    for array in (first, second):
        shapes += [((array.shape[0] // 2,) + array.shape[1:], bf16)] * 2
    halves = in_vmem(pass_on, shapes, places(), *near)
    far = []
    for i in range(2):
        far += [along(halves[2 * i], axes[i], 1), along(halves[2 * i + 1], axes[i], -1)]
    return near, far, halves[0]


def sum_along(array, axis):
    total = array
    for by in range(1, lax.axis_size(axis)):
        total = total + along(array, axis, by)
    return total


def mm(a, b, dims="ij,jk->ik"):
    return jnp.einsum(dims, a, b, preferred_element_type=f32)


def row_scale(x):
    return lax.rsqrt(jnp.mean(x * x, axis=-1, keepdims=True) + norm_eps)


def norm_pull(x, scale, gain, grad):
    unit = x * scale
    scaled = grad * gain
    return scale * (scaled - unit * jnp.mean(scaled * unit, axis=-1, keepdims=True))


def doc_tables(doc_lengths):
    first = lax.axis_index(SEQ_AXES) * TOK - (TAPS - 1)
    ends = jnp.cumsum(doc_lengths, axis=1)
    places = first + jnp.arange(TOK + TAPS - 1, dtype=jnp.int32)
    counted = jnp.sum((places[None, :, None] >= ends[:, None, :]).astype(jnp.int32), axis=2)
    ext = jnp.where(places[None, :] >= 0, counted, -1)
    local = ext[:, TAPS - 1 :]
    columns = [(ext[:, o : o + TOK] == local) for o in range(TAPS - 1)]
    columns.append(local == ext[:, TAPS - 2 : TAPS - 1])
    columns.append(local == local[:, -1:])
    columns.append(local)
    columns += [jnp.zeros_like(local)] * 2
    marks = jnp.stack([c.astype(f32) for c in columns], axis=-1)
    return marks, local.astype(f32)[:, None, :]


def body(
    inputs, doc_lengths, norm_in, query_weight, key_weight, value_weight, outgate_weight,
    scalar_weight, conv_kernel, decay_rate, head_norm, output_weight, norm_ffn, gate_weight,
    up_weight, down_weight, grad_out,
):
    width = inputs.shape[2]
    inner = HEADS * DK
    hidden = gate_weight.shape[1]
    head_index = lax.axis_index("head")
    quarter = 2 * TOK // HEADS

    gains = jnp.stack([norm_in, norm_ffn], axis=1)
    misc = jnp.concatenate([scalar_weight.reshape(-1, 2 * HEADS), gains], axis=1)
    misc = jnp.pad(misc, ((0, 0), (0, 128 - misc.shape[1])))
    part = inner // 2
    left = jnp.concatenate([query_weight, misc, key_weight[:, :part], outgate_weight], axis=1)
    right = jnp.concatenate([key_weight[:, part:], value_weight, output_weight.T], axis=1)
    y_place = place_of("y")
    rows = left.shape[0]
    left, right = in_vmem(
        pair_up,
        [((2 * rows, left.shape[1]), bf16), ((2 * rows, right.shape[1]), bf16)],
        places(),
        left, along(left, "y", 1), right, along(right, "y", 1),
    )
    near, far, _ = near_and_far(left, right, ("x", "z"))
    left, right = in_vmem(
        partial(put_in_place, (0, 1)),
        [((4, 2 * rows, part.shape[1]), bf16) for part in (left, right)],
        places(),
        left, *near[:2], *far[:2], right, *near[2:], *far[2:],
    )
    all_left, all_right, halfway = gather_last(left, right)
    w_gate, w_out_t = all_left[:, -inner:], all_right[:, -inner:]
    w_left, w_right = all_left[:, :-inner], all_right[:, :-inner]
    gains = w_left[:, inner : inner + 128].T[2 * HEADS : 2 * HEADS + 2].astype(f32)
    gain_in, gain_ffn = gains[0:1], gains[1:2]

    units = hidden // 2
    span = -(-units // 128) * 128

    def in_halves(weight):
        halves = weight.reshape(weight.shape[0], 2, units)
        return jnp.pad(halves, ((0, 0), (0, 0), (0, span - units)))

    packed = jnp.concatenate(
        [in_halves(gate_weight), in_halves(up_weight), in_halves(down_weight.T)], axis=2
    )
    other = along(later(pick(packed, 1 - y_place, 1), left), "y", 1)
    packed = later(ordered(pick(packed, y_place, 1), other, y_place), halfway)
    w_ffn = lax.all_gather(packed, ("x", "z"), axis=0, tiled=True)
    w_gateup = w_ffn[:, : 2 * span]
    w_down_t = w_ffn[:, 2 * span :]

    marks, docs_row = doc_tables(doc_lengths)
    taps = jnp.transpose(conv_kernel.astype(f32), (1, 0, 2)).reshape(TAPS, 3 * inner)
    rates = jnp.zeros((1, 128), f32)
    rates = rates.at[0, HEADS : 2 * HEADS].set(decay_rate.astype(f32))
    gain_head = head_norm.astype(f32).reshape(1, DK)

    halo = passed_along(inputs[:, TOK - HALO :], 1)
    tokens = inputs.reshape(2 * TOK, width)
    all_rows = jnp.concatenate([tokens, halo.reshape(2 * HALO, width)], axis=0).astype(f32)
    scale_in = row_scale(all_rows)
    normed_all = (all_rows * scale_in * gain_in).astype(bf16)
    normed_in = normed_all[: 2 * TOK]

    left = mm(normed_all, w_left)
    right = mm(normed_all, w_right)
    pre = jnp.concatenate(
        [left[:, :inner].astype(bf16), left[:, inner + 128 :].astype(bf16), right.astype(bf16)],
        axis=1,
    )
    scal = left[: 2 * TOK, inner : inner + 128]

    grad_rows = grad_out.reshape(2 * TOK, width)
    grad_other = along(grad_rows, "y", 1)
    send, p, z, x, uw = run_chunk_forward(pre, scal, rates, taps, marks, docs_row)
    out_gate = mm(normed_in, w_gate)
    got = exchange(send, SEQ_AXES)
    state = exchange(run_scan_forward(got), SEQ_AXES).reshape(8, DK, DK)
    heads_out, gated_rows = run_gate_forward(
        p, z, state, out_gate, gain_head, (grad_other,)
    )

    mine = partial(lax.dynamic_slice_in_dim, start_index=head_index * quarter, slice_size=quarter)
    residual = mine(tokens).astype(f32) + chip_scatter(
        core_scatter(mm(gated_rows, w_out_t, "ij,kj->ik"))[0]
    )
    scale_ffn = row_scale(residual)
    normed_ffn = group_gather((residual * scale_ffn * gain_ffn).astype(bf16))

    group_grads = ordered(grad_rows, grad_other, y_place)
    grad_act = mm(group_grads, w_down_t)
    gate_up = mm(normed_ffn, w_gateup)
    gate, up = gate_up[:, :span], gate_up[:, span:]
    sig = sigmoid(gate)
    silu = gate * sig
    product = (silu * up).astype(bf16)
    gu_grad = jnp.concatenate(
        [
            (grad_act * up * sig * (1.0 + gate * (1.0 - sig))).astype(bf16),
            (grad_act * silu).astype(bf16),
        ],
        axis=1,
    )
    ffn_part = mm(gu_grad, w_gateup, "ij,kj->ik").astype(bf16)
    grad_normed = group_scatter(ffn_part)[0]
    back = norm_pull(residual, scale_ffn, gain_ffn, grad_normed)
    grad_residual = mine(grad_rows).astype(f32) + back
    grad_mixer = head_gather(grad_residual.astype(bf16))[0]

    grad_gated = mm(grad_mixer, w_out_t)
    do, gate_grad_mix, local, part_gain_head = run_gate_backward(
        grad_gated, heads_out, out_gate, gain_head, p
    )
    local_got = exchange(local, SEQ_AXES)
    early = run_chunk_backward_early(
        pre, scal, rates, taps, marks, docs_row, uw, state, do, ()
    )
    gq, gtaps_q = early[:2]
    ffn_all = run_row_grads(
        [normed_ffn, group_grads], [gu_grad, product], (((0, 0),), ((1, 1),)), (local,)
    )
    ffn = lax.psum_scatter(ffn_all, ("x", "z"), scatter_dimension=0, tiled=True)
    adj_out = run_scan_backward(got, local_got, (gq,))
    ffn_out, ffn_got = group_scatter(mm(later(product, local), w_down_t, "ij,kj->ik"))
    adj = exchange(adj_out, SEQ_AXES).reshape(8, DK, DK)
    gkv, gscal, gtaps_kv, grate = run_chunk_backward_late(
        pre, scal, rates, taps, marks, docs_row, x, state, adj, early[2:], (ffn_got,)
    )

    arrays = (normed_all, grad_mixer, gate_grad_mix, gq, gkv, gscal, gated_rows)
    far = run_mixer_grads((2,), 2, *arrays)
    blocks = run_mixer_grads((1, 3, 0), 1, *arrays, deps=(far[0], ffn_out))
    owns, partials = (blocks[2], blocks[5]), []
    for i, axis in enumerate(("x", "z")):
        partials += blocks[3 * i : 3 * i + 2]
        partials += [along(far[2 * i], axis, 1), along(far[2 * i + 1], axis, -1)]

    gtaps = jnp.concatenate([gtaps_q, gtaps_kv], axis=1).reshape(12, inner)
    tail = jnp.concatenate([part_gain_head[:1], grate[:1]], axis=1)
    tail = jnp.pad(tail, ((0, 3), (0, inner - tail.shape[1])))
    small = jnp.concatenate([gtaps, tail], axis=0)
    rim = jnp.concatenate([gq[2 * TOK :], gkv[2 * TOK :]], axis=1)
    rim = passed_along(rim, -1)
    input_sent = run_input_grads(
        rim, gq, gkv, gscal, gate_grad_mix, all_left, all_right, (blocks[0],)
    )
    partials, near_gate = reduce_near(owns, partials, (input_sent,))
    ffn = ffn.reshape(2, -1, 3, span)[..., :units]
    ffn_other = along(later(pick(ffn, 1 - y_place, 0), near_gate), "y", 1)
    ffn = ordered(pick(ffn, y_place, 0), ffn_other, y_place, 2).astype(f32)
    by_core = core_scatter(later(input_sent, near_gate))[0]
    grad_normed_in = chip_scatter(by_core)
    own = mine(tokens).astype(f32)
    back_in = norm_pull(own, row_scale(own), gain_in, grad_normed_in)
    both = jnp.concatenate([residual + ffn_out, grad_residual + back_in], axis=1)
    both = both.astype(bf16)
    partials, cross_gate = reduce_cross(partials, (both, ffn_other))
    small = sum_along(later(small, partials[5]), "x")
    mixer_w, end_gate = reduce_end(partials, ())
    both, chip_got = head_gather(later(both, end_gate))
    small = sum_along(sum_along(later(small, chip_got), "z"), "y")
    outputs, grad_in = both[:, :width], both[:, width:].astype(f32)

    rows = width // SEQ
    key_at = 2 * inner + 128
    grad_conv = jnp.transpose(small[:12].reshape(TAPS, 3, inner), (1, 0, 2))

    def gain_grad(gain, weights, grads):
        total = 0.0
        for weight, grad in zip(weights, grads):
            total = total + jnp.sum(weight.astype(f32) * grad, axis=1)
        return total / gain.astype(f32)

    grad_scalar = mixer_w[:, 2 * inner : 2 * inner + 2 * HEADS]
    gain_parts = jnp.concatenate(
        [
            gain_grad(
                norm_in,
                (outgate_weight, query_weight, scalar_weight.reshape(rows, -1), key_weight, value_weight),
                (
                    mixer_w[:, :inner],
                    mixer_w[:, inner : 2 * inner],
                    grad_scalar,
                    mixer_w[:, key_at : key_at + inner],
                    mixer_w[:, key_at + inner : key_at + 2 * inner],
                ),
            ),
            gain_grad(norm_ffn, (gate_weight, up_weight), (ffn[:, 0], ffn[:, 1])),
            small[12, :DK],
        ]
    )
    shared = sum_along(gain_parts[None], "head")[0]
    return (
        outputs.reshape(inputs.shape),
        grad_in.reshape(inputs.shape),
        shared[:rows],
        mixer_w[:, inner : 2 * inner],
        mixer_w[:, key_at : key_at + inner],
        mixer_w[:, key_at + inner : key_at + 2 * inner],
        mixer_w[:, :inner],
        grad_scalar.reshape(rows, 2, HEADS),
        grad_conv,
        small[12, DK + HEADS : DK + 2 * HEADS],
        shared[2 * rows :],
        mixer_w[:, key_at + 2 * inner :].T,
        shared[rows : 2 * rows],
        ffn[:, 0],
        ffn[:, 1],
        ffn[:, 2].T,
    )


def solution(mesh):
    mesh = Mesh(mesh.devices.reshape(4, 4, 2, HEADS), ("x", "z", "y", "head"))
    seq = SEQ_AXES
    weight = P(seq, "head")
    weight_t = P("head", seq)
    tokens = P(None, seq, None)
    scalars = P(seq, None, "head")
    taps = P(None, None, "head")
    return jax.shard_map(
        body,
        mesh=mesh,
        in_specs=(
            tokens, P(), P(seq), weight, weight, weight, weight, scalars, taps, P("head"), P(),
            weight_t, P(seq), weight, weight, weight_t, tokens,
        ),
        out_specs=(
            tokens, tokens, P(seq), weight, weight, weight, weight, scalars, taps, P("head"),
            P(), weight_t, P(seq), weight, weight, weight_t,
        ),
        check_vma=False,
    )
```

```python
from functools import partial

import jax
import jax.numpy as jnp
from jax import lax
from jax.experimental import pallas as pl
from jax.experimental.pallas import tpu as pltpu
from jax.sharding import Mesh
from jax.sharding import PartitionSpec as P

f32 = jnp.float32
bf16 = jnp.bfloat16
norm_eps = 1e-06
head_eps = 1e-05
SEQ = 32
HEADS = 4
DK = 128
TOK = 128
TAPS = 4
HALO = 16
VMEM = 56 * 1024 * 1024

NN = (((1,), (0,)), ((), ()))
NT = (((1,), (1,)), ((), ()))
TN = (((0,), (0,)), ((), ()))


def dot1(a, b, dims=NN):
    return lax.dot_general(a.astype(bf16), b.astype(bf16), dims, preferred_element_type=f32)


def split(a):
    high = a.astype(bf16)
    return high, (a - high.astype(f32)).astype(bf16)


def dot3(a, b, dims=NN):
    ah, al = split(a)
    bh, bl = split(b)
    return dot1(ah, bh, dims) + (dot1(ah, bl, dims) + dot1(al, bh, dims))


def dot2(exact, b, dims=NN):
    high = b.astype(bf16)
    rest = b - high.astype(f32)
    mid = rest.astype(bf16)
    low = (rest - mid.astype(f32)).astype(bf16)
    return dot1(exact, high, dims) + (dot1(exact, mid, dims) + dot1(exact, low, dims))


def sigmoid(x):
    return 1.0 / (1.0 + jnp.exp(-x))


def softplus(x):
    return jnp.maximum(x, 0.0) + jnp.log1p(jnp.exp(-jnp.abs(x)))


def iotas():
    rows = lax.broadcasted_iota(jnp.int32, (TOK, TOK), 0)
    cols = lax.broadcasted_iota(jnp.int32, (TOK, TOK), 1)
    return rows, cols


def unit_inverses(stricts):
    rows, cols = iotas()
    eye = (rows == cols).astype(f32)
    apart = jnp.bitwise_xor(rows, cols)
    results = []
    first = (apart == 1) & (rows > cols)
    results = [eye - jnp.where(first, a, 0.0) for a in stricts]
    size = 2
    while size < TOK:
        corner = (apart >= size) & (apart < 2 * size) & (rows > cols)
        parts = [dot3(jnp.where(corner, a, 0.0), x) for a, x in zip(stricts, results)]
        results = [x - dot3(x, c) for x, c in zip(results, parts)]
        size *= 2
    return results


def decays(scal, rates, marks, docs_row):
    rows, cols = iotas()
    strength = sigmoid(scal)
    log_decay = -rates * softplus(scal)
    lower = (rows >= cols).astype(bf16)
    total = dot2(lower, log_decay)
    total_t = jnp.transpose(total)
    same = marks[:, 5:6] == docs_row
    causal = same & (rows >= cols)
    return strength, total, total_t, causal, rows > cols


def conv_parts(ext_ref, weights, marks, lane):
    out = None
    for tap in range(TAPS):
        piece = ext_ref[pl.ds(HALO - TAPS + 1 + tap, TOK), pl.ds(lane, DK)]
        if tap < TAPS - 1:
            piece = piece * marks[:, tap : tap + 1]
        piece = piece * weights[tap : tap + 1, lane : lane + DK]
        out = piece if out is None else out + piece
    return out


def unit_scale(x):
    return lax.rsqrt(jnp.sum(x * x, axis=-1, keepdims=True) + norm_eps)


def chunk_forward(
    pre_ref, rim_ref, scal_ref, rate_ref, taps_ref, marks_ref, docs_ref,
    send_ref, p_ref, z_ref, x_ref, uw_ref, ext_ref,
):
    inner = HEADS * DK
    ext_ref[0:HALO, :] = rim_ref[...].astype(f32)
    ext_ref[HALO:, :] = pre_ref[...].astype(f32)
    marks = marks_ref[0]
    weights = taps_ref[...]
    strength, total, total_t, causal, below = decays(
        scal_ref[...], rate_ref[...], marks, docs_ref[0]
    )
    rows, cols = iotas()
    reached, tail = marks[:, 3:4], marks[:, 4:5]
    heads = []
    for h in range(HEADS):
        acts = []
        for c in range(3):
            conv = conv_parts(ext_ref, weights, marks, c * inner + h * DK)
            acts.append(conv * sigmoid(conv))
        q = (acts[0] * unit_scale(acts[0])).astype(bf16)
        k = (acts[1] * unit_scale(acts[1])).astype(bf16)
        v = acts[2].astype(bf16)
        c_col = total[:, HEADS + h : HEADS + h + 1]
        c_row = total_t[HEADS + h : HEADS + h + 1, :]
        decay = jnp.where(causal, jnp.exp(jnp.where(causal, c_col - c_row, 0.0)), 0.0)
        b = strength[:, h : h + 1]
        gram = dot1(k, k, NT)
        strict = jnp.where(below, b * gram * decay, 0.0)
        heads.append((q, k, v, c_col, decay, b, strict))
    inverses = unit_inverses([head[6] for head in heads])
    for h in range(HEADS):
        q, k, v, c_col, decay, b, strict = heads[h]
        x = inverses[h]
        start = jnp.exp(c_col) * reached
        kf = k.astype(f32)
        uw = dot3(x, jnp.concatenate([b * v.astype(f32), (b * start) * kf], axis=1))
        scores = dot1(q, k, NT) * decay
        suw = dot3(scores, uw)
        last = c_col[TOK - 1 : TOK, :]
        tail_k = kf * (jnp.exp(last - c_col) * tail)
        carry = jnp.exp(last) * reached[TOK - 1 : TOK, :]
        u, w = uw[:, :DK], uw[:, DK:]
        move = jnp.where(rows == cols, carry, 0.0) - dot3(tail_k, w, TN)
        offset_t = dot3(u, tail_k, TN)
        p_ref[h] = (q.astype(f32) * start - suw[:, DK:]).astype(bf16)
        z_ref[h] = suw[:, :DK]
        x_ref[h] = x.astype(bf16)
        uw_ref[h] = uw
        quarter = DK // HEADS
        for j in range(HEADS):
            send_ref[HEADS * h + j, 0:DK, :] = move.astype(bf16)
            send_ref[HEADS * h + j, DK : DK + quarter, :] = offset_t[
                j * quarter : (j + 1) * quarter
            ].astype(bf16)


def scan_forward(got_ref, out_ref):
    state = jnp.zeros((DK // HEADS, DK), f32)
    for i in range(SEQ):
        out_ref[i] = state.astype(bf16)
        if i + 1 < SEQ:
            high, low = split(state)
            both = dot1(jnp.concatenate([high, low], axis=0), got_ref[i, 0:DK, :], NT)
            half = DK // HEADS
            state = both[:half] + both[half:] + got_ref[i, DK : DK + half, :].astype(f32)


def scan_backward(got_ref, local_ref, out_ref):
    state = jnp.zeros((DK // HEADS, DK), f32)
    for i in range(SEQ - 1, -1, -1):
        out_ref[i] = state.astype(bf16)
        if i > 0:
            high, low = split(state)
            both = dot1(jnp.concatenate([high, low], axis=0), got_ref[i, 0:DK, :])
            half = DK // HEADS
            state = both[:half] + both[half:] + local_ref[i].astype(f32)


def gate_forward(p_ref, z_ref, s_ref, og_ref, gain_ref, heads_ref, gated_ref):
    gain = gain_ref[...]
    for h in range(HEADS):
        lanes = slice(h * DK, (h + 1) * DK)
        out = dot1(p_ref[h], s_ref[h], NT) + z_ref[h]
        heads_ref[:, lanes] = out
        r = lax.rsqrt(jnp.mean(out * out, axis=-1, keepdims=True) + head_eps)
        og = og_ref[:, lanes]
        gated_ref[:, lanes] = (out * r * gain * (og * sigmoid(og))).astype(bf16)


def gate_backward(
    gg_ref, heads_ref, og_ref, gain_ref, p_ref, do_ref, mix_ref, local_ref, gain_out_ref
):
    gain = gain_ref[...]
    total = jnp.zeros((1, DK), f32)
    quarter = DK // HEADS
    for h in range(HEADS):
        lanes = slice(h * DK, (h + 1) * DK)
        out = heads_ref[:, lanes]
        og = og_ref[:, lanes]
        gg = gg_ref[:, lanes]
        r = lax.rsqrt(jnp.mean(out * out, axis=-1, keepdims=True) + head_eps)
        u = out * r
        sig = sigmoid(og)
        w = og * sig
        ggw = gg * w
        g = ggw * gain
        total = total + jnp.sum(ggw * u, axis=0, keepdims=True)
        grad = r * (g - u * jnp.mean(g * u, axis=-1, keepdims=True))
        do_ref[:, lanes] = grad
        mix_ref[:, lanes] = (gg * gain * u * sig * (1.0 + og * (1.0 - sig))).astype(bf16)
        local = dot1(grad, p_ref[h], TN).astype(bf16)
        for j in range(HEADS):
            local_ref[HEADS * h + j] = local[j * quarter : (j + 1) * quarter]

    @pl.when(pl.program_id(0) == 0)
    def _():
        gain_out_ref[...] = jnp.zeros_like(gain_out_ref)

    gain_out_ref[0:1, :] += total


def conv_acts(ext_ref, weights, marks, lane):
    conv = conv_parts(ext_ref, weights, marks, lane)
    sig = sigmoid(conv)
    return conv, sig, conv * sig


def conv_pull(d_act, conv, sig, ext_ref, gext_ref, gtaps_ref, weights, marks, lane):
    d_conv = d_act * sig * (1.0 + conv * (1.0 - sig))
    for tap in range(TAPS):
        kept = d_conv * marks[:, tap : tap + 1] if tap < TAPS - 1 else d_conv
        place = (pl.ds(HALO - TAPS + 1 + tap, TOK), pl.ds(lane, DK))
        gtaps_ref[tap : tap + 1, lane : lane + DK] += jnp.sum(
            kept * ext_ref[place], axis=0, keepdims=True
        )
        gext_ref[place] += kept * weights[tap : tap + 1, lane : lane + DK]


def store_rows(gpre_ref, gext_ref):
    s = pl.program_id(0)
    gpre_ref[pl.ds(pl.multiple_of(s * TOK, TOK), TOK), :] = gext_ref[HALO:, :].astype(bf16)
    halo = pl.multiple_of(2 * TOK + s * HALO, HALO)
    gpre_ref[pl.ds(halo, HALO), :] = gext_ref[0:HALO, :].astype(bf16)


def unit_pull(d, hat, scale):
    return scale * (d - hat * jnp.sum(d * hat, axis=-1, keepdims=True))


def chunk_backward_early(
    pre_ref, rim_ref, scal_ref, rate_ref, taps_ref, marks_ref, docs_ref,
    uw_ref, s_ref, do_ref,
    gpre_ref, gtaps_ref, fresh_ref, recalled_ref, df_ref, dk_ref, dc_ref, ext_ref, gext_ref,
):
    inner = HEADS * DK
    ext_ref[0:HALO, :] = rim_ref[...].astype(f32)
    ext_ref[HALO:, :] = pre_ref[...].astype(f32)
    gext_ref[...] = jnp.zeros_like(gext_ref)

    @pl.when(pl.program_id(0) == 0)
    def _():
        gtaps_ref[...] = jnp.zeros_like(gtaps_ref)

    marks = marks_ref[0]
    weights = taps_ref[...]
    strength, total, total_t, causal, below = decays(
        scal_ref[...], rate_ref[...], marks, docs_ref[0]
    )
    rows, cols = iotas()
    reached = marks[:, 3:4]
    grad_c = jnp.zeros((TOK, TOK), f32)
    for h in range(HEADS):
        conv, sig, act = conv_acts(ext_ref, weights, marks, h * DK)
        act_k = conv_acts(ext_ref, weights, marks, inner + h * DK)[2]
        nq = unit_scale(act)
        q_hat = act * nq
        q, k = q_hat.astype(bf16), (act_k * unit_scale(act_k)).astype(bf16)
        c_col = total[:, HEADS + h : HEADS + h + 1]
        c_row = total_t[HEADS + h : HEADS + h + 1, :]
        decay = jnp.where(causal, jnp.exp(jnp.where(causal, c_col - c_row, 0.0)), 0.0)
        scores = dot1(q, k, NT) * decay
        start = jnp.exp(c_col) * reached
        state = s_ref[h]
        do = do_ref[:, h * DK : (h + 1) * DK].astype(bf16)
        fresh = uw_ref[h, :, :DK] - dot1(uw_ref[h, :, DK:], state, NT)
        fresh = fresh.astype(bf16)
        fresh_ref[h] = fresh
        recalled_ref[h] = dot1(k, state, NT)
        df_ref[h] = dot1(scores, do, TN)
        d_scores = dot1(do, fresh, NT)
        pull = d_scores * scores
        d_qk = (d_scores * decay).astype(bf16)
        dk_ref[h] = dot1(d_qk, q, TN)
        do_state = dot1(do, state)
        d_q = dot1(d_qk, k) + start * do_state
        d_start = jnp.sum(q.astype(f32) * do_state, axis=-1, keepdims=True)
        d_c = jnp.sum(pull - jnp.transpose(pull), axis=-1, keepdims=True) + d_start * start
        grad_c = jnp.where(cols == HEADS + h, d_c, grad_c)
        conv_pull(
            unit_pull(d_q, q_hat, nq), conv, sig, ext_ref, gext_ref, gtaps_ref, weights, marks,
            h * DK,
        )
    dc_ref[...] = grad_c
    store_rows(gpre_ref, gext_ref)


def chunk_backward_late(
    pre_ref, rim_ref, scal_ref, rate_ref, taps_ref, marks_ref, docs_ref,
    x_ref, s_ref, d_ref, fresh_ref, recalled_ref, df_ref, dk_ref, dc_ref,
    gpre_ref, gscal_ref, gtaps_ref, grate_ref, ext_ref, gext_ref,
):
    inner = HEADS * DK
    ext_ref[0:HALO, :] = rim_ref[:, inner:].astype(f32)
    ext_ref[HALO:, :] = pre_ref[:, inner:].astype(f32)
    gext_ref[...] = jnp.zeros_like(gext_ref)

    @pl.when(pl.program_id(0) == 0)
    def _():
        gtaps_ref[...] = jnp.zeros_like(gtaps_ref)
        grate_ref[...] = jnp.zeros_like(grate_ref)

    marks = marks_ref[0]
    weights = taps_ref[:, inner:]
    scal = scal_ref[...]
    rates = rate_ref[...]
    strength, total, total_t, causal, below = decays(scal, rates, marks, docs_ref[0])
    rows, cols = iotas()
    reached, tail = marks[:, 3:4], marks[:, 4:5]
    grad_b = jnp.zeros((TOK, TOK), f32)
    grad_c = jnp.zeros((TOK, TOK), f32)
    for h in range(HEADS):
        conv_k, sig_k, act_k = conv_acts(ext_ref, weights, marks, h * DK)
        conv_v, sig_v, act_v = conv_acts(ext_ref, weights, marks, inner + h * DK)
        nk = unit_scale(act_k)
        k_hat = act_k * nk
        k, v = k_hat.astype(bf16), act_v.astype(bf16)
        kf, vf = k.astype(f32), v.astype(f32)
        c_col = total[:, HEADS + h : HEADS + h + 1]
        c_row = total_t[HEADS + h : HEADS + h + 1, :]
        strict = causal & below
        strict_decay = jnp.where(strict, jnp.exp(jnp.where(strict, c_col - c_row, 0.0)), 0.0)
        b = strength[:, h : h + 1]
        gram_decay = dot1(k, k, NT) * strict_decay
        start = jnp.exp(c_col) * reached
        last = c_col[TOK - 1 : TOK, :]
        tail_decay = jnp.exp(last - c_col) * tail
        carry = jnp.exp(last) * reached[TOK - 1 : TOK, :]
        state, adj = s_ref[h], d_ref[h]
        fresh, recalled = fresh_ref[h], recalled_ref[h]
        d_fresh = df_ref[h] + dot1(kf * tail_decay, adj, NT)
        d_r = dot1(x_ref[h], d_fresh, TN)
        d_v = b * d_r
        d_b = jnp.sum(d_r * (vf - start * recalled), axis=-1, keepdims=True)
        d_start = -jnp.sum(d_v * recalled, axis=-1, keepdims=True)
        d_strict = -dot1(d_r, fresh, NT)
        strict_pull = d_strict * gram_decay
        d_b = d_b + jnp.sum(strict_pull, axis=-1, keepdims=True)
        d_gram = (d_strict * (b * strict_decay)).astype(bf16)
        d_k = dk_ref[h] - start * dot1(d_v, state) + dot1(d_gram, k) + dot1(d_gram, k, TN)
        fresh_adj = dot1(fresh, adj)
        d_k = d_k + tail_decay * fresh_adj
        d_tail = jnp.sum(kf * fresh_adj, axis=-1, keepdims=True) * tail_decay
        d_carry = jnp.sum(
            jnp.sum(adj.astype(f32) * state.astype(f32), axis=-1, keepdims=True),
            axis=0, keepdims=True,
        )
        pull = b * strict_pull
        d_c = jnp.sum(pull - jnp.transpose(pull), axis=-1, keepdims=True)
        d_c = d_c + d_start * start - d_tail
        d_last = d_carry * carry + jnp.sum(d_tail, axis=0, keepdims=True)
        d_c = d_c + jnp.where(rows[:, 0:1] == TOK - 1, d_last, 0.0)
        grad_b = jnp.where(cols == h, d_b, grad_b)
        grad_c = jnp.where(cols == HEADS + h, d_c, grad_c)
        conv_pull(
            unit_pull(d_k, k_hat, nk), conv_k, sig_k, ext_ref, gext_ref, gtaps_ref, weights,
            marks, h * DK,
        )
        conv_pull(
            d_v, conv_v, sig_v, ext_ref, gext_ref, gtaps_ref, weights, marks, inner + h * DK
        )
    upper = (cols >= rows).astype(bf16)
    grad_ld = dot2(upper, grad_c + dc_ref[...])
    decay_side = -grad_ld * rates * sigmoid(scal)
    gscal_ref[...] = jnp.where(
        cols < HEADS,
        grad_b * strength * (1.0 - strength),
        jnp.where(cols < 2 * HEADS, decay_side, 0.0),
    ).astype(bf16)
    grate_ref[0:1, :] += -jnp.sum(grad_ld * softplus(scal), axis=0, keepdims=True)
    store_rows(gpre_ref, gext_ref)


def row_grads(groups, lhs_count, rhs_count, *refs):
    out_ref = refs[-1]
    lhs = [refs[i][...] for i in range(lhs_count)]
    rhs = refs[lhs_count : lhs_count + rhs_count]
    lane = 0
    for group in groups:
        total = None
        for i, j in group:
            part = dot1(lhs[i][: rhs[j].shape[0]], rhs[j][...], TN)
            total = part if total is None else total + part
        out_ref[:, lane : lane + total.shape[1]] = total.astype(bf16)
        lane += total.shape[1]


def mixer_grads(
    offsets, place_ref, normed_ref, mixer_ref, og_ref, gq_ref, gkv_ref, gscal_ref, gated_ref, *outs
):
    width = normed_ref.shape[1]
    part = HEADS * DK // 2
    tokens = 2 * TOK

    def rows_x(ref, offset):
        place = lax.rem(place_ref[0] + offset, 4)
        return ref[:, pl.ds(pl.multiple_of(place * (width // 4), 128), width // 4)]

    def rows_z(ref, offset):
        place = lax.rem(place_ref[1] + offset, 4)
        cut = width // 16
        pieces = [
            ref[:, pl.ds(pl.multiple_of((j * 4 + place) * cut, 128), cut)] for j in range(4)
        ]
        return jnp.concatenate(pieces, axis=1)

    def store(outs, columns):
        lane = 0
        for column in columns:
            column = column.astype(bf16)
            lanes = slice(lane, lane + column.shape[1])
            rows = column.shape[0] // len(outs)
            for i, out in enumerate(outs):
                out[:, lanes] = column[i * rows : (i + 1) * rows]
            lane += column.shape[1]

    count = len(outs) // (2 * len(offsets))
    for i, offset in enumerate(offsets):
        normed = rows_x(normed_ref, offset)
        store(
            outs[i * count : (i + 1) * count],
            [
                dot1(normed[:tokens], og_ref[...], TN),
                dot1(normed, gq_ref[...], TN),
                dot1(normed[:tokens], gscal_ref[...], TN),
                dot1(normed, gkv_ref[:, :part], TN),
            ],
        )
        normed = rows_z(normed_ref, offset)
        i += len(offsets)
        store(
            outs[i * count : (i + 1) * count],
            [
                dot1(normed, gkv_ref[:, part:], TN),
                dot1(rows_z(mixer_ref, offset), gated_ref[...], TN),
            ],
        )


def input_grads(
    rim_ref, gq_ref, gkv_ref, gscal_ref, og_ref, left_ref, right_ref, out_ref, first_ref, second_ref
):
    inner = HEADS * DK
    part = inner // 2
    tokens = 2 * TOK

    @pl.when(pl.program_id(0) == 0)
    def _():
        first_ref[:, :inner] = gq_ref[:tokens, :]
        first_ref[:, inner : inner + 128] = gscal_ref[...]
        first_ref[:, inner + 128 : inner + 128 + part] = gkv_ref[:tokens, :part]
        first_ref[:, inner + 128 + part :] = og_ref[...]
        second_ref[...] = gkv_ref[:tokens, part:]
        for s in range(2):
            rows = slice((s + 1) * TOK - HALO, (s + 1) * TOK)
            rim = rim_ref[s * HALO : (s + 1) * HALO, :].astype(f32)

            def put(ref, lanes, came):
                ref[rows, lanes] = (ref[rows, lanes].astype(f32) + came).astype(bf16)

            put(first_ref, slice(0, inner), rim[:, :inner])
            put(
                first_ref,
                slice(inner + 128, inner + 128 + part),
                rim[:, inner : inner + part],
            )
            put(second_ref, slice(0, inner + part), rim[:, inner + part :])

    total = dot1(first_ref[...], left_ref[...], NT)
    total = total + dot1(second_ref[...], right_ref[:, : inner + part], NT)
    out_ref[...] = total.astype(bf16)


def ignoring(kernel, at, count):
    def inner_kernel(*refs):
        kernel(*refs[:at], *refs[at + count :])

    return inner_kernel


def dep_specs(deps):
    return [pl.BlockSpec(memory_space=pl.ANY) for _ in deps]


def cost(flops, moved):
    return pl.CostEstimate(flops=flops, bytes_accessed=moved, transcendentals=0)


def params():
    return pltpu.CompilerParams(vmem_limit_bytes=VMEM)


def whole(shape):
    return pl.BlockSpec(shape, lambda s: (0,) * len(shape))


def by_rows(rows, cols, base=0, lane=0):
    return pl.BlockSpec((rows, cols), lambda s: (base + s, lane))


def by_lead(*shape):
    return pl.BlockSpec(shape, lambda s: (s,) + (0,) * (len(shape) - 1))


def mixer_specs():
    wide = 3 * HEADS * DK
    return [
        by_rows(TOK, wide),
        by_rows(HALO, wide, 2 * TOK // HALO),
        by_rows(TOK, 128),
        whole((1, 128)),
        whole((TAPS, wide)),
        by_lead(1, TOK, 8),
        by_lead(1, 1, TOK),
    ]


def run_chunk_forward(pre, scal, rates, taps, marks, docs):
    quarter = DK // HEADS
    wide = 3 * HEADS * DK
    return pl.pallas_call(
        chunk_forward,
        grid=(2,),
        in_specs=mixer_specs(),
        out_specs=[
            by_lead(16, DK + quarter, DK),
            by_lead(HEADS, TOK, DK),
            by_lead(HEADS, TOK, DK),
            by_lead(HEADS, TOK, DK),
            by_lead(HEADS, TOK, 2 * DK),
        ],
        out_shape=[
            jax.ShapeDtypeStruct((SEQ, DK + quarter, DK), bf16),
            jax.ShapeDtypeStruct((8, TOK, DK), bf16),
            jax.ShapeDtypeStruct((8, TOK, DK), f32),
            jax.ShapeDtypeStruct((8, TOK, DK), bf16),
            jax.ShapeDtypeStruct((8, TOK, 2 * DK), f32),
        ],
        scratch_shapes=[pltpu.VMEM((HALO + TOK, wide), f32)],
        compiler_params=params(),
        cost_estimate=cost(10**10, 6 * 10**6),
    )(pre, pre, scal, rates, taps, marks, docs)


def run_scan_forward(got):
    return pl.pallas_call(
        scan_forward,
        out_shape=jax.ShapeDtypeStruct((SEQ, DK // HEADS, DK), bf16),
        compiler_params=params(),
        cost_estimate=cost(10**9, 3 * 10**6),
    )(got)


def run_scan_backward(got, local, deps):
    vmem = pl.BlockSpec(memory_space=pltpu.VMEM)
    return pl.pallas_call(
        ignoring(scan_backward, 2, len(deps)),
        in_specs=[vmem, vmem] + dep_specs(deps),
        out_specs=vmem,
        out_shape=jax.ShapeDtypeStruct((SEQ, DK // HEADS, DK), bf16),
        compiler_params=params(),
        cost_estimate=cost(10**9, 3 * 10**6),
    )(got, local, *deps)


def run_gate_forward(p, z, state, og, gain, deps):
    inner = HEADS * DK
    return pl.pallas_call(
        ignoring(gate_forward, 5, len(deps)),
        grid=(2,),
        in_specs=[
            by_lead(HEADS, TOK, DK),
            by_lead(HEADS, TOK, DK),
            by_lead(HEADS, DK, DK),
            by_rows(TOK, inner),
            whole((1, DK)),
        ]
        + dep_specs(deps),
        out_specs=[by_rows(TOK, inner), by_rows(TOK, inner)],
        out_shape=[
            jax.ShapeDtypeStruct((2 * TOK, inner), f32),
            jax.ShapeDtypeStruct((2 * TOK, inner), bf16),
        ],
        compiler_params=params(),
        cost_estimate=cost(10**9, 3 * 10**6),
    )(p, z, state, og, gain, *deps)


def run_gate_backward(gg, heads_out, og, gain, p):
    inner = HEADS * DK
    return pl.pallas_call(
        gate_backward,
        grid=(2,),
        in_specs=[
            by_rows(TOK, inner),
            by_rows(TOK, inner),
            by_rows(TOK, inner),
            whole((1, DK)),
            by_lead(HEADS, TOK, DK),
        ],
        out_specs=[
            by_rows(TOK, inner),
            by_rows(TOK, inner),
            by_lead(16, DK // HEADS, DK),
            whole((8, DK)),
        ],
        out_shape=[
            jax.ShapeDtypeStruct((2 * TOK, inner), f32),
            jax.ShapeDtypeStruct((2 * TOK, inner), bf16),
            jax.ShapeDtypeStruct((SEQ, DK // HEADS, DK), bf16),
            jax.ShapeDtypeStruct((8, DK), f32),
        ],
        compiler_params=params(),
        cost_estimate=cost(10**9, 3 * 10**6),
    )(gg, heads_out, og, gain, p)


def run_chunk_backward_early(pre, scal, rates, taps, marks, docs, uw, state, do, deps):
    inner = HEADS * DK
    wide = 3 * inner
    square = jax.ShapeDtypeStruct((8, TOK, DK), f32)
    return pl.pallas_call(
        ignoring(chunk_backward_early, 10, len(deps)),
        grid=(2,),
        in_specs=mixer_specs()
        + [
            by_lead(HEADS, TOK, 2 * DK),
            by_lead(HEADS, DK, DK),
            by_rows(TOK, inner),
        ]
        + dep_specs(deps),
        out_specs=[
            whole((2 * (TOK + HALO), inner)),
            whole((TAPS, inner)),
            by_lead(HEADS, TOK, DK),
            by_lead(HEADS, TOK, DK),
            by_lead(HEADS, TOK, DK),
            by_lead(HEADS, TOK, DK),
            by_rows(TOK, 128),
        ],
        out_shape=[
            jax.ShapeDtypeStruct((2 * (TOK + HALO), inner), bf16),
            jax.ShapeDtypeStruct((TAPS, inner), f32),
            jax.ShapeDtypeStruct((8, TOK, DK), bf16),
            square,
            square,
            square,
            jax.ShapeDtypeStruct((2 * TOK, 128), f32),
        ],
        scratch_shapes=[
            pltpu.VMEM((HALO + TOK, wide), f32),
            pltpu.VMEM((HALO + TOK, inner), f32),
        ],
        compiler_params=params(),
        cost_estimate=cost(5 * 10**9, 10**7),
    )(pre, pre, scal, rates, taps, marks, docs, uw, state, do, *deps)


def run_chunk_backward_late(
    pre, scal, rates, taps, marks, docs, x, state, adj, early, deps
):
    inner = HEADS * DK
    wide = 3 * inner
    return pl.pallas_call(
        ignoring(chunk_backward_late, 15, len(deps)),
        grid=(2,),
        in_specs=mixer_specs()
        + [
            by_lead(HEADS, TOK, DK),
            by_lead(HEADS, DK, DK),
            by_lead(HEADS, DK, DK),
            by_lead(HEADS, TOK, DK),
            by_lead(HEADS, TOK, DK),
            by_lead(HEADS, TOK, DK),
            by_lead(HEADS, TOK, DK),
            by_rows(TOK, 128),
        ]
        + dep_specs(deps),
        out_specs=[
            whole((2 * (TOK + HALO), 2 * inner)),
            by_rows(TOK, 128),
            whole((TAPS, 2 * inner)),
            whole((8, 128)),
        ],
        out_shape=[
            jax.ShapeDtypeStruct((2 * (TOK + HALO), 2 * inner), bf16),
            jax.ShapeDtypeStruct((2 * TOK, 128), bf16),
            jax.ShapeDtypeStruct((TAPS, 2 * inner), f32),
            jax.ShapeDtypeStruct((8, 128), f32),
        ],
        scratch_shapes=[
            pltpu.VMEM((HALO + TOK, 2 * inner), f32),
            pltpu.VMEM((HALO + TOK, 2 * inner), f32),
        ],
        compiler_params=params(),
        cost_estimate=cost(5 * 10**9, 10**7),
    )(pre, pre, scal, rates, taps, marks, docs, x, state, adj, *early, *deps)


def run_row_grads(lhs, rhs, groups, deps=()):
    width = lhs[0].shape[1]
    cols = sum(rhs[group[0][1]].shape[1] for group in groups)
    return pl.pallas_call(
        partial(row_grads, groups, len(lhs), len(rhs)),
        grid=(4,),
        in_specs=[pl.BlockSpec((m.shape[0], width // 4), lambda s: (0, s)) for m in lhs]
        + [whole(m.shape) for m in rhs]
        + dep_specs(deps),
        out_specs=pl.BlockSpec((width // 4, cols), lambda s: (s, 0)),
        out_shape=jax.ShapeDtypeStruct((width, cols), bf16),
        compiler_params=params(),
        cost_estimate=cost(2 * rhs[0].shape[0] * width * cols, 2 * width * cols),
    )(*lhs, *rhs, *deps)


def run_mixer_grads(offsets, halves, *arrays, deps=()):
    width = arrays[0].shape[1]
    inner = HEADS * DK
    vmem = pl.BlockSpec(memory_space=pltpu.VMEM)
    place = jnp.stack([place_of("x"), place_of("z")]).astype(jnp.int32)
    shapes = [
        (width // 4 // halves, cols)
        for cols in (2 * inner + inner // 2 + 128, 2 * inner + inner // 2)
        for _ in range(halves * len(offsets))
    ]
    return pl.pallas_call(
        ignoring(partial(mixer_grads, offsets), 8, len(deps)),
        in_specs=[pl.BlockSpec(memory_space=pltpu.SMEM)] + [vmem] * 7 + dep_specs(deps),
        out_specs=[vmem] * len(shapes),
        out_shape=[jax.ShapeDtypeStruct(shape, bf16) for shape in shapes],
        compiler_params=params(),
        cost_estimate=cost(2 * 256 * width * 5 * inner, 2 * width * 5 * inner),
    )(place, *arrays, *deps)


def run_input_grads(rim, gq, gkv, gscal, og, left, right, deps):
    inner = HEADS * DK
    width = left.shape[0]
    tokens = 2 * TOK
    cut = width // 4
    return pl.pallas_call(
        ignoring(input_grads, 7, len(deps)),
        grid=(4,),
        in_specs=[whole(m.shape) for m in (rim, gq, gkv, gscal, og)]
        + [
            by_rows(cut, left.shape[1]),
            by_rows(cut, right.shape[1]),
        ]
        + dep_specs(deps),
        out_specs=pl.BlockSpec((tokens, cut), lambda s: (0, s)),
        out_shape=jax.ShapeDtypeStruct((tokens, width), bf16),
        scratch_shapes=[
            pltpu.VMEM((tokens, left.shape[1]), bf16),
            pltpu.VMEM((tokens, inner + inner // 2), bf16),
        ],
        compiler_params=params(),
        cost_estimate=cost(2 * tokens * width * 5 * inner, 2 * width * 5 * inner),
    )(rim, gq, gkv, gscal, og, left, right, *deps)


SEQ_AXES = ("x", "z", "y")
GROUP_AXES = ("y", "head")


def passed_along(array, by):
    pairs = [(i, i + by) for i in range(SEQ) if 0 <= i + by < SEQ]
    return lax.ppermute(array, SEQ_AXES, pairs)


def along(array, axis, by):
    count = lax.axis_size(axis)
    return lax.ppermute(array, axis, [(i, (i + by) % count) for i in range(count)])


def place_of(axis):
    return lax.axis_index(axis)


def flipped(array, axes, mask):
    count = lax.axis_size(axes)
    return lax.ppermute(array, axes, [(i, i ^ mask) for i in range(count)])


def pick(array, index, dim):
    return lax.dynamic_index_in_dim(array, index, dim, keepdims=False)


def ordered(mine, other, place, axis=0):
    first = place == 0
    return jnp.concatenate(
        [jnp.where(first, mine, other), jnp.where(first, other, mine)], axis=axis
    )


def later(array, *deps):
    for dep in deps:
        first = lax.slice(dep, (0,) * dep.ndim, (1,) * dep.ndim).reshape(())
        array = array + (first * 0).astype(array.dtype)
    return array


def gather_last(first, second):
    near, far, halfway = near_and_far(first, second, ("z", "x"))
    outs = []
    for i, (array, axis, dim) in enumerate(((first, "z", 1), (second, "x", 0))):
        place = place_of(axis)
        shape = list(array.shape)
        shape.insert(dim, 4)
        out = jnp.zeros(shape, array.dtype)
        block = jnp.concatenate(far[2 * i : 2 * i + 2], axis=0)
        for offset, block in ((0, array), (-1, near[2 * i]), (-2, block), (1, near[2 * i + 1])):
            out = lax.dynamic_update_index_in_dim(out, block, (place + offset) % 4, dim)
        outs.append(out.reshape(-1, array.shape[-1]))
    return outs[0], outs[1], halfway


def exchange(array, axis):
    return lax.all_to_all(array, axis, split_axis=0, concat_axis=0, tiled=True)


def head_place():
    index = lax.axis_index("head")
    return index // 2, index % 2


def core_scatter(partial_rows):
    core = head_place()[1]
    rows = partial_rows.shape[0] // HEADS
    blocks = partial_rows.astype(bf16).reshape(2, 2, rows, -1)
    got = flipped(pick(blocks, 1 - core, 1), "head", 1)
    return pick(blocks, core, 1).astype(f32) + got.astype(f32), got


def chip_scatter(both, *gates):
    chip = head_place()[0]
    got = flipped(later(pick(both, 1 - chip, 0), *gates).astype(bf16), "head", 2)
    return pick(both, chip, 0) + got.astype(f32)


def head_gather(rows):
    chip, core = head_place()
    chip_got = flipped(rows, "head", 2)
    first = chip == 0
    chips = [jnp.where(first, rows, chip_got), jnp.where(first, chip_got, rows)]
    chips = jnp.stack(chips)
    got = flipped(chips, "head", 1)
    first = core == 0
    cores = [jnp.where(first, chips, got), jnp.where(first, got, chips)]
    return jnp.stack(cores, axis=1).reshape(HEADS * rows.shape[0], -1), chip_got


def group_scatter(partial_rows):
    chip, core = head_place()
    place = place_of("y") * 2 + chip
    blocks = partial_rows.astype(bf16).reshape(4, 2, -1, partial_rows.shape[1])
    got = flipped(pick(blocks, 1 - core, 1), GROUP_AXES, 1)
    both = pick(blocks, core, 1).astype(f32) + got.astype(f32)
    total = pick(both, place, 0)
    for mask in (2, 1, 3):
        part = pick(both, jnp.bitwise_xor(place, mask), 0).astype(bf16)
        total = total + flipped(part, GROUP_AXES, 2 * mask).astype(f32)
    return total, got


def group_gather(rows):
    chip, core = head_place()
    place = place_of("y") * 2 + chip
    out = jnp.zeros((4,) + rows.shape, rows.dtype)
    for mask in (2, 1, 3, 0):
        got = flipped(rows, GROUP_AXES, 2 * mask) if mask else rows
        out = lax.dynamic_update_index_in_dim(out, got, jnp.bitwise_xor(place, mask), 0)
    got = flipped(out, GROUP_AXES, 1)
    first = core == 0
    cores = [jnp.where(first, out, got), jnp.where(first, got, out)]
    return jnp.stack(cores, axis=1).reshape(8 * rows.shape[0], -1)


def in_vmem(kernel, shapes, place, *arrays, deps=()):
    vmem = pl.BlockSpec(memory_space=pltpu.VMEM)
    moved = sum(2 * a.size for a in arrays)
    return pl.pallas_call(
        ignoring(kernel, 1 + len(arrays), len(deps)),
        in_specs=[pl.BlockSpec(memory_space=pltpu.SMEM)] + [vmem] * len(arrays) + dep_specs(deps),
        out_specs=[vmem] * len(shapes),
        out_shape=[jax.ShapeDtypeStruct(shape, kind) for shape, kind in shapes],
        compiler_params=params(),
        cost_estimate=cost(moved, moved),
    )(place, *arrays, *deps)


def add_far(place_ref, *refs):
    for i in range(2):
        right, left, ahead, behind = refs[4 * i : 4 * i + 4]
        right_out, left_out = refs[8 + 2 * i : 10 + 2 * i]
        half = ahead.shape[0]
        total = right[:half].astype(f32) + ahead[...].astype(f32)
        right_out[:half] = total.astype(bf16)
        right_out[half:] = right[half:]
        left_out[:half] = left[:half]
        total = left[half:].astype(f32) + behind[...].astype(f32)
        left_out[half:] = total.astype(bf16)


def add_and_cut(place_ref, *refs):
    for i in range(2):
        members = refs[3 * i : 3 * i + 3]
        outs = refs[6 + 4 * i : 10 + 4 * i]
        rows = members[0].shape[0] // 4
        for out, by in zip(outs, (0, 2, 1, 3)):
            start = pl.multiple_of(lax.rem(place_ref[1 - i] + by, 4) * rows, rows)
            total = members[0][pl.ds(start, rows), :].astype(f32)
            for member in members[1:]:
                total = total + member[pl.ds(start, rows), :].astype(f32)
            out[...] = total.astype(bf16)


def add_and_halve(place_ref, *refs):
    kept, sent = refs[8:]
    rows = kept.shape[0]
    lane = 0
    for i in range(2):
        parts = refs[4 * i : 4 * i + 4]
        lanes = slice(lane, lane + parts[0].shape[1])
        lane += parts[0].shape[1]
        for out, at in ((kept, place_ref[2]), (sent, 1 - place_ref[2])):
            start = pl.multiple_of(at * rows, rows)
            total = parts[0][pl.ds(start, rows), :].astype(f32)
            for part in parts[1:]:
                total = total + part[pl.ds(start, rows), :].astype(f32)
            out[:, lanes] = total.astype(out.dtype)


def places():
    return jnp.stack([place_of(axis) for axis in SEQ_AXES]).astype(jnp.int32)


def reduce_near(owns, arrays, deps):
    shapes = [(arrays[i].shape, bf16) for i in (0, 1, 4, 5)]
    sums = in_vmem(add_far, shapes, places(), *arrays, deps=deps)
    gate = sums[0]
    arrays = []
    for i, axis in enumerate(("x", "z")):
        arrays += [owns[i], along(sums[2 * i], axis, 1), along(sums[2 * i + 1], axis, -1)]
    return arrays, gate


def reduce_cross(arrays, deps):
    shapes = []
    for own in (arrays[0], arrays[3]):
        shapes += [((own.shape[0] // 4, own.shape[1]), bf16)] * 4
    cut = in_vmem(add_and_cut, shapes, places(), *arrays, deps=deps)
    arrays = []
    for i, axis in enumerate(("z", "x")):
        own, two, one, three = cut[4 * i : 4 * i + 4]
        arrays += [own, along(two, axis, 2), along(one, axis, 1), along(three, axis, -1)]
    return arrays, cut[0]


def reduce_end(arrays, deps):
    rows, cols = arrays[0].shape[0] // 2, arrays[0].shape[1] + arrays[4].shape[1]
    shapes = [((rows, cols), f32), ((rows, cols), bf16)]
    kept, sent = in_vmem(add_and_halve, shapes, places(), *arrays, deps=deps)
    return kept + along(sent, "y", 1).astype(f32), sent


def pair_up(place_ref, left, left_other, right, right_other, left_out, right_out):
    rows = left.shape[0]
    mine = pl.multiple_of(place_ref[2] * rows, rows)
    other = pl.multiple_of((1 - place_ref[2]) * rows, rows)
    left_out[pl.ds(mine, rows), :] = left[...]
    left_out[pl.ds(other, rows), :] = left_other[...]
    right_out[pl.ds(mine, rows), :] = right[...]
    right_out[pl.ds(other, rows), :] = right_other[...]


def pass_on(place_ref, *refs):
    for i in range(2):
        half = refs[4 + 2 * i].shape[0]
        refs[4 + 2 * i][...] = refs[2 * i][:half]
        refs[5 + 2 * i][...] = refs[2 * i + 1][half:]


def put_in_place(axes, place_ref, *refs):
    for i in range(2):
        out = refs[10 + i]
        own, left, right, far_a, far_b = refs[5 * i : 5 * i + 5]
        place = place_ref[axes[i]]
        half = far_a.shape[0]
        out[place] = own[...]
        out[lax.rem(place + 3, 4)] = left[...]
        out[lax.rem(place + 1, 4)] = right[...]
        out[lax.rem(place + 2, 4), :half] = far_a[...]
        out[lax.rem(place + 2, 4), half:] = far_b[...]


def near_and_far(first, second, axes):
    near = []
    for array, axis in ((first, axes[0]), (second, axes[1])):
        near += [along(array, axis, 1), along(array, axis, -1)]
    shapes = []
    for array in (first, second):
        shapes += [((array.shape[0] // 2,) + array.shape[1:], bf16)] * 2
    halves = in_vmem(pass_on, shapes, places(), *near)
    far = []
    for i in range(2):
        far += [along(halves[2 * i], axes[i], 1), along(halves[2 * i + 1], axes[i], -1)]
    return near, far, halves[0]


def sum_along(array, axis):
    total = array
    for by in range(1, lax.axis_size(axis)):
        total = total + along(array, axis, by)
    return total


def mm(a, b, dims="ij,jk->ik"):
    return jnp.einsum(dims, a, b, preferred_element_type=f32)


def row_scale(x):
    return lax.rsqrt(jnp.mean(x * x, axis=-1, keepdims=True) + norm_eps)


def norm_pull(x, scale, gain, grad):
    unit = x * scale
    scaled = grad * gain
    return scale * (scaled - unit * jnp.mean(scaled * unit, axis=-1, keepdims=True))


def doc_tables(doc_lengths):
    first = lax.axis_index(SEQ_AXES) * TOK - (TAPS - 1)
    ends = jnp.cumsum(doc_lengths, axis=1)
    places = first + jnp.arange(TOK + TAPS - 1, dtype=jnp.int32)
    counted = jnp.sum((places[None, :, None] >= ends[:, None, :]).astype(jnp.int32), axis=2)
    ext = jnp.where(places[None, :] >= 0, counted, -1)
    local = ext[:, TAPS - 1 :]
    columns = [(ext[:, o : o + TOK] == local) for o in range(TAPS - 1)]
    columns.append(local == ext[:, TAPS - 2 : TAPS - 1])
    columns.append(local == local[:, -1:])
    columns.append(local)
    columns += [jnp.zeros_like(local)] * 2
    marks = jnp.stack([c.astype(f32) for c in columns], axis=-1)
    return marks, local.astype(f32)[:, None, :]


def body(
    inputs, doc_lengths, norm_in, query_weight, key_weight, value_weight, outgate_weight,
    scalar_weight, conv_kernel, decay_rate, head_norm, output_weight, norm_ffn, gate_weight,
    up_weight, down_weight, grad_out,
):
    width = inputs.shape[2]
    inner = HEADS * DK
    hidden = gate_weight.shape[1]
    head_index = lax.axis_index("head")
    quarter = 2 * TOK // HEADS

    gains = jnp.stack([norm_in, norm_ffn], axis=1)
    misc = jnp.concatenate([scalar_weight.reshape(-1, 2 * HEADS), gains], axis=1)
    misc = jnp.pad(misc, ((0, 0), (0, 128 - misc.shape[1])))
    part = inner // 2
    left = jnp.concatenate([query_weight, misc, key_weight[:, :part], outgate_weight], axis=1)
    right = jnp.concatenate([key_weight[:, part:], value_weight, output_weight.T], axis=1)
    y_place = place_of("y")
    rows = left.shape[0]
    left, right = in_vmem(
        pair_up,
        [((2 * rows, left.shape[1]), bf16), ((2 * rows, right.shape[1]), bf16)],
        places(),
        left, along(left, "y", 1), right, along(right, "y", 1),
    )
    near, far, _ = near_and_far(left, right, ("x", "z"))
    left, right = in_vmem(
        partial(put_in_place, (0, 1)),
        [((4, 2 * rows, part.shape[1]), bf16) for part in (left, right)],
        places(),
        left, *near[:2], *far[:2], right, *near[2:], *far[2:],
    )
    all_left, all_right, halfway = gather_last(left, right)
    w_gate, w_out_t = all_left[:, -inner:], all_right[:, -inner:]
    w_left, w_right = all_left[:, :-inner], all_right[:, :-inner]
    gains = w_left[:, inner : inner + 128].T[2 * HEADS : 2 * HEADS + 2].astype(f32)
    gain_in, gain_ffn = gains[0:1], gains[1:2]

    units = hidden // 2
    span = -(-units // 128) * 128

    def in_halves(weight):
        halves = weight.reshape(weight.shape[0], 2, units)
        return jnp.pad(halves, ((0, 0), (0, 0), (0, span - units)))

    packed = jnp.concatenate(
        [in_halves(gate_weight), in_halves(up_weight), in_halves(down_weight.T)], axis=2
    )
    other = along(later(pick(packed, 1 - y_place, 1), left), "y", 1)
    packed = later(ordered(pick(packed, y_place, 1), other, y_place), halfway)
    w_ffn = lax.all_gather(packed, ("x", "z"), axis=0, tiled=True)
    w_gateup = w_ffn[:, : 2 * span]
    w_down_t = w_ffn[:, 2 * span :]

    marks, docs_row = doc_tables(doc_lengths)
    taps = jnp.transpose(conv_kernel.astype(f32), (1, 0, 2)).reshape(TAPS, 3 * inner)
    rates = jnp.zeros((1, 128), f32)
    rates = rates.at[0, HEADS : 2 * HEADS].set(decay_rate.astype(f32))
    gain_head = head_norm.astype(f32).reshape(1, DK)

    halo = passed_along(inputs[:, TOK - HALO :], 1)
    tokens = inputs.reshape(2 * TOK, width)
    all_rows = jnp.concatenate([tokens, halo.reshape(2 * HALO, width)], axis=0).astype(f32)
    scale_in = row_scale(all_rows)
    normed_all = (all_rows * scale_in * gain_in).astype(bf16)
    normed_in = normed_all[: 2 * TOK]

    left = mm(normed_all, w_left)
    right = mm(normed_all, w_right)
    pre = jnp.concatenate(
        [left[:, :inner].astype(bf16), left[:, inner + 128 :].astype(bf16), right.astype(bf16)],
        axis=1,
    )
    scal = left[: 2 * TOK, inner : inner + 128]

    grad_rows = grad_out.reshape(2 * TOK, width)
    grad_other = along(grad_rows, "y", 1)
    send, p, z, x, uw = run_chunk_forward(pre, scal, rates, taps, marks, docs_row)
    out_gate = mm(normed_in, w_gate)
    got = exchange(send, SEQ_AXES)
    state = exchange(run_scan_forward(got), SEQ_AXES).reshape(8, DK, DK)
    heads_out, gated_rows = run_gate_forward(
        p, z, state, out_gate, gain_head, (grad_other,)
    )

    mine = partial(lax.dynamic_slice_in_dim, start_index=head_index * quarter, slice_size=quarter)
    residual = mine(tokens).astype(f32) + chip_scatter(
        core_scatter(mm(gated_rows, w_out_t, "ij,kj->ik"))[0]
    )
    scale_ffn = row_scale(residual)
    normed_ffn = group_gather((residual * scale_ffn * gain_ffn).astype(bf16))

    group_grads = ordered(grad_rows, grad_other, y_place)
    grad_act = mm(group_grads, w_down_t)
    gate_up = mm(normed_ffn, w_gateup)
    gate, up = gate_up[:, :span], gate_up[:, span:]
    sig = sigmoid(gate)
    silu = gate * sig
    product = (silu * up).astype(bf16)
    gu_grad = jnp.concatenate(
        [
            (grad_act * up * sig * (1.0 + gate * (1.0 - sig))).astype(bf16),
            (grad_act * silu).astype(bf16),
        ],
        axis=1,
    )
    ffn_part = mm(gu_grad, w_gateup, "ij,kj->ik").astype(bf16)
    grad_normed = group_scatter(ffn_part)[0]
    back = norm_pull(residual, scale_ffn, gain_ffn, grad_normed)
    grad_residual = mine(grad_rows).astype(f32) + back
    grad_mixer = head_gather(grad_residual.astype(bf16))[0]

    grad_gated = mm(grad_mixer, w_out_t)
    do, gate_grad_mix, local, part_gain_head = run_gate_backward(
        grad_gated, heads_out, out_gate, gain_head, p
    )
    local_got = exchange(local, SEQ_AXES)
    early = run_chunk_backward_early(
        pre, scal, rates, taps, marks, docs_row, uw, state, do, ()
    )
    gq, gtaps_q = early[:2]
    ffn_all = run_row_grads(
        [normed_ffn, group_grads], [gu_grad, product], (((0, 0),), ((1, 1),)), (local,)
    )
    ffn = lax.psum_scatter(ffn_all, ("x", "z"), scatter_dimension=0, tiled=True)
    adj_out = run_scan_backward(got, local_got, (gq,))
    ffn_out, ffn_got = group_scatter(mm(later(product, local), w_down_t, "ij,kj->ik"))
    adj = exchange(adj_out, SEQ_AXES).reshape(8, DK, DK)
    gkv, gscal, gtaps_kv, grate = run_chunk_backward_late(
        pre, scal, rates, taps, marks, docs_row, x, state, adj, early[2:], (ffn_got,)
    )

    arrays = (normed_all, grad_mixer, gate_grad_mix, gq, gkv, gscal, gated_rows)
    far = run_mixer_grads((2,), 2, *arrays)
    blocks = run_mixer_grads((1, 3, 0), 1, *arrays, deps=(far[0], ffn_out))
    owns, partials = (blocks[2], blocks[5]), []
    for i, axis in enumerate(("x", "z")):
        partials += blocks[3 * i : 3 * i + 2]
        partials += [along(far[2 * i], axis, 1), along(far[2 * i + 1], axis, -1)]

    gtaps = jnp.concatenate([gtaps_q, gtaps_kv], axis=1).reshape(12, inner)
    tail = jnp.concatenate([part_gain_head[:1], grate[:1]], axis=1)
    tail = jnp.pad(tail, ((0, 3), (0, inner - tail.shape[1])))
    small = jnp.concatenate([gtaps, tail], axis=0)
    rim = jnp.concatenate([gq[2 * TOK :], gkv[2 * TOK :]], axis=1)
    rim = passed_along(rim, -1)
    input_sent = run_input_grads(
        rim, gq, gkv, gscal, gate_grad_mix, all_left, all_right, (blocks[0],)
    )
    partials, near_gate = reduce_near(owns, partials, (input_sent,))
    ffn = ffn.reshape(2, -1, 3, span)[..., :units]
    ffn_other = along(later(pick(ffn, 1 - y_place, 0), near_gate), "y", 1)
    ffn = ordered(pick(ffn, y_place, 0), ffn_other, y_place, 2).astype(f32)
    by_core = core_scatter(later(input_sent, near_gate))[0]
    grad_normed_in = chip_scatter(by_core)
    own = mine(tokens).astype(f32)
    back_in = norm_pull(own, row_scale(own), gain_in, grad_normed_in)
    both = jnp.concatenate([residual + ffn_out, grad_residual + back_in], axis=1)
    both = both.astype(bf16)
    partials, cross_gate = reduce_cross(partials, (both, ffn_other))
    small = sum_along(later(small, partials[5]), "x")
    mixer_w, end_gate = reduce_end(partials, ())
    both, chip_got = head_gather(later(both, cross_gate))
    small = sum_along(sum_along(later(small, chip_got), "z"), "y")
    outputs, grad_in = both[:, :width], both[:, width:].astype(f32)

    rows = width // SEQ
    key_at = 2 * inner + 128
    grad_conv = jnp.transpose(small[:12].reshape(TAPS, 3, inner), (1, 0, 2))

    def gain_grad(gain, weights, grads):
        total = 0.0
        for weight, grad in zip(weights, grads):
            total = total + jnp.sum(weight.astype(f32) * grad, axis=1)
        return total / gain.astype(f32)

    grad_scalar = mixer_w[:, 2 * inner : 2 * inner + 2 * HEADS]
    gain_parts = jnp.concatenate(
        [
            gain_grad(
                norm_in,
                (outgate_weight, query_weight, scalar_weight.reshape(rows, -1), key_weight, value_weight),
                (
                    mixer_w[:, :inner],
                    mixer_w[:, inner : 2 * inner],
                    grad_scalar,
                    mixer_w[:, key_at : key_at + inner],
                    mixer_w[:, key_at + inner : key_at + 2 * inner],
                ),
            ),
            gain_grad(norm_ffn, (gate_weight, up_weight), (ffn[:, 0], ffn[:, 1])),
            small[12, :DK],
        ]
    )
    shared = sum_along(gain_parts[None], "head")[0]
    return (
        outputs.reshape(inputs.shape),
        grad_in.reshape(inputs.shape),
        shared[:rows],
        mixer_w[:, inner : 2 * inner],
        mixer_w[:, key_at : key_at + inner],
        mixer_w[:, key_at + inner : key_at + 2 * inner],
        mixer_w[:, :inner],
        grad_scalar.reshape(rows, 2, HEADS),
        grad_conv,
        small[12, DK + HEADS : DK + 2 * HEADS],
        shared[2 * rows :],
        mixer_w[:, key_at + 2 * inner :].T,
        shared[rows : 2 * rows],
        ffn[:, 0],
        ffn[:, 1],
        ffn[:, 2].T,
    )


def solution(mesh):
    mesh = Mesh(mesh.devices.reshape(4, 4, 2, HEADS), ("x", "z", "y", "head"))
    seq = SEQ_AXES
    weight = P(seq, "head")
    weight_t = P("head", seq)
    tokens = P(None, seq, None)
    scalars = P(seq, None, "head")
    taps = P(None, None, "head")
    return jax.shard_map(
        body,
        mesh=mesh,
        in_specs=(
            tokens, P(), P(seq), weight, weight, weight, weight, scalars, taps, P("head"), P(),
            weight_t, P(seq), weight, weight, weight_t, tokens,
        ),
        out_specs=(
            tokens, tokens, P(seq), weight, weight, weight, weight, scalars, taps, P("head"),
            P(), weight_t, P(seq), weight, weight, weight_t,
        ),
        check_vma=False,
    )
```
